32 devices in a mesh: dp: 8 (over z, x), tensor: 4 (over y, core).
Axes of the slice: x: 2, y: 2, z: 4, core: 2. Of those that a mesh axis runs over, the one named last changes fastest.
Arguments:
- tokens: bfloat16 [2, 8960, 768], P(None, ('dp', 'tensor')), may hold values from -6 to 6
- out_grad: bfloat16 [2, 8960, 768], P(None, ('dp', 'tensor')), may hold values from -6 to 6
- global_count: int32 [8, 2], P('dp'), may hold values from 1 to 4, as said below
- local_count: int32 [8, 2], P('dp'), may hold values from 4 to 8, as said below
- attn_gain: float32 [768], replicated, may hold values from 0.1 to 1.9
- qkv_weight: bfloat16 [768, 2304], P(None, 'tensor'), may hold values from -0.3125 to 0.3125
- proj_weight: bfloat16 [768, 768], P('tensor'), may hold values from -2.5 to 2.5
- attn_scale: float32 [768], replicated, may hold values from 0.3 to 1.5
- mlp_gain: float32 [768], replicated, may hold values from 0.1 to 1.9
- up_weight: bfloat16 [768, 3072], P(None, 'tensor'), may hold values from -0.21875 to 0.21875
- down_weight: bfloat16 [3072, 768], P('tensor'), may hold values from -0.109375 to 0.109375
- mlp_scale: float32 [768], replicated, may hold values from 0.3 to 1.5
Outputs:
- block_out: bfloat16 [2, 8960, 768], P(None, ('dp', 'tensor'))
- input_grad: bfloat16 [2, 8960, 768], P(None, ('dp', 'tensor'))
- attngain_grad: float32 [768], P('dp')
- qkv_grad: float32 [768, 2304], P('dp', 'tensor')
- proj_grad: float32 [768, 768], P('tensor', 'dp')
- attnscale_grad: float32 [768], P('dp')
- mlpgain_grad: float32 [768], P('dp')
- up_grad: float32 [768, 3072], P('dp', 'tensor')
- down_grad: float32 [3072, 768], P('tensor', 'dp')
- mlpscale_grad: float32 [768], P('dp')
The draws below stay inside these ranges and needn't reach their ends.
Inputs may be any that keep to these rules, and one draw needn't show every extreme that they name: `global_count`: the k-th global crop of a unit fills global slot k; some entry equals 4. `local_count`: the k-th local crop of a unit fills local slot k; some entry equals 8.
All inputs are finite; a program needn't handle non-finite values.
Results may differ from the reference program's by a relative error of at most 0.015.
The reference program's roundings to bfloat16 on the way count: a program that leaves them out, or rounds other values in their place, can miss the bound.
Values may be sent and summed in bfloat16 or wider, within the bound.
No kernel may reach another device: no remote copies, remote signals or barrier semaphores. Data moves between devices by JAX's collectives and lax.ppermute only.
A program may use at most 128 MiB of HBM per device.

```python
import math
import jax
import jax.numpy as jnp
from jax import lax

D = 768
HEADS = 12
HD = 64
FF = 3072
MICRO = 2
GLEN = 197
GPAD = 200
LLEN = 37
LPAD = 40
ROWS = 8960
N_DP = 8
N_TENSOR = 4


def draw_global_count(key, part):
    key = jax.random.fold_in(key, 11)
    first_key, second_key = jax.random.split(key)
    counts = jax.random.randint(first_key, (N_DP * MICRO,), 1, N_TENSOR + 1)
    chosen = jax.random.randint(second_key, (), 0, N_DP * MICRO)
    counts = counts.at[chosen].set(N_TENSOR)
    return counts.reshape(N_DP, MICRO).astype(jnp.int32)


def draw_local_count(key, part):
    key = jax.random.fold_in(key, 23)
    first_key, second_key = jax.random.split(key)
    counts = jax.random.randint(first_key, (N_DP * MICRO,), N_TENSOR, 2 * N_TENSOR + 1)
    chosen = jax.random.randint(second_key, (), 0, N_DP * MICRO)
    counts = counts.at[chosen].set(2 * N_TENSOR)
    return counts.reshape(N_DP, MICRO).astype(jnp.int32)


def with_spikes(values, key, source, target, parts, factor):
    def block_of(dim):
        return (jnp.arange(values.shape[dim]) // (values.shape[dim] // parts)).reshape((-1,) + (1,) * (values.ndim - 1 - dim))

    one_side = jax.random.permutation(key, parts)[block_of(target)]
    other_side = (block_of(target) + parts // 2) % parts
    return jnp.where((block_of(source) == one_side) | (block_of(source) == other_side), factor * values, values)


def levels(own_key, shape, pieces, low, high):
    factor_of = 1.0
    for position, shards_of in pieces:
        steps = jax.random.uniform(jax.random.fold_in(jax.random.fold_in(own_key, 6), position), (shards_of,), jnp.float32, low / len(pieces), high / len(pieces))
        factor_of = factor_of * jnp.repeat(jnp.exp(steps), shape[position] // shards_of).reshape((-1,) + (1,) * (len(shape) - 1 - position))
    return factor_of


def noise(key, dims, scale, most, cuts=(), kind=jnp.bfloat16):
    factor_of = levels(key, dims, cuts, -0.22, 0.18) if cuts else 1.0
    array = jax.random.normal(key, dims, jnp.float32) * scale * factor_of
    return jnp.minimum(jnp.maximum(array, -most), most).astype(kind)


def bell_draw_with(key, shape, deviation, bound, cuts, heavy, held_as=jnp.bfloat16):
    drawn = deviation * jax.random.normal(key, shape, jnp.float32)
    if cuts:
        drawn = drawn * levels(key, shape, cuts, -0.22, 0.18)
    return jnp.clip(with_spikes(drawn, jax.random.fold_in(key, 3), *heavy), -bound, bound).astype(held_as)


def setup_inputs(seed: int = 0) -> dict:
    streams_of = jax.random.split(jax.random.key(seed), 13)
    tokens = bell_draw_with(streams_of[0], (MICRO, ROWS, D), 1.0, 6.0, ((1, 32),), (1, 2, 32, 2.75))
    out_grad = noise(streams_of[1], (MICRO, ROWS, D), 1.0, 6.0, ((1, 32),))
    global_count = draw_global_count(jax.random.fold_in(streams_of[12], 71), 0)
    local_count = draw_local_count(jax.random.fold_in(streams_of[12], 71), 0)
    attn_gain = jnp.clip(1.0 + 0.18 * jax.random.normal(streams_of[4], (D,), jnp.float32), 0.1, 1.9)
    qkv_weight = noise(streams_of[5], (D, 3 * D), (D // 2) ** -0.5, 0.3125, ((1, 4),))
    proj_weight = noise(streams_of[6], (D, D), (max(D // 128, 1)) ** -0.5, 2.5, ((0, 4),))
    attn_scale = jnp.clip(jnp.exp(jax.random.uniform(streams_of[7], (D,), jnp.float32, math.log(0.3), math.log(1.5))), 0.3, 1.5)
    mlp_gain = jnp.clip(1.0 + 0.18 * jax.random.normal(streams_of[8], (D,), jnp.float32), 0.1, 1.9)
    up_weight = noise(streams_of[9], (D, FF), D ** -0.5, 0.21875, ((1, 4),))
    down_weight = noise(streams_of[10], (FF, D), FF ** -0.5, 0.109375, ((0, 4),))
    mlp_scale = jnp.clip(jnp.exp(jax.random.uniform(streams_of[11], (D,), jnp.float32, math.log(0.3), math.log(1.5))), 0.3, 1.5)
    return dict(tokens=tokens, out_grad=out_grad, global_count=global_count, local_count=local_count, attn_gain=attn_gain, qkv_weight=qkv_weight, proj_weight=proj_weight, attn_scale=attn_scale, mlp_gain=mlp_gain, up_weight=up_weight, down_weight=down_weight, mlp_scale=mlp_scale)


@jax.custom_vjp
def low(v):
    return lax.optimization_barrier(v.astype(jnp.bfloat16)).astype(jnp.float32)

@jax.custom_vjp
def low_back(v):
    return v

def low_keep(v):
    return (low(v), None)

def low_pass(kept, grad):
    return (grad,)

def back_keep(v):
    return (v, None)

def back_low(kept, grad):
    return (low(grad),)
low.defvjp(low_keep, low_pass)
low_back.defvjp(back_keep, back_low)
exact_mode = lax.Precision.HIGHEST

def crop_keep(global_num, local_num, groups):
    slot_ids = jnp.arange(groups)[:, None]
    global_rows = jnp.arange(GPAD)[None, :]
    global_part = (global_rows < GLEN) & (slot_ids < global_num)
    local_rows = jnp.arange(2 * LPAD)[None, :]
    crop_ids = slot_ids + groups * (local_rows // LPAD)
    local_part = (local_rows % LPAD < LLEN) & (crop_ids < local_num)
    return jnp.concatenate([global_part, local_part], axis=1).astype(jnp.float32)

def split_crops(values, groups):
    shaped = values.reshape((groups, GPAD + 2 * LPAD) + values.shape[1:])
    global_part = shaped[:, :GPAD]
    local_part = shaped[:, GPAD:].reshape((groups * 2, LPAD) + values.shape[1:])
    return (global_part, local_part)

def join_crops(global_part, local_part, groups):
    local_back = local_part.reshape((groups, 2 * LPAD) + local_part.shape[2:])
    joined = jnp.concatenate([global_part, local_back], axis=1)
    return joined.reshape((-1,) + joined.shape[2:])

def layer_norm(values, gain):
    center = values - lax.optimization_barrier(jnp.mean(values, axis=-1, keepdims=True))
    return center * lax.rsqrt(lax.optimization_barrier(jnp.mean(center * center, axis=-1, keepdims=True)) + 1e-06) * gain

def attend(packed, keep_rows):
    queries = packed[:, :, :, 0]
    key_rows = packed[:, :, :, 1]
    value_rows = packed[:, :, :, 2]
    raw = jnp.einsum('blhe,bmhe->bhlm', queries, key_rows, precision=exact_mode) * HD ** (-0.5)
    scores = low_back(raw)
    scores = jnp.where(keep_rows[:, None, None, :] > 0, scores, -30000.0)
    peak = lax.optimization_barrier(jnp.max(scores, axis=-1, keepdims=True))
    raised = jnp.exp(scores - peak)
    probs = raised / lax.optimization_barrier(jnp.sum(raised, axis=-1, keepdims=True))
    return jnp.einsum('bhlm,bmhe->blhe', low(probs), value_rows, precision=exact_mode)

def unit_forward(rows_in, keep_all, gain_one, weight_qkv, weight_proj, scale_one, gain_two, weight_up, weight_down, scale_two):
    groups = keep_all.shape[0]
    row_keep = keep_all.reshape(-1, 1)
    normed_one = low(layer_norm(rows_in, gain_one))
    packed = low(low_back(jnp.dot(normed_one, weight_qkv, precision=exact_mode)))
    packed = packed.reshape(packed.shape[0], HEADS, 3, HD)
    global_packed, local_packed = split_crops(packed, groups)
    global_keep, local_keep = split_crops(keep_all.reshape(-1), groups)
    context = join_crops(attend(global_packed, global_keep), attend(local_packed, local_keep), groups)
    context = low(low_back(context.reshape(context.shape[0], D)))
    attn_out = low_back(jnp.dot(context, weight_proj, precision=exact_mode))
    middle = rows_in + row_keep * scale_one * attn_out
    normed_two = low(layer_norm(middle, gain_two))
    hidden = low_back(jnp.dot(normed_two, weight_up, precision=exact_mode))
    active = low(jax.nn.gelu(hidden, approximate=False))
    mlp_out = low_back(jnp.dot(active, weight_down, precision=exact_mode))
    return middle + row_keep * scale_two * mlp_out

def reference(tokens, out_grad, global_count, local_count, attn_gain, qkv_weight, proj_weight, attn_scale, mlp_gain, up_weight, down_weight, mlp_scale):
    weights = (attn_gain.astype(jnp.float32), qkv_weight.astype(jnp.float32), proj_weight.astype(jnp.float32), attn_scale.astype(jnp.float32), mlp_gain.astype(jnp.float32), up_weight.astype(jnp.float32), down_weight.astype(jnp.float32), mlp_scale.astype(jnp.float32))
    unit_rows = N_TENSOR * (GPAD + 2 * LPAD)
    rows_all = tokens.astype(jnp.float32).reshape(MICRO * N_DP, unit_rows, D)
    grads_all = out_grad.astype(jnp.float32).reshape(MICRO * N_DP, unit_rows, D)
    global_flat = global_count.T.reshape(-1)
    local_flat = local_count.T.reshape(-1)

    def unit_step(running, item):
        rows_in, grad_in, global_num, local_num = item
        keep_all = crop_keep(global_num, local_num, N_TENSOR)
        result, pull = jax.vjp(lambda rows, *params: unit_forward(rows, keep_all, *params), rows_in, *weights)
        pulled = pull(grad_in)
        running = tuple((before + fresh for before, fresh in zip(running, pulled[1:])))
        return (running, (result.astype(jnp.bfloat16), pulled[0].astype(jnp.bfloat16)))
    start_grads = tuple((jnp.zeros_like(weight) for weight in weights))
    totals, (outputs, backs) = lax.scan(unit_step, start_grads, (rows_all, grads_all, global_flat, local_flat))
    block_out = outputs.reshape(MICRO, ROWS, D)
    input_grad = backs.reshape(MICRO, ROWS, D)
    return (block_out, input_grad, totals[0], totals[1], totals[2], totals[3], totals[4], totals[5], totals[6], totals[7])
```

```python
from functools import partial

import jax
import jax.numpy as jnp
from jax import lax
from jax.sharding import PartitionSpec as P

D = 768
HD = 64
GLEN = 197
GPAD = 200
LLEN = 37
LPAD = 40
F32 = jnp.float32
BF16 = jnp.bfloat16


def crop_keep(global_num, local_num, groups):
    slot_ids = jnp.arange(groups)[:, None]
    global_rows = jnp.arange(GPAD)[None, :]
    global_part = (global_rows < GLEN) & (slot_ids < global_num)
    local_rows = jnp.arange(2 * LPAD)[None, :]
    crop_ids = slot_ids + groups * (local_rows // LPAD)
    local_part = (local_rows % LPAD < LLEN) & (crop_ids < local_num)
    return jnp.concatenate([global_part, local_part], axis=1).astype(F32)


def split_crops(values, blocks):
    shaped = values.reshape((blocks, GPAD + 2 * LPAD) + values.shape[1:])
    global_part = shaped[:, :GPAD]
    local_part = shaped[:, GPAD:].reshape((blocks * 2, LPAD) + values.shape[1:])
    return (global_part, local_part)


def join_crops(global_part, local_part, blocks):
    local_back = local_part.reshape((blocks, 2 * LPAD) + local_part.shape[2:])
    joined = jnp.concatenate([global_part, local_back], axis=1)
    return joined.reshape((-1,) + joined.shape[2:])


def layer_stats(values, gain):
    center = values - jnp.mean(values, axis=-1, keepdims=True)
    inverse = lax.rsqrt(jnp.mean(center * center, axis=-1, keepdims=True) + 1e-06)
    normed = center * inverse
    return (normed * gain, normed, inverse)


def layer_back(grad_norm, gain, normed, inverse):
    scaled = grad_norm * gain
    centered = scaled - jnp.mean(scaled, axis=-1, keepdims=True)
    return inverse * (centered - normed * jnp.mean(scaled * normed, axis=-1, keepdims=True))


def masked_scores(packed, keep_rows, factor):
    scores = (
        jnp.einsum(
            "blhe,bmhe->bhlm",
            packed[:, :, :, 0],
            packed[:, :, :, 1],
            preferred_element_type=F32,
        )
        * factor
    )
    return jnp.where(keep_rows[:, None, None, :] > 0, scores, -30000.0)


def attend_forward(packed, keep_rows, factor):
    scores = masked_scores(packed, keep_rows, factor)
    peak = jnp.max(scores, axis=-1, keepdims=True)
    raised = jnp.exp(scores - peak)
    totals = jnp.sum(raised, axis=-1, keepdims=True)
    probs = (raised / totals).astype(BF16)
    context = jnp.einsum("bhlm,bmhe->blhe", probs, packed[:, :, :, 2], preferred_element_type=F32)
    return (context, peak + jnp.log(totals))


def attend_backward(packed, keep_rows, log_total, grad_context, factor):
    probs = jnp.exp(masked_scores(packed, keep_rows, factor) - log_total)
    grad_probs = jnp.einsum(
        "blhe,bmhe->bhlm", grad_context, packed[:, :, :, 2], preferred_element_type=F32
    )
    row_dot = jnp.sum(probs * grad_probs, axis=-1, keepdims=True)
    grad_scores = (probs * (grad_probs - row_dot)).astype(BF16)
    grad_query = (
        jnp.einsum("bhlm,bmhe->blhe", grad_scores, packed[:, :, :, 1], preferred_element_type=F32)
        * factor
    )
    grad_key = (
        jnp.einsum("bhlm,blhe->bmhe", grad_scores, packed[:, :, :, 0], preferred_element_type=F32)
        * factor
    )
    grad_value = jnp.einsum(
        "bhlm,blhe->bmhe", probs.astype(BF16), grad_context, preferred_element_type=F32
    )
    return jnp.stack([grad_query, grad_key, grad_value], axis=3)


def swap(value, axis, bit):
    size = lax.axis_size(axis)
    return lax.ppermute(value, axis, [(i, i ^ bit) for i in range(size)])


def gather_quarters(own):
    one = swap(own, "tensor", 1)
    two = swap(own, "tensor", 2)
    three = swap(two, "tensor", 1)
    return [own, one, two, three]


def dp_halve(value, bit):
    slices = value.shape[0]
    mine = (lax.axis_index("dp") // bit) % 2
    paired = value.reshape((slices // 2, 2) + value.shape[1:])
    keep = lax.dynamic_index_in_dim(paired, mine, 1, keepdims=False)
    give = lax.dynamic_index_in_dim(paired, 1 - mine, 1, keepdims=False)
    got = swap(give.astype(BF16), "dp", bit)
    return keep + got.astype(F32)


def scatter_sum(parts, first_dp):
    shards = lax.axis_size("dp")
    zero = parts[0] + swap(parts[1].astype(BF16), "tensor", 1).astype(F32)
    two = parts[2] + swap(parts[3].astype(BF16), "tensor", 1).astype(F32)
    shape = (shards, D // shards, parts[0].shape[1])
    zero = zero.reshape(shape)
    two = two.reshape(shape)
    bit = 1
    if first_dp:
        zero = dp_halve(zero, bit)
        two = dp_halve(two, bit)
        bit = 2
    zero = zero + swap(two.astype(BF16), "tensor", 2).astype(F32)
    while bit < shards:
        zero = dp_halve(zero, bit)
        bit = bit * 2
    return zero[0]


def body(
    tokens,
    out_grad,
    global_count,
    local_count,
    attn_gain,
    qkv_weight,
    proj_weight,
    attn_scale,
    mlp_gain,
    up_weight,
    down_weight,
    mlp_scale,
):
    groups = lax.axis_size("tensor")
    shards = lax.axis_size("dp")
    member = lax.axis_index("tensor")
    micro, group_rows, _ = tokens.shape
    factor = HD ** (-0.5)
    heads = groups * qkv_weight.shape[1] // (3 * HD)
    rows = micro * group_rows

    qkv_use = jnp.concatenate(gather_quarters(qkv_weight), axis=1)
    proj_use = jnp.concatenate(gather_quarters(proj_weight), axis=0)
    up_use = jnp.concatenate(gather_quarters(up_weight), axis=1)
    down_use = jnp.concatenate(gather_quarters(down_weight), axis=0)

    keep_list = []
    for i in range(micro):
        keep_all = crop_keep(global_count[0, i], local_count[0, i], groups)
        keep_list.append(lax.dynamic_index_in_dim(keep_all, member, 0, keepdims=False))
    keep_vector = jnp.concatenate(keep_list)
    own_keep = keep_vector[:, None]
    global_keep, local_keep = split_crops(keep_vector, micro)

    residual = tokens.reshape(rows, D).astype(F32)
    normed_first, unit_first, inverse_first = layer_stats(residual, attn_gain)
    first_low = normed_first.astype(BF16)
    packed = jnp.dot(first_low, qkv_use, preferred_element_type=F32).astype(BF16)
    packed = packed.reshape(rows, heads, 3, HD)
    global_packed, local_packed = split_crops(packed, micro)
    global_context, global_total = attend_forward(global_packed, global_keep, factor)
    local_context, local_total = attend_forward(local_packed, local_keep, factor)
    context = join_crops(global_context, local_context, micro)
    context = context.reshape(rows, D).astype(BF16)
    attn_out = jnp.dot(context, proj_use, preferred_element_type=F32)
    middle = residual + own_keep * attn_scale * attn_out
    normed_second, unit_second, inverse_second = layer_stats(middle, mlp_gain)
    second_low = normed_second.astype(BF16)
    hidden = jnp.dot(second_low, up_use, preferred_element_type=F32)
    active = jax.nn.gelu(hidden, approximate=False).astype(BF16)
    mlp_out = jnp.dot(active, down_use, preferred_element_type=F32)
    block_rows = middle + own_keep * mlp_scale * mlp_out
    grad_out = out_grad.reshape(rows, D).astype(F32)
    mlpscale_part = jnp.sum(own_keep * mlp_out * grad_out, axis=0)
    grad_mlp = (own_keep * mlp_scale * grad_out).astype(BF16)
    down_part = jnp.einsum("rd,rf->df", grad_mlp, active, preferred_element_type=F32)
    grad_active = jnp.einsum("rd,fd->rf", grad_mlp, down_use, preferred_element_type=F32)
    unused_value, gelu_pull = jax.vjp(partial(jax.nn.gelu, approximate=False), hidden)
    grad_hidden = gelu_pull(grad_active)[0].astype(BF16)
    up_part = jnp.einsum("rd,rf->df", second_low, grad_hidden, preferred_element_type=F32)
    grad_second = jnp.einsum("rf,df->rd", grad_hidden, up_use, preferred_element_type=F32)
    mlpgain_part = jnp.sum(grad_second * unit_second, axis=0)
    grad_middle = grad_out + layer_back(grad_second, mlp_gain, unit_second, inverse_second)
    attnscale_part = jnp.sum(own_keep * attn_out * grad_middle, axis=0)
    grad_attn = (own_keep * attn_scale * grad_middle).astype(BF16)
    proj_part = jnp.einsum("rd,rc->dc", grad_attn, context, preferred_element_type=F32)
    grad_context = jnp.einsum("rd,cd->rc", grad_attn, proj_use, preferred_element_type=F32)
    grad_context = grad_context.astype(BF16).reshape(rows, heads, HD)
    global_grad, local_grad = split_crops(grad_context, micro)
    grad_packed = join_crops(
        attend_backward(global_packed, global_keep, global_total, global_grad, factor),
        attend_backward(local_packed, local_keep, local_total, local_grad, factor),
        micro,
    )
    grad_packed = grad_packed.reshape(rows, 3 * D).astype(BF16)
    qkv_part = jnp.einsum("rd,rc->dc", first_low, grad_packed, preferred_element_type=F32)
    grad_first = jnp.einsum("rc,dc->rd", grad_packed, qkv_use, preferred_element_type=F32)
    attngain_part = jnp.sum(grad_first * unit_first, axis=0)
    grad_rows = grad_middle + layer_back(grad_first, attn_gain, unit_first, inverse_first)

    down_grad = scatter_sum(jnp.split(down_part, groups, axis=1), True).T
    up_grad = scatter_sum(jnp.split(up_part, groups, axis=1), False)
    proj_grad = scatter_sum(jnp.split(proj_part, groups, axis=1), True).T
    qkv_grad = scatter_sum(jnp.split(qkv_part, groups, axis=1), False)
    small = jnp.stack([attngain_part, attnscale_part, mlpgain_part, mlpscale_part])
    small = lax.psum(small, ("dp", "tensor"))
    width = D // shards
    small = lax.dynamic_slice_in_dim(small, lax.axis_index("dp") * width, width, axis=1)
    return (
        block_rows.astype(BF16).reshape(tokens.shape),
        grad_rows.astype(BF16).reshape(tokens.shape),
        small[0],
        qkv_grad,
        proj_grad,
        small[1],
        small[2],
        up_grad,
        down_grad,
        small[3],
    )


def solution(mesh):
    in_specs = (
        P(None, ("dp", "tensor"), None),
        P(None, ("dp", "tensor"), None),
        P("dp", None),
        P("dp", None),
        P(),
        P(None, "tensor"),
        P("tensor", None),
        P(),
        P(),
        P(None, "tensor"),
        P("tensor", None),
        P(),
    )
    out_specs = (
        P(None, ("dp", "tensor"), None),
        P(None, ("dp", "tensor"), None),
        P("dp"),
        P("dp", "tensor"),
        P("tensor", "dp"),
        P("dp"),
        P("dp"),
        P("dp", "tensor"),
        P("tensor", "dp"),
        P("dp"),
    )
    return jax.shard_map(body, mesh=mesh, in_specs=in_specs, out_specs=out_specs, check_vma=False)
```

```python
import math

import jax
import jax.numpy as jnp
from jax import lax
from jax.experimental import pallas as pl
from jax.experimental.pallas import tpu as pltpu
from jax.sharding import PartitionSpec as P

D = 768
HD = 64
GLEN = 197
GPAD = 200
LLEN = 37
LPAD = 40
SLOT = GPAD + 2 * LPAD
GROW = 208
LROW = 2 * LPAD
BLOCK = GROW + LROW
FACTOR = HD ** (-0.5)
HEAD_COLS = 640
F32 = jnp.float32
BF16 = jnp.bfloat16
NN = (((1,), (0,)), ((), ()))
NT = (((1,), (1,)), ((), ()))
TN = (((0,), (0,)), ((), ()))
MIB = 1024 * 1024


def dot(left, right, dims=NN):
    return lax.dot_general(left, right, dims, preferred_element_type=F32)


def pad_rows(values):
    return jnp.concatenate(
        [values[:GPAD], jnp.zeros((GROW - GPAD, values.shape[1]), values.dtype), values[GPAD:]], axis=0
    )


def drop_rows(values):
    return jnp.concatenate([values[:GPAD], values[GROW:]], axis=0)


def row_keep(info_ref, micro, groups):
    member = info_ref[0]
    row = lax.broadcasted_iota(jnp.int32, (BLOCK, 1), 0)
    live = jnp.where(member < info_ref[1 + micro], GLEN, 0)
    first = jnp.where(member < info_ref[3 + micro], LLEN, 0)
    second = jnp.where(member + groups < info_ref[3 + micro], LLEN, 0)
    keep = (
        (row < live)
        | ((row >= GROW) & (row < GROW + first))
        | ((row >= GROW + LPAD) & (row < GROW + LPAD + second))
    )
    return jnp.where(keep, 1.0, 0.0).astype(F32)


def global_mask(info_ref, micro, axis):
    shape = (1, GROW) if axis == 1 else (GROW, 1)
    key = lax.broadcasted_iota(jnp.int32, shape, axis)
    live = jnp.where(info_ref[0] < info_ref[1 + micro], GLEN, 0)
    fill = jnp.where(key < GPAD, -30000.0, -3e38).astype(F32)
    return key < live, fill


def local_mask(info_ref, micro, groups, axis):
    key = lax.broadcasted_iota(jnp.int32, (LROW, LROW), axis)
    query = lax.broadcasted_iota(jnp.int32, (LROW, LROW), 1 - axis)
    member = info_ref[0]
    first = jnp.where(member < info_ref[3 + micro], LLEN, 0)
    second = jnp.where(member + groups < info_ref[3 + micro], LLEN, 0)
    same = (key < LPAD) == (query < LPAD)
    alive = (key < first) | ((key >= LPAD) & (key < LPAD + second))
    fill = jnp.where(same, -30000.0, -3e38).astype(F32)
    return same & alive, fill


def unit_rows(values):
    center = values - jnp.mean(values, axis=-1, keepdims=True)
    inverse = lax.rsqrt(jnp.mean(center * center, axis=-1, keepdims=True) + 1e-06)
    return center * inverse, inverse


def norm_back(grad_norm, gain, unit, inverse):
    scaled = grad_norm * gain
    centered = scaled - jnp.mean(scaled, axis=-1, keepdims=True)
    return inverse * (centered - unit * jnp.mean(scaled * unit, axis=-1, keepdims=True))


def low_half(tile):
    lane = lax.broadcasted_iota(jnp.int32, tile.shape, 1)
    return jnp.where(lane < HD, tile, jnp.zeros_like(tile))


def high_half(tile):
    lane = lax.broadcasted_iota(jnp.int32, tile.shape, 1)
    return jnp.where(lane < HD, jnp.zeros_like(tile), tile)


def turn(tile):
    return pltpu.roll(tile.astype(F32), HD, 1).astype(tile.dtype)


def softmax_rows(scores, live, fill):
    scores = jnp.where(live, scores * FACTOR, fill)
    raised = jnp.exp(scores - jnp.max(scores, axis=1, keepdims=True))
    return (raised * (1.0 / jnp.sum(raised, axis=1, keepdims=True))).astype(BF16)


def softmax_columns(scores, live, fill):
    scores = jnp.where(live, scores * FACTOR, fill)
    raised = jnp.exp(scores - jnp.max(scores, axis=0, keepdims=True))
    return raised * (1.0 / jnp.sum(raised, axis=0, keepdims=True))


def prepare_kernel(
    groups, info_ref, tokens_ref, grad_ref, gain_ref, scale_ref, norm_ref, norm_t_ref, gmlp_ref, gmlp_t_ref
):
    for micro in range(2):
        rows = slice(micro * BLOCK, (micro + 1) * BLOCK)
        values = pad_rows(tokens_ref[micro].astype(F32))
        unit, _ = unit_rows(values)
        norm_ref[rows, :] = (unit * gain_ref[...]).astype(BF16)
        keep = row_keep(info_ref, micro, groups)
        grad = pad_rows(grad_ref[micro].astype(F32))
        gmlp_ref[rows, :] = (keep * scale_ref[...] * grad).astype(BF16)
    norm_t_ref[...] = norm_ref[...].T
    gmlp_t_ref[...] = gmlp_ref[...].T


def attend_kernel(groups, first, last, *refs):
    info_ref, norm_ref, w_ref = refs[:3]
    at = 3
    if not first:
        acc_ref = refs[at]
        at += 1
    if last:
        tokens_ref, scale_ref, gain_ref = refs[at : at + 3]
        at += 3
    packed_ref, ctx_ref, out_ref = refs[at : at + 3]
    at += 3
    if last:
        middle_ref, norm_two_ref, norm_two_t_ref = refs[at : at + 3]
    packed_ref[...] = dot(norm_ref[...], w_ref[:, :HEAD_COLS]).astype(BF16)
    for micro in range(2):
        masks = (
            global_mask(info_ref, micro, 1),
            local_mask(info_ref, micro, groups, 1),
        )
        for part in range(2):
            start = micro * BLOCK + (0, GROW)[part]
            rows = slice(start, start + (GROW, LROW)[part])
            live, fill = masks[part]
            t0, t1, t2, t3, t4 = (packed_ref[rows, 128 * i : 128 * i + 128] for i in range(5))
            t0r, t1r, t2r, t3r, t4r = turn(t0), turn(t1), turn(t2), turn(t3), turn(t4)
            pa = softmax_rows(dot(low_half(t0), t0r, NT), live, fill)
            ctx_ref[rows, :128] = dot(pa, high_half(t1r)).astype(BF16)
            pb = softmax_rows(dot(high_half(t1), t2r, NT), live, fill)
            pc = softmax_rows(dot(low_half(t3), t3r, NT), live, fill)
            ctx_ref[rows, 128:] = (dot(pb, low_half(t2r)) + dot(pc, high_half(t4r))).astype(BF16)
    out = dot(ctx_ref[...], w_ref[:, 512:], NT)
    if not first:
        out = out + acc_ref[...]
    out_ref[...] = out
    if last:
        for micro in range(2):
            rows = slice(micro * BLOCK, (micro + 1) * BLOCK)
            keep = row_keep(info_ref, micro, groups)
            middle = pad_rows(tokens_ref[micro].astype(F32)) + keep * scale_ref[...] * out_ref[rows, :]
            middle_ref[rows, :] = middle
            unit, _ = unit_rows(middle)
            norm_two_ref[rows, :] = (unit * gain_ref[...]).astype(BF16)
        norm_two_t_ref[...] = norm_two_ref[...].T


def mlp_kernel(groups, first, last, *refs):
    norm_ref, norm_t_ref, gmlp_ref, gmlp_t_ref, up_ref, down_ref = refs[:6]
    at = 6
    if not first:
        mlp_in, grad_in = refs[at : at + 2]
        at += 2
    if last:
        info_ref, middle_ref, attn_ref, og_ref, gain_ref, mscale_ref, ascale_ref = refs[at : at + 7]
        at += 7
    wgrad_ref = refs[at]
    at += 1
    if not last:
        mlp_ref, grad_ref = refs[at : at + 2]
    else:
        block_ref, gmid_ref, gattn_ref, gattn_t_ref, small_ref, mlp_ref, grad_ref = refs[at : at + 7]
    step = pl.program_id(0)

    @pl.when(step == 0)
    def _():
        if first:
            mlp_ref[...] = jnp.zeros_like(mlp_ref)
            grad_ref[...] = jnp.zeros_like(grad_ref)
        else:
            mlp_ref[...] = mlp_in[...]
            grad_ref[...] = grad_in[...]

    up = up_ref[...]
    down = down_ref[...]
    hidden = dot(norm_ref[...], up)
    grad_active = dot(gmlp_ref[...], down, NT)
    cdf = 0.5 + 0.5 * lax.erf(hidden * (0.5**0.5))
    active = (hidden * cdf).astype(BF16)
    slope = cdf + hidden * (jnp.exp(-0.5 * hidden * hidden) * (1.0 / math.sqrt(2.0 * math.pi)))
    grad_hidden = (grad_active * slope).astype(BF16)
    mlp_ref[...] += dot(active, down)
    grad_ref[...] += dot(grad_hidden, up, NT)
    wgrad_ref[0] = dot(norm_t_ref[...], grad_hidden).astype(BF16)
    wgrad_ref[1] = dot(gmlp_t_ref[...], active).astype(BF16)

    if last:

        @pl.when(step == pl.num_programs(0) - 1)
        def _():
            small = [0.0, 0.0, 0.0]
            for micro in range(2):
                rows = slice(micro * BLOCK, (micro + 1) * BLOCK)
                keep = row_keep(info_ref, micro, groups)
                middle = middle_ref[rows, :]
                mlp = mlp_ref[rows, :]
                grad_out = pad_rows(og_ref[micro].astype(F32))
                block = middle + keep * mscale_ref[...] * mlp
                block_ref[micro] = drop_rows(block).astype(BF16)
                small[0] += jnp.sum(keep * mlp * grad_out, axis=0, keepdims=True)
                unit, inverse = unit_rows(middle)
                grad_two = grad_ref[rows, :]
                small[1] += jnp.sum(grad_two * unit, axis=0, keepdims=True)
                grad_mid = grad_out + norm_back(grad_two, gain_ref[...], unit, inverse)
                gmid_ref[rows, :] = grad_mid
                small[2] += jnp.sum(keep * attn_ref[rows, :] * grad_mid, axis=0, keepdims=True)
                gattn_ref[rows, :] = (keep * ascale_ref[...] * grad_mid).astype(BF16)
            gattn_t_ref[...] = gattn_ref[...].T
            small_ref[...] = jnp.concatenate(small, axis=0)


def attend_back_kernel(groups, *refs):
    info_ref, w_ref, packed_ref, ctx_ref, gattn_ref, gattn_t_ref, norm_t_ref = refs[:7]
    wgrad_ref, gpack_ref, gctx_ref = refs[7:]
    gctx_ref[...] = dot(gattn_ref[...], w_ref[:, 512:]).astype(BF16)
    for micro in range(2):
        masks = (
            global_mask(info_ref, micro, 0),
            local_mask(info_ref, micro, groups, 0),
        )
        for part in range(2):
            start = micro * BLOCK + (0, GROW)[part]
            rows = slice(start, start + (GROW, LROW)[part])
            live, fill = masks[part]
            t0, t1, t2, t3, t4 = (packed_ref[rows, 128 * i : 128 * i + 128] for i in range(5))
            g0, g1 = gctx_ref[rows, :128], gctx_ref[rows, 128:]
            t0r, t1r, t2r, t3r, t4r = turn(t0), turn(t1), turn(t2), turn(t3), turn(t4)
            g0r, g1r = turn(g0), turn(g1)

            def back(key, query, value, grad):
                probs = softmax_columns(dot(key, query, NT), live, fill)
                gp = dot(value, grad, NT)
                row_dot = jnp.sum(probs * gp, axis=0, keepdims=True)
                return probs.astype(BF16), (probs * (gp - row_dot) * FACTOR).astype(BF16)

            probs, gs = back(low_half(t0r), t0, high_half(t1r), g0)
            gpack_ref[rows, :128] = (dot(gs, low_half(t0r), TN) + dot(gs, high_half(t0r))).astype(BF16)
            dva = dot(probs, low_half(g0r))
            probs, gs = back(low_half(t2), t1r, low_half(t2r), g1)
            gpack_ref[rows, 128:256] = (dva + dot(gs, high_half(t2r), TN)).astype(BF16)
            gpack_ref[rows, 256:384] = (dot(gs, low_half(t1r)) + dot(probs, high_half(g1r))).astype(BF16)
            probs, gs = back(low_half(t3r), t3, high_half(t4r), g1)
            gpack_ref[rows, 384:512] = (dot(gs, low_half(t3r), TN) + dot(gs, high_half(t3r))).astype(BF16)
            gpack_ref[rows, 512:640] = dot(probs, low_half(g1r)).astype(BF16)
    wgrad_ref[0, :, :512] = dot(norm_t_ref[...], gpack_ref[:, :512]).astype(BF16)
    tail = dot(gattn_t_ref[...], ctx_ref[...])
    wgrad_ref[0, :, 512:640] = (dot(norm_t_ref[...], gpack_ref[:, 512:640]) + tail[:, :128]).astype(BF16)
    wgrad_ref[0, :, 640:] = tail[:, 128:].astype(BF16)


def input_back_kernel(*refs):
    gpacks, weights = refs[:4], refs[4:8]
    tokens_ref, gmid_ref, gain_ref, igrad_ref, small_ref, sum_ref = refs[8:]
    sum_ref[...] = dot(gpacks[0][...], weights[0][:, :HEAD_COLS], NT)
    for gpack_ref, w_ref in zip(gpacks[1:], weights[1:]):
        sum_ref[...] += dot(gpack_ref[...], w_ref[:, :HEAD_COLS], NT)
    small = 0.0
    for micro in range(2):
        rows = slice(micro * BLOCK, (micro + 1) * BLOCK)
        unit, inverse = unit_rows(pad_rows(tokens_ref[micro].astype(F32)))
        own = sum_ref[rows, :]
        small += jnp.sum(own * unit, axis=0, keepdims=True)
        back_rows = gmid_ref[rows, :] + norm_back(own, gain_ref[...], unit, inverse)
        igrad_ref[micro] = drop_rows(back_rows).astype(BF16)
    small_ref[...] = small


def assemble_kernel(info_ref, *refs):
    own_ref, one_ref, two_ref, three_a_ref, three_b_ref, out_ref = refs
    place = info_ref[0]
    out_ref[place] = own_ref[...]
    out_ref[place ^ 1] = one_ref[...]
    out_ref[place ^ 2] = two_ref[...]
    half = out_ref.shape[1] // 2
    out_ref[place ^ 3, :half] = three_a_ref[...]
    out_ref[place ^ 3, half:] = three_b_ref[...]


def add(left, right):
    return (left.astype(F32) + right.astype(F32)).astype(BF16)


THIRDS = (slice(0, 256), slice(256, 512), slice(512, 768))


def scatter_first_kernel(info_ref, *refs):
    g0, r1, g2, r3, give_a, give_b, give_c, keep_a, keep_b, keep_c = refs
    x, z = info_ref[1], info_ref[2]
    for i in range(g0.shape[0]):
        for s in range(8):
            give_a[i, s] = add(g2[i, s, :, THIRDS[0]], r3[i, s, :, THIRDS[0]])
            keep_a[i, s] = add(g0[i, s, :, THIRDS[0]], r1[i, s, :, THIRDS[0]])
        for side, (own, got) in enumerate(((g0, r1), (g2, r3))):
            for s in range(4):
                for out, pick in ((keep_b, x), (give_b, 1 - x)):
                    at = 2 * s + pick
                    out[i, side, s] = add(own[i, at, :, THIRDS[1]], got[i, at, :, THIRDS[1]])
                for out, pick in ((keep_c, z), (give_c, 1 - z)):
                    at = 4 * (s // 2) + 2 * pick + s % 2
                    out[i, side, s] = add(own[i, at, :, THIRDS[2]], got[i, at, :, THIRDS[2]])


def scatter_second_kernel(info_ref, *refs):
    old_a, old_b, old_c, got_a, got_b, got_c, give_a, give_b, give_c, keep_a, keep_b, keep_c = refs
    x, z = info_ref[1], info_ref[2]
    for i in range(old_a.shape[0]):
        for s in range(4):
            for out, pick in ((keep_a, x), (give_a, 1 - x)):
                out[i, s] = add(old_a[i, 2 * s + pick], got_a[i, 2 * s + pick])
            for side, out in enumerate((keep_c, give_c)):
                out[i, s] = add(old_c[i, side, s], got_c[i, side, s])
        for side in range(2):
            for s in range(2):
                for out, pick in ((keep_b, z), (give_b, 1 - z)):
                    out[i, side, s] = add(old_b[i, side, 2 * s + pick], got_b[i, side, 2 * s + pick])


def scatter_third_kernel(info_ref, *refs):
    old_a, old_b, old_c, got_a, got_b, got_c, give_a, give_b, give_c, keep_a, keep_b, keep_c = refs
    x, z = info_ref[1], info_ref[2]
    for i in range(old_a.shape[0]):
        for s in range(2):
            for out, pick in ((keep_a, z), (give_a, 1 - z)):
                out[i, s] = add(old_a[i, 2 * s + pick], got_a[i, 2 * s + pick])
            for side, out in enumerate((keep_b, give_b)):
                out[i, s] = add(old_b[i, side, s], got_b[i, side, s])
            for out, pick in ((keep_c, x), (give_c, 1 - x)):
                out[i, s] = add(old_c[i, 2 * s + pick], got_c[i, 2 * s + pick])


def scatter_fourth_kernel(info_ref, *refs):
    olds, gots, give, keep = refs[:3], refs[3:6], refs[6], refs[7]
    z = info_ref[3]
    for i in range(give.shape[0]):
        for old, got, third in zip(olds, gots, THIRDS):
            for out, pick in ((keep, z), (give, 1 - z)):
                out[i, :, third] = add(old[i, pick], got[i, pick])


def scatter_last_kernel(transposed, *refs):
    old, got = refs[:2]
    for i in range(old.shape[0]):
        total = old[i].astype(F32) + got[i].astype(F32)
        if transposed is None:
            refs[2][...] = total[:, :576]
            refs[3][...] = total.T[576:]
        else:
            refs[2 + i][...] = total.T if transposed[i] else total


VMEM = pl.BlockSpec(memory_space=pltpu.VMEM)
SMEM = pl.BlockSpec(memory_space=pltpu.SMEM)


def shape(dims, dtype):
    return jax.ShapeDtypeStruct(dims, dtype)


def call(kernel, args, outs, flops, scratch=(), limit=20):
    specs = [SMEM if a.dtype == jnp.int32 else VMEM for a in args]
    moved = sum(a.size * a.dtype.itemsize for a in args)
    moved += sum(math.prod(o.shape) * o.dtype.itemsize for o in outs)
    return pl.pallas_call(
        kernel,
        in_specs=specs,
        out_specs=[VMEM] * len(outs),
        out_shape=outs,
        scratch_shapes=list(scratch),
        compiler_params=pltpu.CompilerParams(vmem_limit_bytes=limit * MIB),
        cost_estimate=pl.CostEstimate(flops=flops, bytes_accessed=moved, transcendentals=0),
    )(*args)


def swap(value, axis, bit):
    size = lax.axis_size(axis)
    return lax.ppermute(value, axis, [(i, i ^ bit) for i in range(size)])


def fetch(value, info):
    blocks = value.reshape((4, value.shape[0] // 4, value.shape[1]))
    place = lax.axis_index("dp") % 4
    own = swap(lax.dynamic_index_in_dim(blocks, place, 0, keepdims=False), "tensor", 2)
    one = swap(own, "dp", 1)
    two = swap(own, "dp", 2)
    half = own.shape[0] // 2
    three_a = swap(two[:half], "dp", 1)
    three_b = swap(one[half:], "dp", 2)
    out = call(
        assemble_kernel,
        (info, own, one, two, three_a, three_b),
        (shape(blocks.shape, BF16),),
        1,
    )[0]
    return out.reshape(value.shape)


def gather_quarters(own, info):
    one = swap(own, "tensor", 1)
    two = fetch(own, info)
    three = swap(two, "tensor", 1)
    return [own, one, two, three]


def scatter_group(parts, info, finals, transposed):
    count = parts[0].shape[0]
    width = D // 8
    view = lambda a: a.reshape((count, 8, width, D))
    block = lambda *dims: shape((count,) + dims + (width, 256), BF16)
    got_one = swap(parts[1], "tensor", 1)
    got_three = swap(parts[3], "tensor", 1)
    send = {"y": ("tensor", 2), "x": ("dp", 1), "z": ("dp", 2)}

    def stage(kernel, args, outs, order):
        out = call(kernel, (info,) + args, outs + outs, 1)
        got = tuple(swap(give, *send[way]) for give, way in zip(out[:3], order))
        return tuple(out[3:]) + got

    args = (view(parts[0]), view(got_one), view(parts[2]), view(got_three))
    args = stage(scatter_first_kernel, args, (block(8), block(2, 4), block(2, 4)), "yxz")
    args = stage(scatter_second_kernel, args, (block(4), block(2, 2), block(4)), "xzy")
    args = stage(scatter_third_kernel, args, (block(2), block(2), block(2)), "zyx")
    whole = shape((count, width, D), BF16)
    give, keep = call(scatter_fourth_kernel, (info,) + args, (whole, whole), 1)
    got = swap(give, "dp", 4)

    def last(*refs):
        scatter_last_kernel(transposed, *refs)

    return call(last, (keep, got), finals, 1)


def dp_halve(value, bit):
    slices = value.shape[0]
    mine = (lax.axis_index("dp") // bit) % 2
    paired = value.reshape((slices // 2, 2) + value.shape[1:])
    keep = lax.dynamic_index_in_dim(paired, mine, 1, keepdims=False)
    give = lax.dynamic_index_in_dim(paired, 1 - mine, 1, keepdims=False)
    got = swap(give.astype(BF16), "dp", bit)
    return keep.astype(F32) + got.astype(F32)


def scatter_sum(parts, first_dp):
    shards = lax.axis_size("dp")
    zero = parts[0].astype(F32) + swap(parts[1], "tensor", 1).astype(F32)
    two = parts[2].astype(F32) + swap(parts[3], "tensor", 1).astype(F32)
    form = (shards, D // shards, parts[0].shape[1])
    zero = zero.reshape(form)
    two = two.reshape(form)
    bit = 1
    if first_dp:
        zero = dp_halve(zero, bit)
        two = dp_halve(two, bit)
        bit = 2
    zero = zero + swap(two.astype(BF16), "tensor", 2).astype(F32)
    while bit < shards:
        zero = dp_halve(zero, bit)
        bit = bit * 2
    return zero[0]


def body(
    tokens,
    out_grad,
    global_count,
    local_count,
    attn_gain,
    qkv_weight,
    proj_weight,
    attn_scale,
    mlp_gain,
    up_weight,
    down_weight,
    mlp_scale,
):
    groups = lax.axis_size("tensor")
    shards = lax.axis_size("dp")
    member = lax.axis_index("tensor")
    rows = 2 * BLOCK
    info = jnp.concatenate([member.astype(jnp.int32)[None], global_count[0], local_count[0]])
    row = lambda vector: vector.reshape(1, D)

    place = lax.axis_index("dp").astype(jnp.int32)
    where = jnp.stack([place % 4, place % 2, (place // 2) % 2, (place // 4) % 2])
    mixed = jnp.concatenate([qkv_weight, proj_weight.T], axis=1)
    wa = gather_quarters(mixed, where)
    up = gather_quarters(up_weight, where)
    down = gather_quarters(down_weight, where)

    act = shape((rows, D), BF16)
    act_t = shape((D, rows), BF16)
    acc = shape((rows, D), F32)
    packed = shape((rows, HEAD_COLS), BF16)
    ctx = shape((rows, 256), BF16)
    unit_flops = 2 * rows * D * D

    def bind(kernel, *flags):
        def run(*refs):
            return kernel(groups, *flags, *refs)

        return run

    norm, norm_t, gmlp, gmlp_t = call(
        bind(prepare_kernel),
        (info, tokens, out_grad, row(attn_gain), row(mlp_scale)),
        (act, act_t, act, act_t),
        rows * D * 40,
    )
    packs, ctxs, part = [], [], ()
    for r in range(4):
        last = r == 3
        got = call(
            bind(attend_kernel, r == 0, last),
            (info, norm, wa[r]) + part + ((tokens, row(attn_scale), row(mlp_gain)) if last else ()),
            (packed, ctx, acc) + ((acc, act, act_t) if last else ()),
            unit_flops,
        )
        packs.append(got[0])
        ctxs.append(got[1])
        part = (got[2],)
    attn_out = got[2]
    middle, norm_two, norm_two_t = got[3:]

    def mlp(quarter, carried, extra, outs, first, last):
        width = 256
        whole = lambda a: pl.BlockSpec(a.shape, lambda i: (0,) * len(a.shape))
        args = (norm_two, norm_two_t, gmlp, gmlp_t)
        specs = [whole(a) for a in args]
        specs += [
            pl.BlockSpec((D, width), lambda i: (0, i)),
            pl.BlockSpec((width, D), lambda i: (i, 0)),
        ]
        args = args + (up[quarter], down[quarter]) + carried + extra
        specs += [whole(a) for a in carried]
        specs += [SMEM if a.dtype == jnp.int32 else whole(a) for a in extra]
        hidden = up[quarter].shape[1]
        out_shape = [shape((2, D, hidden), BF16)] + list(outs)
        out_specs = [pl.BlockSpec((2, D, width), lambda i: (0, 0, i))] + [whole(o) for o in outs]
        return pl.pallas_call(
            bind(mlp_kernel, first, last),
            grid=(hidden // width,),
            in_specs=specs,
            out_specs=out_specs,
            out_shape=out_shape,
            scratch_shapes=[pltpu.VMEM((rows, D), F32)] * 2 if last else [],
            compiler_params=pltpu.CompilerParams(vmem_limit_bytes=30 * MIB),
            cost_estimate=pl.CostEstimate(
                flops=6 * unit_flops, bytes_accessed=12 * MIB, transcendentals=0
            ),
        )(*args)

    wg0, mlp_sum, grad_sum = mlp(0, (), (), (acc, acc), True, False)
    wg1, mlp_sum, grad_sum = mlp(1, (mlp_sum, grad_sum), (), (acc, acc), False, False)
    wg2, mlp_sum, grad_sum = mlp(2, (mlp_sum, grad_sum), (), (acc, acc), False, False)
    extra = (info, middle, attn_out, out_grad, row(mlp_gain), row(mlp_scale), row(attn_scale))
    outs = (shape(tokens.shape, BF16), acc, act, act_t, shape((3, D), F32))
    wg3, block_out, grad_mid, gattn, gattn_t, small_three = mlp(
        3, (mlp_sum, grad_sum), extra, outs, False, True
    )
    wgrads = (wg0, wg1, wg2, wg3)

    agrads, gpacks = [], []
    for r in range(4):
        grad, gpack = call(
            bind(attend_back_kernel),
            (info, wa[r], packs[r], ctxs[r], gattn, gattn_t, norm_t),
            (shape((1, D, D), BF16), packed),
            3 * unit_flops,
            scratch=[pltpu.VMEM((rows, 256), BF16)],
        )
        agrads.append(grad)
        gpacks.append(gpack)
    input_grad, small_one = call(
        input_back_kernel,
        tuple(gpacks) + tuple(wa) + (tokens, grad_mid, row(attn_gain)),
        (shape(tokens.shape, BF16), shape((1, D), F32)),
        3 * unit_flops,
        scratch=[pltpu.VMEM((rows, D), F32)],
    )
    width = D // shards
    split = qkv_weight.shape[1]
    if shards == 8:
        up_grad, down_grad = scatter_group(
            wgrads, where, (shape((width, D), F32), shape((D, width), F32)), (False, True)
        )
        qkv_grad, proj_grad = scatter_group(
            agrads, where, (shape((width, split), F32), shape((D - split, width), F32)), None
        )
    else:
        up_grad = scatter_sum([g[0] for g in wgrads], False)
        down_grad = scatter_sum([g[1] for g in wgrads], True).T
        mixed_grad = scatter_sum([g[0] for g in agrads], False)
        qkv_grad = mixed_grad[:, :split]
        proj_grad = mixed_grad[:, split:].T
    small = jnp.concatenate([small_three, small_one], axis=0)
    for bit in (1, 2):
        small = small + swap(small, "tensor", bit)
    bit = 1
    while bit < shards:
        small = small + swap(small, "dp", bit)
        bit = bit * 2
    small = lax.dynamic_slice_in_dim(small, lax.axis_index("dp") * width, width, axis=1)
    return (
        block_out,
        input_grad,
        small[3],
        qkv_grad,
        proj_grad,
        small[2],
        small[1],
        up_grad,
        down_grad,
        small[0],
    )


def solution(mesh):
    in_specs = (
        P(None, ("dp", "tensor"), None),
        P(None, ("dp", "tensor"), None),
        P("dp", None),
        P("dp", None),
        P(),
        P(None, "tensor"),
        P("tensor", None),
        P(),
        P(),
        P(None, "tensor"),
        P("tensor", None),
        P(),
    )
    out_specs = (
        P(None, ("dp", "tensor"), None),
        P(None, ("dp", "tensor"), None),
        P("dp"),
        P("dp", "tensor"),
        P("tensor", "dp"),
        P("dp"),
        P("dp"),
        P("dp", "tensor"),
        P("tensor", "dp"),
        P("dp"),
    )
    return jax.shard_map(body, mesh=mesh, in_specs=in_specs, out_specs=out_specs, check_vma=False)
```

```python
import math

import jax
import jax.numpy as jnp
from jax import lax
from jax.experimental import pallas as pl
from jax.experimental.pallas import tpu as pltpu
from jax.sharding import PartitionSpec as P

D = 768
HD = 64
GLEN = 197
GPAD = 200
LLEN = 37
LPAD = 40
SLOT = GPAD + 2 * LPAD
GROW = 208
LROW = 2 * LPAD
BLOCK = GROW + LROW
FACTOR = HD ** (-0.5)
HEAD_COLS = 640
F32 = jnp.float32
BF16 = jnp.bfloat16
NN = (((1,), (0,)), ((), ()))
NT = (((1,), (1,)), ((), ()))
TN = (((0,), (0,)), ((), ()))
MIB = 1024 * 1024


def dot(left, right, dims=NN):
    return lax.dot_general(left, right, dims, preferred_element_type=F32)


def pad_rows(values):
    return jnp.concatenate(
        [values[:GPAD], jnp.zeros((GROW - GPAD, values.shape[1]), values.dtype), values[GPAD:]], axis=0
    )


def drop_rows(values):
    return jnp.concatenate([values[:GPAD], values[GROW:]], axis=0)


def row_keep(info_ref, micro, groups):
    member = info_ref[0]
    row = lax.broadcasted_iota(jnp.int32, (BLOCK, 1), 0)
    live = jnp.where(member < info_ref[1 + micro], GLEN, 0)
    first = jnp.where(member < info_ref[3 + micro], LLEN, 0)
    second = jnp.where(member + groups < info_ref[3 + micro], LLEN, 0)
    keep = (
        (row < live)
        | ((row >= GROW) & (row < GROW + first))
        | ((row >= GROW + LPAD) & (row < GROW + LPAD + second))
    )
    return jnp.where(keep, 1.0, 0.0).astype(F32)


def global_mask(info_ref, micro, axis):
    shape = (1, GROW) if axis == 1 else (GROW, 1)
    key = lax.broadcasted_iota(jnp.int32, shape, axis)
    live = jnp.where(info_ref[0] < info_ref[1 + micro], GLEN, 0)
    fill = jnp.where(key < GPAD, -30000.0, -3e38).astype(F32)
    return key < live, fill


def local_mask(info_ref, micro, groups, axis):
    key = lax.broadcasted_iota(jnp.int32, (LROW, LROW), axis)
    query = lax.broadcasted_iota(jnp.int32, (LROW, LROW), 1 - axis)
    member = info_ref[0]
    first = jnp.where(member < info_ref[3 + micro], LLEN, 0)
    second = jnp.where(member + groups < info_ref[3 + micro], LLEN, 0)
    same = (key < LPAD) == (query < LPAD)
    alive = (key < first) | ((key >= LPAD) & (key < LPAD + second))
    fill = jnp.where(same, -30000.0, -3e38).astype(F32)
    return same & alive, fill


def unit_rows(values):
    center = values - jnp.mean(values, axis=-1, keepdims=True)
    inverse = lax.rsqrt(jnp.mean(center * center, axis=-1, keepdims=True) + 1e-06)
    return center * inverse, inverse


def norm_back(grad_norm, gain, unit, inverse):
    scaled = grad_norm * gain
    centered = scaled - jnp.mean(scaled, axis=-1, keepdims=True)
    return inverse * (centered - unit * jnp.mean(scaled * unit, axis=-1, keepdims=True))


def low_half(tile):
    lane = lax.broadcasted_iota(jnp.int32, tile.shape, 1)
    return jnp.where(lane < HD, tile, jnp.zeros_like(tile))


def high_half(tile):
    lane = lax.broadcasted_iota(jnp.int32, tile.shape, 1)
    return jnp.where(lane < HD, jnp.zeros_like(tile), tile)


def turn(tile):
    return pltpu.roll(tile.astype(F32), HD, 1).astype(tile.dtype)


def softmax_rows(scores, live, fill):
    scores = jnp.where(live, scores * FACTOR, fill)
    raised = jnp.exp(scores - jnp.max(scores, axis=1, keepdims=True))
    return (raised * (1.0 / jnp.sum(raised, axis=1, keepdims=True))).astype(BF16)


def softmax_columns(scores, live, fill):
    scores = jnp.where(live, scores * FACTOR, fill)
    raised = jnp.exp(scores - jnp.max(scores, axis=0, keepdims=True))
    return raised * (1.0 / jnp.sum(raised, axis=0, keepdims=True))


def start_kernel(info_ref, *refs):
    qkv_hbm, proj_hbm, up_hbm, down_hbm, mixed_ref, block_ref, block_b, qkv_ref, proj_ref, sems = refs
    place = info_ref[5]
    quarter = D // 4
    half = D // 2
    copies = [pltpu.make_async_copy(proj_hbm, proj_ref, sems.at[4])]
    for i in range(4):
        rows = pl.ds(i * quarter, quarter)
        copies.append(pltpu.make_async_copy(qkv_hbm.at[rows], qkv_ref.at[rows], sems.at[i]))
    for copy in copies:
        copy.start()
    chosen = pl.ds(pl.multiple_of((place % 2) * half, half), half)

    @pl.when(place < 2)
    def _():
        pltpu.make_async_copy(up_hbm.at[chosen], block_b, sems.at[5]).start()

    @pl.when(place >= 2)
    def _():
        pltpu.make_async_copy(down_hbm.at[chosen], block_b, sems.at[5]).start()

    for copy in copies:
        copy.wait()
    mixed_ref[:, :512] = qkv_ref[:, :512]
    mixed_ref[:, 512:] = jnp.concatenate([qkv_ref[:, 512:], proj_ref[...].T], axis=1)
    block_ref[...] = mixed_ref[pl.ds(pl.multiple_of(place * quarter, quarter), quarter), :]
    pltpu.make_async_copy(up_hbm.at[chosen], block_b, sems.at[5]).wait()


def prepare_kernel(
    groups, info_ref, tokens_ref, grad_ref, gain_ref, scale_ref, norm_ref, norm_t_ref, gmlp_ref, gmlp_t_ref
):
    for micro in range(2):
        rows = slice(micro * BLOCK, (micro + 1) * BLOCK)
        values = pad_rows(tokens_ref[micro].astype(F32))
        unit, _ = unit_rows(values)
        norm_ref[rows, :] = (unit * gain_ref[...]).astype(BF16)
        keep = row_keep(info_ref, micro, groups)
        grad = pad_rows(grad_ref[micro].astype(F32))
        gmlp_ref[rows, :] = (keep * scale_ref[...] * grad).astype(BF16)
    norm_t_ref[...] = norm_ref[...].T
    gmlp_t_ref[...] = gmlp_ref[...].T


def attend_kernel(groups, first, last, *refs):
    info_ref, norm_ref, w_ref = refs[:3]
    at = 3
    if not first:
        acc_ref = refs[at]
        at += 1
    if last:
        tokens_ref, scale_ref, gain_ref = refs[at : at + 3]
        at += 3
    packed_ref, ctx_ref, out_ref = refs[at : at + 3]
    at += 3
    if last:
        middle_ref, norm_two_ref, norm_two_t_ref = refs[at : at + 3]
    packed_ref[...] = dot(norm_ref[...], w_ref[:, :HEAD_COLS]).astype(BF16)
    for micro in range(2):
        masks = (
            global_mask(info_ref, micro, 1),
            local_mask(info_ref, micro, groups, 1),
        )
        for part in range(2):
            start = micro * BLOCK + (0, GROW)[part]
            rows = slice(start, start + (GROW, LROW)[part])
            live, fill = masks[part]
            t0, t1, t2, t3, t4 = (packed_ref[rows, 128 * i : 128 * i + 128] for i in range(5))
            t0r, t1r, t2r, t3r, t4r = turn(t0), turn(t1), turn(t2), turn(t3), turn(t4)
            pa = softmax_rows(dot(low_half(t0), t0r, NT), live, fill)
            ctx_ref[rows, :128] = dot(pa, high_half(t1r)).astype(BF16)
            pb = softmax_rows(dot(high_half(t1), t2r, NT), live, fill)
            pc = softmax_rows(dot(low_half(t3), t3r, NT), live, fill)
            ctx_ref[rows, 128:] = (dot(pb, low_half(t2r)) + dot(pc, high_half(t4r))).astype(BF16)
    out = dot(ctx_ref[...], w_ref[:, 512:], NT)
    if not first:
        out = out + acc_ref[...]
    out_ref[...] = out
    if last:
        for micro in range(2):
            rows = slice(micro * BLOCK, (micro + 1) * BLOCK)
            keep = row_keep(info_ref, micro, groups)
            middle = pad_rows(tokens_ref[micro].astype(F32)) + keep * scale_ref[...] * out_ref[rows, :]
            middle_ref[rows, :] = middle
            unit, _ = unit_rows(middle)
            norm_two_ref[rows, :] = (unit * gain_ref[...]).astype(BF16)
        norm_two_t_ref[...] = norm_two_ref[...].T


def mlp_kernel(groups, first, last, joined, *refs):
    info_ref, norm_ref, norm_t_ref, gmlp_ref, gmlp_t_ref = refs[:5]
    at = 5
    if joined:
        both_ref = refs[at]
        at += 1
    else:
        up_ref, down_ref = refs[at : at + 2]
        at += 2
    if not first:
        mlp_in, grad_in = refs[at : at + 2]
        at += 2
    if last:
        middle_ref, attn_ref, og_ref, gain_ref, mscale_ref, ascale_ref = refs[at : at + 6]
        at += 6
    wgrad_ref = refs[at]
    at += 1
    if not last:
        mlp_ref, grad_ref = refs[at : at + 2]
    else:
        block_ref, gmid_ref, gattn_ref, gattn_t_ref, small_ref, mlp_ref, grad_ref = refs[at : at + 7]
    width = 256
    for c in range(D // width):
        cols = slice(c * width, (c + 1) * width)
        if joined:
            up = both_ref[:2, :, cols].reshape(D, width)
            half = D // 2
            pieces = []
            for h in range(2):
                low = max(c * width, h * half)
                high = min((c + 1) * width, (h + 1) * half)
                if low < high:
                    pieces.append(both_ref[2 + h, low - h * half : high - h * half, :])
            down = pieces[0] if len(pieces) == 1 else jnp.concatenate(pieces, axis=0)
        else:
            up = up_ref[:, cols]
            down = down_ref[cols, :]
        hidden = dot(norm_ref[...], up)
        grad_active = dot(gmlp_ref[...], down, NT)
        cdf = 0.5 + 0.5 * lax.erf(hidden * (0.5**0.5))
        active = (hidden * cdf).astype(BF16)
        slope = cdf + hidden * (jnp.exp(-0.5 * hidden * hidden) * (1.0 / math.sqrt(2.0 * math.pi)))
        grad_hidden = (grad_active * slope).astype(BF16)
        mlp = dot(active, down)
        grad = dot(grad_hidden, up, NT)
        if c > 0:
            mlp_ref[...] += mlp
            grad_ref[...] += grad
        elif first:
            mlp_ref[...] = mlp
            grad_ref[...] = grad
        else:
            mlp_ref[...] = mlp_in[...] + mlp
            grad_ref[...] = grad_in[...] + grad
        wgrad_ref[0, :, cols] = dot(norm_t_ref[...], grad_hidden).astype(BF16)
        wgrad_ref[1, :, cols] = dot(gmlp_t_ref[...], active).astype(BF16)
    if last:
        small = [0.0, 0.0, 0.0]
        for micro in range(2):
            rows = slice(micro * BLOCK, (micro + 1) * BLOCK)
            keep = row_keep(info_ref, micro, groups)
            middle = middle_ref[rows, :]
            mlp = mlp_ref[rows, :]
            grad_out = pad_rows(og_ref[micro].astype(F32))
            block = middle + keep * mscale_ref[...] * mlp
            block_ref[micro] = drop_rows(block).astype(BF16)
            small[0] += jnp.sum(keep * mlp * grad_out, axis=0, keepdims=True)
            unit, inverse = unit_rows(middle)
            grad_two = grad_ref[rows, :]
            small[1] += jnp.sum(grad_two * unit, axis=0, keepdims=True)
            grad_mid = grad_out + norm_back(grad_two, gain_ref[...], unit, inverse)
            gmid_ref[rows, :] = grad_mid
            small[2] += jnp.sum(keep * attn_ref[rows, :] * grad_mid, axis=0, keepdims=True)
            gattn_ref[rows, :] = (keep * ascale_ref[...] * grad_mid).astype(BF16)
        gattn_t_ref[...] = gattn_ref[...].T
        small_ref[...] = jnp.concatenate(small, axis=0)


def attend_back_kernel(groups, *refs):
    info_ref, w_ref, packed_ref, ctx_ref, gattn_ref, gattn_t_ref, norm_t_ref = refs[:7]
    gpack_ref, low_ref, high_ref, gctx_ref = refs[7:]
    gctx_ref[...] = dot(gattn_ref[...], w_ref[:, 512:]).astype(BF16)
    for micro in range(2):
        masks = (
            global_mask(info_ref, micro, 0),
            local_mask(info_ref, micro, groups, 0),
        )
        for part in range(2):
            start = micro * BLOCK + (0, GROW)[part]
            rows = slice(start, start + (GROW, LROW)[part])
            live, fill = masks[part]
            t0, t1, t2, t3, t4 = (packed_ref[rows, 128 * i : 128 * i + 128] for i in range(5))
            g0, g1 = gctx_ref[rows, :128], gctx_ref[rows, 128:]
            t0r, t1r, t2r, t3r, t4r = turn(t0), turn(t1), turn(t2), turn(t3), turn(t4)
            g0r, g1r = turn(g0), turn(g1)

            def back(key, query, value, grad):
                probs = softmax_columns(dot(key, query, NT), live, fill)
                gp = dot(value, grad, NT)
                row_dot = jnp.sum(probs * gp, axis=0, keepdims=True)
                return probs.astype(BF16), (probs * (gp - row_dot) * FACTOR).astype(BF16)

            probs, gs = back(low_half(t0r), t0, high_half(t1r), g0)
            gpack_ref[rows, :128] = (dot(gs, low_half(t0r), TN) + dot(gs, high_half(t0r))).astype(BF16)
            dva = dot(probs, low_half(g0r))
            probs, gs = back(low_half(t2), t1r, low_half(t2r), g1)
            gpack_ref[rows, 128:256] = (dva + dot(gs, high_half(t2r), TN)).astype(BF16)
            gpack_ref[rows, 256:384] = (dot(gs, low_half(t1r)) + dot(probs, high_half(g1r))).astype(BF16)
            probs, gs = back(low_half(t3r), t3, high_half(t4r), g1)
            gpack_ref[rows, 384:512] = (dot(gs, low_half(t3r), TN) + dot(gs, high_half(t3r))).astype(BF16)
            gpack_ref[rows, 512:640] = dot(probs, low_half(g1r)).astype(BF16)
    half = D // 2
    for top, out in enumerate((low_ref, high_ref)):
        rows = slice(top * half, (top + 1) * half)
        norm_t = norm_t_ref[rows, :]
        out[0, :, :512] = dot(norm_t, gpack_ref[:, :512]).astype(BF16)
        tail = dot(gattn_t_ref[rows, :], ctx_ref[...])
        out[0, :, 512:640] = (dot(norm_t, gpack_ref[:, 512:640]) + tail[:, :128]).astype(BF16)
        out[0, :, 640:] = tail[:, 128:].astype(BF16)


def input_back_kernel(info_ref, *refs):
    gpacks, weights = refs[:4], refs[4:8]
    tokens_ref, gmid_ref, gain_ref, three_ref, igrad_ref, small_ref, sum_ref = refs[8:]
    sum_ref[...] = dot(gpacks[0][...], weights[0][:, :HEAD_COLS], NT)
    for gpack_ref, w_ref in zip(gpacks[1:], weights[1:]):
        sum_ref[...] += dot(gpack_ref[...], w_ref[:, :HEAD_COLS], NT)
    small = 0.0
    for micro in range(2):
        rows = slice(micro * BLOCK, (micro + 1) * BLOCK)
        unit, inverse = unit_rows(pad_rows(tokens_ref[micro].astype(F32)))
        own = sum_ref[rows, :]
        small += jnp.sum(own * unit, axis=0, keepdims=True)
        back_rows = gmid_ref[rows, :] + norm_back(own, gain_ref[...], unit, inverse)
        igrad_ref[micro] = drop_rows(back_rows).astype(BF16)
    small_ref[...] = jnp.concatenate([three_ref[...], small], axis=0)


def assemble_kernel(info_ref, *refs):
    own_ref, one_ref, two_ref = refs[:3]
    out_ref = refs[-1]
    place = info_ref[5]
    out_ref[place] = own_ref[...]
    out_ref[place ^ 1] = one_ref[...]
    out_ref[place ^ 2] = two_ref[...]
    if len(refs) == 5:
        out_ref[place ^ 3] = refs[3][...]
    else:
        half = out_ref.shape[1] // 2
        out_ref[place ^ 3, :half] = refs[3][...]
        out_ref[place ^ 3, half:] = refs[4][...]


def add(left, right):
    return (left.astype(F32) + right.astype(F32)).astype(BF16)


THIRDS = (slice(0, 256), slice(256, 512), slice(512, 768))


def sum_refs(refs):
    total = refs[0][...]
    for ref in refs[1:]:
        total = total + ref[...]
    return total


def halve_first(sources, count, info_ref, gives, keeps, base):
    x, z = info_ref[6], info_ref[7]
    give_y, give_x, give_z = gives
    keep_a, keep_b, keep_c = keeps

    def pair(low, third, i, high, s):
        return add(sources(low, third, i, high, s), sources(low + 1, third, i, high, s))

    for i in range(count):
        for s in range(8):
            give_y[base + 8 * i + s] = pair(2, 0, i, s // 4, s % 4)
            keep_a[8 * i + s] = pair(0, 0, i, s // 4, s % 4)
        for side in range(2):
            for s in range(4):
                at = 8 * i + 4 * side + s
                low = 2 * (s % 2)
                keep_b[at] = pair(2 * side, 1, i, s // 2, low + x)
                give_x[base + at] = pair(2 * side, 1, i, s // 2, low + 1 - x)
                low = s % 2
                keep_c[at] = pair(2 * side, 2, i, s // 2, low + 2 * z)
                give_z[base + at] = pair(2 * side, 2, i, s // 2, low + 2 * (1 - z))


def halve_second(olds, gots, count, info_ref, gives, keeps):
    x, z = info_ref[6], info_ref[7]
    give_x, give_z, give_y = gives
    keep_a, keep_b, keep_c = keeps
    old_a, old_b, old_c = olds
    got_a, got_b, got_c = gots
    for i in range(count):
        for s in range(4):
            at, low = 4 * i + s, 8 * i + 2 * s
            keep_a[at] = add(old_a[low + x], got_a[low + x])
            give_x[at] = add(old_a[low + 1 - x], got_a[low + 1 - x])
            keep_c[at] = add(old_c[8 * i + s], got_c[8 * i + s])
            give_y[at] = add(old_c[8 * i + 4 + s], got_c[8 * i + 4 + s])
        for side in range(2):
            for s in range(2):
                at, low = 4 * i + 2 * side + s, 8 * i + 4 * side + 2 * s
                keep_b[at] = add(old_b[low + z], got_b[low + z])
                give_z[at] = add(old_b[low + 1 - z], got_b[low + 1 - z])


def halve_third(olds, gots, skip, count, info_ref, gives, keeps):
    x, z = info_ref[6], info_ref[7]
    give_z, give_y, give_x = gives
    keep_a, keep_b, keep_c = keeps
    old_a, old_b, old_c = olds
    got_a, got_b, got_c = gots
    for i in range(count):
        for s in range(2):
            at, low = 2 * i + s, 4 * i + 2 * s
            keep_a[at] = add(old_a[low + z], got_a[skip + low + z])
            give_z[at] = add(old_a[low + 1 - z], got_a[skip + low + 1 - z])
            low = 4 * i + s
            keep_b[at] = add(old_b[low], got_b[skip + low])
            give_y[at] = add(old_b[low + 2], got_b[skip + low + 2])
            low = 4 * i + 2 * s
            keep_c[at] = add(old_c[low + x], got_c[skip + low + x])
            give_x[at] = add(old_c[low + 1 - x], got_c[skip + low + 1 - x])


def halve_fourth(olds, gots, count, info_ref, give, keep):
    z = info_ref[8]
    for i in range(count):
        for old, got, third in zip(olds, gots, THIRDS):
            keep[i, :, third] = add(old[2 * i + z], got[2 * i + z])
            give[i, :, third] = add(old[2 * i + 1 - z], got[2 * i + 1 - z])


class Shifted:
    def __init__(self, ref, offset):
        self.ref = ref
        self.offset = offset

    def __getitem__(self, at):
        return self.ref[self.offset + at]

    def __setitem__(self, at, value):
        self.ref[self.offset + at] = value


def shift(refs, offset):
    return tuple(Shifted(ref, offset) for ref in refs)


def merge_zero_kernel(info_ref, *refs):
    parts, gives, keeps = refs[:4], refs[4:7], refs[7:10]

    def source(part, third, i, high, s):
        return parts[part][i, 4 * high + s, :, THIRDS[third]]

    halve_first(source, 2, info_ref, gives, keeps, 0)


def merge_one_kernel(info_ref, *refs):
    olds, gots, parts = refs[:3], refs[3:6], refs[6:14]
    give_y, give_x, give_z = refs[14:17]
    keeps_m, keeps_a = refs[17:20], refs[20:23]

    def source(part, third, i, high, s):
        return parts[2 * part + high][i, s, :, THIRDS[third]]

    halve_second(olds, gots, 2, info_ref, (give_x, give_z, give_y), keeps_m)
    halve_first(source, 1, info_ref, (give_y, give_x, give_z), keeps_a, 8)


def merge_two_kernel(info_ref, *refs):
    olds_m, olds_a = refs[:3], refs[3:6]
    got_y, got_x, got_z = refs[6:9]
    smalls = refs[9:11]
    give_y, give_x, give_z = refs[11:14]
    keeps_m, keeps_a, small_ref = refs[14:17], refs[17:20], refs[20]
    halve_third(
        olds_m, (got_x, got_z, got_y), 0, 2, info_ref, (give_z, give_y, give_x), keeps_m
    )
    halve_second(
        olds_a,
        shift((got_y, got_x, got_z), 8),
        1,
        info_ref,
        shift((give_x, give_z, give_y), 4),
        keeps_a,
    )
    small_ref[...] = sum_refs(smalls)


def merge_three_kernel(info_ref, *refs):
    olds_m, olds_a = refs[:3], refs[3:6]
    got_y, got_x, got_z = refs[6:9]
    smalls = refs[9:11]
    give_y, give_x, give_z, give_far = refs[11:15]
    keep_m, keeps_a, small_ref = refs[15], refs[16:19], refs[19]
    halve_fourth(olds_m, (got_z, got_y, got_x), 2, info_ref, give_far, keep_m)
    halve_third(
        olds_a, (got_x, got_z, got_y), 4, 1, info_ref, (give_z, give_y, give_x), keeps_a
    )
    small_ref[...] = sum_refs(smalls)


def merge_four_kernel(info_ref, *refs):
    old_m, olds_a = refs[0], refs[1:4]
    got_y, got_x, got_z, got_far = refs[4:8]
    smalls = refs[8:10]
    give_far, keep_a, up_ref, down_ref, small_ref = refs[10:]
    halve_fourth(olds_a, (got_z, got_y, got_x), 1, info_ref, give_far, keep_a)
    small_ref[...] = sum_refs(smalls)
    up_ref[...] = old_m[0].astype(F32) + got_far[0].astype(F32)
    down_ref[...] = (old_m[1].astype(F32) + got_far[1].astype(F32)).T


def merge_last_kernel(info_ref, *refs):
    old, got = refs[:2]
    small = sum_refs(refs[2:6])
    qkv_ref, proj_ref = refs[6:8]
    total = old[0].astype(F32) + got[0].astype(F32)
    split = qkv_ref.shape[1]
    qkv_ref[...] = total[:, :split]
    proj_ref[...] = total.T[split:]
    width = small.shape[1] // 8
    place = info_ref[5] + 4 * info_ref[8]
    for d in range(8):

        @pl.when(place == d)
        def _():
            for i, ref in enumerate(refs[8:]):
                ref[...] = small[i : i + 1, d * width : (d + 1) * width]


VMEM = pl.BlockSpec(memory_space=pltpu.VMEM)
ANY = pl.BlockSpec(memory_space=pl.ANY)
SMEM = pl.BlockSpec(memory_space=pltpu.SMEM)


def shape(dims, dtype):
    return jax.ShapeDtypeStruct(dims, dtype)


class Order:
    def __init__(self, info):
        self.info = info

    def call(self, kernel, args, outs, scratch=(), limit=16, spaces=None):
        specs = [SMEM] + [VMEM] * len(args)
        out_specs = [VMEM] * len(outs)
        if spaces is not None:
            specs[1:] = spaces[0]
            out_specs = spaces[1]
        out = pl.pallas_call(
            kernel,
            in_specs=specs,
            out_specs=out_specs,
            out_shape=outs,
            scratch_shapes=list(scratch),
            compiler_params=pltpu.CompilerParams(vmem_limit_bytes=limit * MIB),
            cost_estimate=pl.CostEstimate(flops=1000, bytes_accessed=1000, transcendentals=0),
        )(self.info, *args)
        self.info = after(self.info, out[0])
        return out


def swap(value, axis, bit):
    size = lax.axis_size(axis)
    return lax.ppermute(value, axis, [(i, i ^ bit) for i in range(size)])


def after(value, *others):
    return lax.optimization_barrier((value,) + others)[0]


def second_hop(own):
    return swap(own, "dp", 1), swap(own, "dp", 2)


def third_hop(one, two):
    half = one.shape[0] // 2
    return swap(two[:half], "dp", 1), swap(one[half:], "dp", 2)


def assemble(order, pieces):
    dims = (4,) + pieces[0].shape
    return order.call(assemble_kernel, tuple(pieces), (shape(dims, BF16),))[0]


def swap_y(value):
    return swap(value, "tensor", 2)


def swap_x(value):
    return swap(value, "dp", 1)


def swap_z(value):
    return swap(value, "dp", 2)


def swap_far(value):
    return swap(value, "dp", 4)


def dp_halve(value, bit):
    slices = value.shape[0]
    mine = (lax.axis_index("dp") // bit) % 2
    paired = value.reshape((slices // 2, 2) + value.shape[1:])
    keep = lax.dynamic_index_in_dim(paired, mine, 1, keepdims=False)
    give = lax.dynamic_index_in_dim(paired, 1 - mine, 1, keepdims=False)
    got = swap(give.astype(BF16), "dp", bit)
    return keep.astype(F32) + got.astype(F32)


def scatter_sum(parts, first_dp):
    shards = lax.axis_size("dp")
    zero = parts[0].astype(F32) + swap(parts[1], "tensor", 1).astype(F32)
    two = parts[2].astype(F32) + swap(parts[3], "tensor", 1).astype(F32)
    form = (shards, D // shards, parts[0].shape[1])
    zero = zero.reshape(form)
    two = two.reshape(form)
    bit = 1
    if first_dp:
        zero = dp_halve(zero, bit)
        two = dp_halve(two, bit)
        bit = 2
    zero = zero + swap(two.astype(BF16), "tensor", 2).astype(F32)
    while bit < shards:
        zero = dp_halve(zero, bit)
        bit = bit * 2
    return zero[0]


def body(
    tokens,
    out_grad,
    global_count,
    local_count,
    attn_gain,
    qkv_weight,
    proj_weight,
    attn_scale,
    mlp_gain,
    up_weight,
    down_weight,
    mlp_scale,
):
    groups = lax.axis_size("tensor")
    shards = lax.axis_size("dp")
    rows = 2 * BLOCK
    place = lax.axis_index("dp").astype(jnp.int32)
    member = lax.axis_index("tensor").astype(jnp.int32)
    where = jnp.stack([place % 4, place % 2, (place // 2) % 2, (place // 4) % 2])
    info = jnp.concatenate([member[None], global_count[0], local_count[0], where])
    row = lambda vector: vector.reshape(1, D)

    act = shape((rows, D), BF16)
    act_t = shape((D, rows), BF16)
    acc = shape((rows, D), F32)
    packed = shape((rows, HEAD_COLS), BF16)
    ctx = shape((rows, 256), BF16)
    unit_flops = 2 * rows * D * D

    def bind(kernel, *flags):
        def run(*refs):
            return kernel(groups, *flags, *refs)

        return run

    order = Order(info)

    mixed, block_a, block_b = order.call(
        start_kernel,
        (qkv_weight, proj_weight, up_weight, down_weight),
        (shape((D, D), BF16), shape((D // 4, D), BF16), shape((D // 2, D), BF16)),
        scratch=[
            pltpu.VMEM(qkv_weight.shape, BF16),
            pltpu.VMEM(proj_weight.shape, BF16),
            pltpu.SemaphoreType.DMA((6,)),
        ],
        spaces=([ANY] * 4, [VMEM, VMEM, ANY]),
    )
    own_a = swap(block_a, "tensor", 2)
    wa = [mixed, swap(mixed, "tensor", 1)]
    norm, norm_t, gmlp, gmlp_t = order.call(
        bind(prepare_kernel),
        (tokens, out_grad, row(attn_gain), row(mlp_scale)),
        (act, act_t, act, act_t),
    )
    packs, ctxs = {}, {}

    def attend(r, part):
        last = r == 3
        got = order.call(
            bind(attend_kernel, r == 0, last),
            (norm, wa[r]) + part + ((tokens, row(attn_scale), row(mlp_gain)) if last else ()),
            (packed, ctx, acc) + ((acc, act, act_t) if last else ()),
        )
        packs[r], ctxs[r] = got[:2]
        return tuple(got[2:])

    half_rows = D // 2
    part = attend(0, ())
    own_a = after(own_a, part[0])
    one_a, two_a = second_hop(own_a)
    own_b = swap(after(block_b, own_a), "tensor", 2)
    part = attend(1, part)
    one_a, two_a = after((one_a, two_a), part[0])
    own_a = after(own_a, own_b)
    wa.append(assemble(order, (own_a, one_a, two_a) + third_hop(one_a, two_a)).reshape(D, D))
    wa.append(swap(wa[2], "tensor", 1))
    own_b = after(own_b, wa[2])
    one_b, two_b = second_hop(own_b)
    part = attend(2, part)
    up_one = swap(after(up_weight, part[0]), "tensor", 1)
    down_one = swap(after(down_weight, part[0]), "tensor", 1)
    attn_out, middle, norm_two, norm_two_t = attend(3, part)

    def mlp(weights, carried, extra, outs, first, last):
        return order.call(
            bind(mlp_kernel, first, last, len(weights) == 1),
            (norm_two, norm_two_t, gmlp, gmlp_t) + weights + carried + extra,
            (shape((2, D, D), BF16),) + tuple(outs),
            scratch=[pltpu.VMEM((rows, D), F32)] * 2 if last else [],
            limit=16,
        )

    wgrads = {}
    wgrads[0], mlp_sum, grad_sum = mlp((up_weight, down_weight), (), (), (acc, acc), True, False)
    one_b, two_b = after((one_b, two_b), mlp_sum)
    three_b = third_hop(one_b, two_b)
    wgrads[1], mlp_sum, grad_sum = mlp((up_one, down_one), (mlp_sum, grad_sum), (), (acc, acc), False, False)
    both_two = assemble(order, (own_b, one_b, two_b) + three_b)
    both_three = swap(both_two, "tensor", 1)
    got_one = swap(after(wgrads[1], both_two), "tensor", 1)
    wgrads[2], mlp_sum, grad_sum = mlp((both_two,), (mlp_sum, grad_sum), (), (acc, acc), False, False)
    extra = (middle, attn_out, out_grad, row(mlp_gain), row(mlp_scale), row(attn_scale))
    outs = (shape(tokens.shape, BF16), acc, act, act_t, shape((3, D), F32))
    wgrads[3], block_out, grad_mid, gattn, gattn_t, small = mlp(
        (both_three,), (mlp_sum, grad_sum), extra, outs, False, True
    )
    got_three = swap(wgrads[3], "tensor", 1)

    agrads, gpacks = {}, {}
    half = shape((1, D // 2, D), BF16)

    def back(r):
        out = order.call(
            bind(attend_back_kernel),
            (wa[r], packs[r], ctxs[r], gattn, gattn_t, norm_t),
            (packed, half, half),
            scratch=[pltpu.VMEM((rows, 256), BF16)],
        )
        gpacks[r] = out[0]
        agrads[r] = tuple(out[1:])

    def input_back():
        return order.call(
            input_back_kernel,
            tuple(gpacks[r] for r in range(4)) + tuple(wa) + (tokens, grad_mid, row(attn_gain), small),
            (shape(tokens.shape, BF16), shape((4, D), F32)),
            scratch=[pltpu.VMEM((rows, D), F32)],
        )

    width = D // shards
    split = qkv_weight.shape[1]
    back(1)
    if shards == 8:
        view = lambda a: a.reshape((a.shape[0], a.shape[1] // width, width, D))
        swap_core = lambda values: tuple(swap(value, "tensor", 1) for value in values)
        tiny = shape((4, D), F32)
        blocks = lambda count: shape((count, width, 256), BF16)
        whole = lambda count: shape((count, width, D), BF16)
        args = tuple(view(a) for a in (wgrads[0], got_one, wgrads[2], got_three))
        out = order.call(merge_zero_kernel, args, (blocks(16),) * 6)
        keeps_m = tuple(out[3:6])
        got_m = (swap_y(out[0]), swap_x(out[1]), swap_z(out[2]))
        got_one = swap_core(after(agrads[1], keeps_m[0]))
        back(3)
        got_three = swap_core(agrads[3])
        back(0)
        back(2)
        args = tuple(view(a) for a in agrads[0] + got_one + agrads[2] + got_three)
        out = order.call(
            merge_one_kernel, keeps_m + got_m + args, (blocks(16),) * 3 + (blocks(8),) * 6
        )
        keeps = tuple(out[3:9])
        got = (swap_y(out[0]), swap_x(out[1]), swap_z(out[2]))
        input_grad, small = input_back()
        smalls = (small, swap(small, "tensor", 1))
        out = order.call(
            merge_two_kernel, keeps + got + smalls, (blocks(8),) * 3 + (blocks(4),) * 6 + (tiny,)
        )
        keeps = tuple(out[3:9])
        got = (swap_y(out[0]), swap_x(out[1]), swap_z(out[2]))
        smalls = (out[9], swap_y(out[9]))
        out = order.call(
            merge_three_kernel,
            keeps + got + smalls,
            (blocks(2),) * 3 + (whole(2), whole(2)) + (blocks(2),) * 3 + (tiny,),
        )
        keeps = tuple(out[4:8])
        got = (swap_y(out[0]), swap_x(out[1]), swap_z(out[2]), swap_far(out[3]))
        smalls = (out[8], swap_x(out[8]))
        give, keep, up_grad, down_grad, small = order.call(
            merge_four_kernel,
            keeps + got + smalls,
            (whole(1), whole(1), shape((width, D), F32), shape((D, width), F32), tiny),
        )
        smalls = (small,) + tuple(swap(small, "dp", bit) for bit in (2, 4, 6))
        out = order.call(
            merge_last_kernel,
            (keep, swap_far(give)) + smalls,
            (shape((width, split), F32), shape((D - split, width), F32)) + (shape((1, width), F32),) * 4,
        )
        qkv_grad, proj_grad = out[:2]
        smalls = [value.reshape(width) for value in out[2:]]
    else:
        for r in (3, 0, 2):
            back(r)
        input_grad, small = input_back()
        up_grad = scatter_sum([wgrads[r][0] for r in range(4)], False)
        down_grad = scatter_sum([wgrads[r][1] for r in range(4)], True).T
        mixed_grad = scatter_sum([jnp.concatenate(agrads[r], axis=1)[0] for r in range(4)], False)
        qkv_grad = mixed_grad[:, :split]
        proj_grad = mixed_grad[:, split:].T
        small = lax.psum(small, ("dp", "tensor"))
        small = lax.dynamic_slice_in_dim(small, place * width, width, axis=1)
        smalls = [small[i] for i in range(4)]
    return (
        block_out,
        input_grad,
        smalls[3],
        qkv_grad,
        proj_grad,
        smalls[2],
        smalls[1],
        up_grad,
        down_grad,
        smalls[0],
    )


def solution(mesh):
    in_specs = (
        P(None, ("dp", "tensor"), None),
        P(None, ("dp", "tensor"), None),
        P("dp", None),
        P("dp", None),
        P(),
        P(None, "tensor"),
        P("tensor", None),
        P(),
        P(),
        P(None, "tensor"),
        P("tensor", None),
        P(),
    )
    out_specs = (
        P(None, ("dp", "tensor"), None),
        P(None, ("dp", "tensor"), None),
        P("dp"),
        P("dp", "tensor"),
        P("tensor", "dp"),
        P("dp"),
        P("dp"),
        P("dp", "tensor"),
        P("tensor", "dp"),
        P("dp"),
    )
    return jax.shard_map(body, mesh=mesh, in_specs=in_specs, out_specs=out_specs, check_vma=False)
```

```python
import math

import jax
import jax.numpy as jnp
from jax import lax
from jax.experimental import pallas as pl
from jax.experimental.pallas import tpu as pltpu
from jax.sharding import PartitionSpec as P

D = 768
HD = 64
GLEN = 197
GPAD = 200
LLEN = 37
LPAD = 40
SLOT = GPAD + 2 * LPAD
GROW = 208
LROW = 2 * LPAD
BLOCK = GROW + LROW
FACTOR = HD ** (-0.5)
HEAD_COLS = 640
F32 = jnp.float32
BF16 = jnp.bfloat16
NN = (((1,), (0,)), ((), ()))
NT = (((1,), (1,)), ((), ()))
TN = (((0,), (0,)), ((), ()))
MIB = 1024 * 1024


def dot(left, right, dims=NN):
    return lax.dot_general(left, right, dims, preferred_element_type=F32)


def pad_rows(values):
    return jnp.concatenate(
        [values[:GPAD], jnp.zeros((GROW - GPAD, values.shape[1]), values.dtype), values[GPAD:]], axis=0
    )


def drop_rows(values):
    return jnp.concatenate([values[:GPAD], values[GROW:]], axis=0)


def row_keep(info_ref, micro, groups):
    member = info_ref[0]
    row = lax.broadcasted_iota(jnp.int32, (BLOCK, 1), 0)
    live = jnp.where(member < info_ref[1 + micro], GLEN, 0)
    first = jnp.where(member < info_ref[3 + micro], LLEN, 0)
    second = jnp.where(member + groups < info_ref[3 + micro], LLEN, 0)
    keep = (
        (row < live)
        | ((row >= GROW) & (row < GROW + first))
        | ((row >= GROW + LPAD) & (row < GROW + LPAD + second))
    )
    return jnp.where(keep, 1.0, 0.0).astype(F32)


def global_mask(info_ref, micro, axis):
    shape = (1, GROW) if axis == 1 else (GROW, 1)
    key = lax.broadcasted_iota(jnp.int32, shape, axis)
    live = jnp.where(info_ref[0] < info_ref[1 + micro], GLEN, 0)
    fill = jnp.where(key < GPAD, -30000.0, -3e38).astype(F32)
    return key < live, fill


def local_mask(info_ref, micro, groups, axis):
    key = lax.broadcasted_iota(jnp.int32, (LROW, LROW), axis)
    query = lax.broadcasted_iota(jnp.int32, (LROW, LROW), 1 - axis)
    member = info_ref[0]
    first = jnp.where(member < info_ref[3 + micro], LLEN, 0)
    second = jnp.where(member + groups < info_ref[3 + micro], LLEN, 0)
    same = (key < LPAD) == (query < LPAD)
    alive = (key < first) | ((key >= LPAD) & (key < LPAD + second))
    fill = jnp.where(same, -30000.0, -3e38).astype(F32)
    return same & alive, fill


def unit_rows(values):
    center = values - jnp.mean(values, axis=-1, keepdims=True)
    inverse = lax.rsqrt(jnp.mean(center * center, axis=-1, keepdims=True) + 1e-06)
    return center * inverse, inverse


def norm_back(grad_norm, gain, unit, inverse):
    scaled = grad_norm * gain
    centered = scaled - jnp.mean(scaled, axis=-1, keepdims=True)
    return inverse * (centered - unit * jnp.mean(scaled * unit, axis=-1, keepdims=True))


def low_half(tile):
    lane = lax.broadcasted_iota(jnp.int32, tile.shape, 1)
    return jnp.where(lane < HD, tile, jnp.zeros_like(tile))


def high_half(tile):
    lane = lax.broadcasted_iota(jnp.int32, tile.shape, 1)
    return jnp.where(lane < HD, jnp.zeros_like(tile), tile)


def turn(tile):
    return pltpu.roll(tile.astype(F32), HD, 1).astype(tile.dtype)


def softmax_rows(scores, live, fill):
    scores = jnp.where(live, scores * FACTOR, fill)
    raised = jnp.exp(scores - jnp.max(scores, axis=1, keepdims=True))
    return (raised * (1.0 / jnp.sum(raised, axis=1, keepdims=True))).astype(BF16)


def softmax_columns(scores, live, fill):
    scores = jnp.where(live, scores * FACTOR, fill)
    raised = jnp.exp(scores - jnp.max(scores, axis=0, keepdims=True))
    return raised * (1.0 / jnp.sum(raised, axis=0, keepdims=True))


def start_kernel(qkv_hbm, proj_hbm, up_hbm, down_hbm, mixed_ref, block_ref, block_b, sems):
    place = lax.rem(lax.axis_index("dp"), 4)
    quarter = D // 4
    half = D // 2
    blocks = [qkv_hbm.at[pl.ds(i * quarter, quarter)] for i in range(3)] + [proj_hbm]
    for i, block in enumerate(blocks):
        pltpu.make_async_copy(block, mixed_ref.at[pl.ds(i * quarter, quarter)], sems.at[i]).start()
    chosen = pl.ds(pl.multiple_of(lax.rem(place, 2) * half, half), half)

    @pl.when(place < 2)
    def _():
        pltpu.make_async_copy(up_hbm.at[chosen], block_b, sems.at[4]).start()

    @pl.when(place >= 2)
    def _():
        pltpu.make_async_copy(down_hbm.at[chosen], block_b, sems.at[4]).start()

    for i, block in enumerate(blocks):
        pltpu.make_async_copy(block, mixed_ref.at[pl.ds(i * quarter, quarter)], sems.at[i]).wait()
    block_ref[...] = mixed_ref[pl.ds(pl.multiple_of(place * quarter, quarter), quarter), :]
    pltpu.make_async_copy(up_hbm.at[chosen], block_b, sems.at[4]).wait()


def prepare_kernel(
    groups, info_ref, tokens_ref, grad_ref, gain_ref, scale_ref, norm_ref, norm_t_ref, gmlp_ref, gmlp_t_ref
):
    for micro in range(2):
        rows = slice(micro * BLOCK, (micro + 1) * BLOCK)
        values = pad_rows(tokens_ref[micro].astype(F32))
        unit, _ = unit_rows(values)
        norm_ref[rows, :] = (unit * gain_ref[...]).astype(BF16)
        keep = row_keep(info_ref, micro, groups)
        grad = pad_rows(grad_ref[micro].astype(F32))
        gmlp_ref[rows, :] = (keep * scale_ref[...] * grad).astype(BF16)
    norm_t_ref[...] = norm_ref[...].T
    gmlp_t_ref[...] = gmlp_ref[...].T


def attend_kernel(groups, first, last, *refs):
    info_ref, norm_ref, w_ref = refs[:3]
    at = 3
    if not first:
        acc_ref = refs[at]
        at += 1
    if last:
        tokens_ref, scale_ref, gain_ref, up_hbm, down_hbm = refs[at : at + 5]
        at += 5
    packed_ref, ctx_ref, out_ref = refs[at : at + 3]
    at += 3
    if last:
        middle_ref, norm_two_ref, norm_two_t_ref, up_ref, down_ref, sems = refs[at : at + 6]
        fetches = (
            pltpu.make_async_copy(up_hbm, up_ref, sems.at[0]),
            pltpu.make_async_copy(down_hbm, down_ref, sems.at[1]),
        )
        for fetch in fetches:
            fetch.start()
    packed_ref[...] = dot(norm_ref[...], w_ref[:HEAD_COLS, :], NT).astype(BF16)
    for micro in range(2):
        masks = (
            global_mask(info_ref, micro, 1),
            local_mask(info_ref, micro, groups, 1),
        )
        for part in range(2):
            start = micro * BLOCK + (0, GROW)[part]
            rows = slice(start, start + (GROW, LROW)[part])
            live, fill = masks[part]
            t0, t1, t2, t3, t4 = (packed_ref[rows, 128 * i : 128 * i + 128] for i in range(5))
            t0r, t1r, t2r, t3r, t4r = turn(t0), turn(t1), turn(t2), turn(t3), turn(t4)
            pa = softmax_rows(dot(low_half(t0), t0r, NT), live, fill)
            ctx_ref[rows, :128] = dot(pa, high_half(t1r)).astype(BF16)
            pb = softmax_rows(dot(high_half(t1), t2r, NT), live, fill)
            pc = softmax_rows(dot(low_half(t3), t3r, NT), live, fill)
            ctx_ref[rows, 128:] = (dot(pb, low_half(t2r)) + dot(pc, high_half(t4r))).astype(BF16)
    out = dot(ctx_ref[...], w_ref[512:, :])
    if not first:
        out = out + acc_ref[...]
    out_ref[...] = out
    if last:
        for micro in range(2):
            rows = slice(micro * BLOCK, (micro + 1) * BLOCK)
            keep = row_keep(info_ref, micro, groups)
            middle = pad_rows(tokens_ref[micro].astype(F32)) + keep * scale_ref[...] * out_ref[rows, :]
            middle_ref[rows, :] = middle
            unit, _ = unit_rows(middle)
            norm_two_ref[rows, :] = (unit * gain_ref[...]).astype(BF16)
        norm_two_t_ref[...] = norm_two_ref[...].T
        for fetch in fetches:
            fetch.wait()


def mlp_kernel(groups, first, last, joined, *refs):
    info_ref, norm_ref, norm_t_ref, gmlp_ref, gmlp_t_ref = refs[:5]
    at = 5
    if joined:
        both_ref = refs[at]
        at += 1
    else:
        up_ref, down_ref = refs[at : at + 2]
        at += 2
    if not first:
        mlp_in, grad_in = refs[at : at + 2]
        at += 2
    if last:
        middle_ref, attn_ref, og_ref, gain_ref, mscale_ref, ascale_ref = refs[at : at + 6]
        at += 6
    wgrad_ref = refs[at]
    at += 1
    if not last:
        mlp_ref, grad_ref = refs[at : at + 2]
    else:
        block_ref, gmid_ref, gattn_ref, gattn_t_ref, small_ref, mlp_ref, grad_ref = refs[at : at + 7]
    width = 768
    for c in range(D // width):
        cols = slice(c * width, (c + 1) * width)
        if joined:
            up = both_ref[:2, :, cols].reshape(D, width)
            half = D // 2
            pieces = []
            for h in range(2):
                low = max(c * width, h * half)
                high = min((c + 1) * width, (h + 1) * half)
                if low < high:
                    pieces.append(both_ref[2 + h, low - h * half : high - h * half, :])
            down = pieces[0] if len(pieces) == 1 else jnp.concatenate(pieces, axis=0)
        else:
            up = up_ref[:, cols]
            down = down_ref[cols, :]
        hidden = dot(norm_ref[...], up)
        grad_active = dot(gmlp_ref[...], down, NT)
        cdf = 0.5 + 0.5 * lax.erf(hidden * (0.5**0.5))
        active = (hidden * cdf).astype(BF16)
        slope = cdf + hidden * (jnp.exp(-0.5 * hidden * hidden) * (1.0 / math.sqrt(2.0 * math.pi)))
        grad_hidden = (grad_active * slope).astype(BF16)
        mlp = dot(active, down)
        grad = dot(grad_hidden, up, NT)
        if c > 0:
            mlp_ref[...] += mlp
            grad_ref[...] += grad
        elif first:
            mlp_ref[...] = mlp
            grad_ref[...] = grad
        else:
            mlp_ref[...] = mlp_in[...] + mlp
            grad_ref[...] = grad_in[...] + grad
        wgrad_ref[0, :, cols] = dot(norm_t_ref[...], grad_hidden).astype(BF16)
        wgrad_ref[1, :, cols] = dot(gmlp_t_ref[...], active).astype(BF16)
    if last:
        small = [0.0, 0.0, 0.0]
        for micro in range(2):
            rows = slice(micro * BLOCK, (micro + 1) * BLOCK)
            keep = row_keep(info_ref, micro, groups)
            middle = middle_ref[rows, :]
            mlp = mlp_ref[rows, :]
            grad_out = pad_rows(og_ref[micro].astype(F32))
            block = middle + keep * mscale_ref[...] * mlp
            block_ref[micro] = drop_rows(block).astype(BF16)
            small[0] += jnp.sum(keep * mlp * grad_out, axis=0, keepdims=True)
            unit, inverse = unit_rows(middle)
            grad_two = grad_ref[rows, :]
            small[1] += jnp.sum(grad_two * unit, axis=0, keepdims=True)
            grad_mid = grad_out + norm_back(grad_two, gain_ref[...], unit, inverse)
            gmid_ref[rows, :] = grad_mid
            small[2] += jnp.sum(keep * attn_ref[rows, :] * grad_mid, axis=0, keepdims=True)
            gattn_ref[rows, :] = (keep * ascale_ref[...] * grad_mid).astype(BF16)
        gattn_t_ref[...] = gattn_ref[...].T
        small_ref[...] = jnp.concatenate(small, axis=0)


def attend_back_kernel(groups, *refs):
    info_ref, w_ref, packed_ref, ctx_ref, gattn_ref, gattn_t_ref, norm_t_ref = refs[:7]
    gpack_ref, low_ref, high_ref, gctx_ref = refs[7:]
    gctx_ref[...] = dot(gattn_ref[...], w_ref[512:, :], NT).astype(BF16)
    for micro in range(2):
        masks = (
            global_mask(info_ref, micro, 0),
            local_mask(info_ref, micro, groups, 0),
        )
        for part in range(2):
            start = micro * BLOCK + (0, GROW)[part]
            rows = slice(start, start + (GROW, LROW)[part])
            live, fill = masks[part]
            t0, t1, t2, t3, t4 = (packed_ref[rows, 128 * i : 128 * i + 128] for i in range(5))
            g0, g1 = gctx_ref[rows, :128], gctx_ref[rows, 128:]
            t0r, t1r, t2r, t3r, t4r = turn(t0), turn(t1), turn(t2), turn(t3), turn(t4)
            g0r, g1r = turn(g0), turn(g1)

            def back(key, query, value, grad):
                probs = softmax_columns(dot(key, query, NT), live, fill)
                gp = dot(value, grad, NT)
                row_dot = jnp.sum(probs * gp, axis=0, keepdims=True)
                return probs.astype(BF16), (probs * (gp - row_dot) * FACTOR).astype(BF16)

            probs, gs = back(low_half(t0r), t0, high_half(t1r), g0)
            gpack_ref[rows, :128] = (dot(gs, low_half(t0r), TN) + dot(gs, high_half(t0r))).astype(BF16)
            dva = dot(probs, low_half(g0r))
            probs, gs = back(low_half(t2), t1r, low_half(t2r), g1)
            gpack_ref[rows, 128:256] = (dva + dot(gs, high_half(t2r), TN)).astype(BF16)
            gpack_ref[rows, 256:384] = (dot(gs, low_half(t1r)) + dot(probs, high_half(g1r))).astype(BF16)
            probs, gs = back(low_half(t3r), t3, high_half(t4r), g1)
            gpack_ref[rows, 384:512] = (dot(gs, low_half(t3r), TN) + dot(gs, high_half(t3r))).astype(BF16)
            gpack_ref[rows, 512:640] = dot(probs, low_half(g1r)).astype(BF16)
    half = D // 2
    for top, out in enumerate((low_ref, high_ref)):
        rows = slice(top * half, (top + 1) * half)
        norm_t = norm_t_ref[rows, :]
        out[0, :, :512] = dot(norm_t, gpack_ref[:, :512]).astype(BF16)
        tail = dot(gattn_t_ref[rows, :], ctx_ref[...])
        out[0, :, 512:640] = (dot(norm_t, gpack_ref[:, 512:640]) + tail[:, :128]).astype(BF16)
        out[0, :, 640:] = tail[:, 128:].astype(BF16)


def input_back_kernel(info_ref, *refs):
    gpacks, weights = refs[:4], refs[4:8]
    tokens_ref, gmid_ref, gain_ref, three_ref, igrad_ref, small_ref, sum_ref = refs[8:]
    sum_ref[...] = dot(gpacks[0][...], weights[0][:HEAD_COLS, :])
    for gpack_ref, w_ref in zip(gpacks[1:], weights[1:]):
        sum_ref[...] += dot(gpack_ref[...], w_ref[:HEAD_COLS, :])
    small = 0.0
    for micro in range(2):
        rows = slice(micro * BLOCK, (micro + 1) * BLOCK)
        unit, inverse = unit_rows(pad_rows(tokens_ref[micro].astype(F32)))
        own = sum_ref[rows, :]
        small += jnp.sum(own * unit, axis=0, keepdims=True)
        back_rows = gmid_ref[rows, :] + norm_back(own, gain_ref[...], unit, inverse)
        igrad_ref[micro] = drop_rows(back_rows).astype(BF16)
    small_ref[...] = jnp.concatenate([three_ref[...], small], axis=0)


def assemble_kernel(info_ref, *refs):
    own_ref, one_ref, two_ref = refs[:3]
    out_ref = refs[-1]
    place = info_ref[5]
    out_ref[place] = own_ref[...]
    out_ref[place ^ 1] = one_ref[...]
    out_ref[place ^ 2] = two_ref[...]
    if len(refs) == 5:
        out_ref[place ^ 3] = refs[3][...]
    else:
        half = out_ref.shape[1] // 2
        out_ref[place ^ 3, :half] = refs[3][...]
        out_ref[place ^ 3, half:] = refs[4][...]


def add(left, right):
    return (left.astype(F32) + right.astype(F32)).astype(BF16)


THIRDS = (slice(0, 256), slice(256, 512), slice(512, 768))


def sum_refs(refs):
    total = refs[0][...]
    for ref in refs[1:]:
        total = total + ref[...]
    return total


def halve_first(sources, count, info_ref, gives, keeps, base):
    x, z = info_ref[6], info_ref[7]
    give_y, give_x, give_z = gives
    keep_a, keep_b, keep_c = keeps

    def pair(low, third, i, high, s):
        return add(sources(low, third, i, high, s), sources(low + 1, third, i, high, s))

    for i in range(count):
        for s in range(8):
            give_y[base + 8 * i + s] = pair(2, 0, i, s // 4, s % 4)
            keep_a[8 * i + s] = pair(0, 0, i, s // 4, s % 4)
        for side in range(2):
            for s in range(4):
                at = 8 * i + 4 * side + s
                low = 2 * (s % 2)
                keep_b[at] = pair(2 * side, 1, i, s // 2, low + x)
                give_x[base + at] = pair(2 * side, 1, i, s // 2, low + 1 - x)
                low = s % 2
                keep_c[at] = pair(2 * side, 2, i, s // 2, low + 2 * z)
                give_z[base + at] = pair(2 * side, 2, i, s // 2, low + 2 * (1 - z))


def halve_second(olds, gots, count, info_ref, gives, keeps):
    x, z = info_ref[6], info_ref[7]
    give_x, give_z, give_y = gives
    keep_a, keep_b, keep_c = keeps
    old_a, old_b, old_c = olds
    got_a, got_b, got_c = gots
    for i in range(count):
        for s in range(4):
            at, low = 4 * i + s, 8 * i + 2 * s
            keep_a[at] = add(old_a[low + x], got_a[low + x])
            give_x[at] = add(old_a[low + 1 - x], got_a[low + 1 - x])
            keep_c[at] = add(old_c[8 * i + s], got_c[8 * i + s])
            give_y[at] = add(old_c[8 * i + 4 + s], got_c[8 * i + 4 + s])
        for side in range(2):
            for s in range(2):
                at, low = 4 * i + 2 * side + s, 8 * i + 4 * side + 2 * s
                keep_b[at] = add(old_b[low + z], got_b[low + z])
                give_z[at] = add(old_b[low + 1 - z], got_b[low + 1 - z])


def halve_third(olds, gots, skip, count, info_ref, gives, keeps):
    x, z = info_ref[6], info_ref[7]
    give_z, give_y, give_x = gives
    keep_a, keep_b, keep_c = keeps
    old_a, old_b, old_c = olds
    got_a, got_b, got_c = gots
    for i in range(count):
        for s in range(2):
            at, low = 2 * i + s, 4 * i + 2 * s
            keep_a[at] = add(old_a[low + z], got_a[skip + low + z])
            give_z[at] = add(old_a[low + 1 - z], got_a[skip + low + 1 - z])
            low = 4 * i + s
            keep_b[at] = add(old_b[low], got_b[skip + low])
            give_y[at] = add(old_b[low + 2], got_b[skip + low + 2])
            low = 4 * i + 2 * s
            keep_c[at] = add(old_c[low + x], got_c[skip + low + x])
            give_x[at] = add(old_c[low + 1 - x], got_c[skip + low + 1 - x])


def halve_fourth(olds, gots, count, info_ref, give, keep):
    z = info_ref[8]
    for i in range(count):
        for old, got, third in zip(olds, gots, THIRDS):
            keep[i, :, third] = add(old[2 * i + z], got[2 * i + z])
            give[i, :, third] = add(old[2 * i + 1 - z], got[2 * i + 1 - z])


class Shifted:
    def __init__(self, ref, offset):
        self.ref = ref
        self.offset = offset

    def __getitem__(self, at):
        return self.ref[self.offset + at]

    def __setitem__(self, at, value):
        self.ref[self.offset + at] = value


def shift(refs, offset):
    return tuple(Shifted(ref, offset) for ref in refs)


def add_kernel(info_ref, left, right, out_ref):
    out_ref[...] = left[...] + right[...]


def merge_zero_kernel(info_ref, *refs):
    parts, gives, keeps = refs[:4], refs[4:7], refs[7:10]

    def source(part, third, i, high, s):
        return parts[part][i, 4 * high + s, :, THIRDS[third]]

    halve_first(source, 2, info_ref, gives, keeps, 0)


def merge_one_kernel(info_ref, *refs):
    olds, gots, parts = refs[:3], refs[3:6], refs[6:14]
    give_y, give_x, give_z = refs[14:17]
    keeps_m, keeps_a = refs[17:20], refs[20:23]

    def source(part, third, i, high, s):
        return parts[2 * part + high][i, s, :, THIRDS[third]]

    halve_second(olds, gots, 2, info_ref, (give_x, give_z, give_y), keeps_m)
    halve_first(source, 1, info_ref, (give_y, give_x, give_z), keeps_a, 8)


def merge_two_kernel(info_ref, *refs):
    olds_m, olds_a = refs[:3], refs[3:6]
    got_y, got_x, got_z = refs[6:9]
    smalls = refs[9:11]
    give_y, give_x, give_z = refs[11:14]
    keeps_m, keeps_a, small_ref = refs[14:17], refs[17:20], refs[20]
    halve_third(
        olds_m, (got_x, got_z, got_y), 0, 2, info_ref, (give_z, give_y, give_x), keeps_m
    )
    halve_second(
        olds_a,
        shift((got_y, got_x, got_z), 8),
        1,
        info_ref,
        shift((give_x, give_z, give_y), 4),
        keeps_a,
    )
    small_ref[...] = sum_refs(smalls)


def merge_three_kernel(info_ref, *refs):
    olds_m, olds_a = refs[:3], refs[3:6]
    got_y, got_x, got_z = refs[6:9]
    smalls = refs[9:11]
    give_y, give_x, give_z, give_far = refs[11:15]
    keep_m, keeps_a, small_ref = refs[15], refs[16:19], refs[19]
    halve_fourth(olds_m, (got_z, got_y, got_x), 2, info_ref, give_far, keep_m)
    halve_third(
        olds_a, (got_x, got_z, got_y), 4, 1, info_ref, (give_z, give_y, give_x), keeps_a
    )
    small_ref[...] = sum_refs(smalls)


def merge_four_kernel(info_ref, *refs):
    old_m, olds_a = refs[0], refs[1:4]
    got_y, got_x, got_z, got_far = refs[4:8]
    give_far, keep_a, up_ref, down_ref, small_ref = refs[10:]
    halve_fourth(olds_a, (got_z, got_y, got_x), 1, info_ref, give_far, keep_a)
    small_ref[...] = sum_refs(refs[8:10])
    up_ref[...] = old_m[0].astype(F32) + got_far[0].astype(F32)
    down_ref[...] = old_m[1].astype(F32) + got_far[1].astype(F32)


def merge_last_kernel(info_ref, *refs):
    old, got, qkv_ref, proj_ref = refs[:2] + refs[4:6]
    small = sum_refs(refs[2:4])
    total = old[0].astype(F32) + got[0].astype(F32)
    split = qkv_ref.shape[1]
    qkv_ref[...] = total[:, :split]
    proj_ref[...] = total[:, 512:].T[split - 512 :]
    width = small.shape[1] // 8
    place = info_ref[5] + 4 * info_ref[8]
    for d in range(8):

        @pl.when(place == d)
        def _():
            for i, ref in enumerate(refs[6:]):
                ref[...] = small[i : i + 1, d * width : (d + 1) * width]


VMEM = pl.BlockSpec(memory_space=pltpu.VMEM)
HBM = pl.BlockSpec(memory_space=pltpu.HBM)
SMEM = pl.BlockSpec(memory_space=pltpu.SMEM)


def shape(dims, dtype):
    return jax.ShapeDtypeStruct(dims, dtype)


class Order:
    def __init__(self, info):
        self.info = info

    def call(self, kernel, args, outs, scratch=(), limit=16, spaces=None):
        specs = [SMEM] + [VMEM] * len(args)
        out_specs = [VMEM] * len(outs)
        if spaces is not None:
            specs[1:] = spaces[0]
            out_specs = spaces[1]
        out = pl.pallas_call(
            kernel,
            in_specs=specs,
            out_specs=out_specs,
            out_shape=outs,
            scratch_shapes=list(scratch),
            compiler_params=pltpu.CompilerParams(vmem_limit_bytes=limit * MIB),
            cost_estimate=pl.CostEstimate(flops=1000, bytes_accessed=1000, transcendentals=0),
        )(self.info, *args)
        self.info = after(self.info, out[0])
        return out


def swap(value, axis, bit):
    size = lax.axis_size(axis)
    return lax.ppermute(value, axis, [(i, i ^ bit) for i in range(size)])


def after(value, *others):
    return lax.optimization_barrier((value,) + others)[0]


def second_hop(own):
    return swap(own, "dp", 1), swap(own, "dp", 2)


def third_hop(one, two):
    half = one.shape[0] // 2
    return swap(two[:half], "dp", 1), swap(one[half:], "dp", 2)


def assemble(order, pieces):
    dims = (4,) + pieces[0].shape
    return order.call(assemble_kernel, tuple(pieces), (shape(dims, BF16),))[0]


def swap_y(value):
    return swap(value, "tensor", 2)


def swap_x(value):
    return swap(value, "dp", 1)


def swap_z(value):
    return swap(value, "dp", 2)


def swap_far(value):
    return swap(value, "dp", 4)


def dp_halve(value, bit):
    slices = value.shape[0]
    mine = (lax.axis_index("dp") // bit) % 2
    paired = value.reshape((slices // 2, 2) + value.shape[1:])
    keep = lax.dynamic_index_in_dim(paired, mine, 1, keepdims=False)
    give = lax.dynamic_index_in_dim(paired, 1 - mine, 1, keepdims=False)
    got = swap(give.astype(BF16), "dp", bit)
    return keep.astype(F32) + got.astype(F32)


def scatter_sum(parts, first_dp):
    shards = lax.axis_size("dp")
    zero = parts[0].astype(F32) + swap(parts[1], "tensor", 1).astype(F32)
    two = parts[2].astype(F32) + swap(parts[3], "tensor", 1).astype(F32)
    form = (shards, D // shards, parts[0].shape[1])
    zero = zero.reshape(form)
    two = two.reshape(form)
    bit = 1
    if first_dp:
        zero = dp_halve(zero, bit)
        two = dp_halve(two, bit)
        bit = 2
    zero = zero + swap(two.astype(BF16), "tensor", 2).astype(F32)
    while bit < shards:
        zero = dp_halve(zero, bit)
        bit = bit * 2
    return zero[0]


def body(
    tokens,
    out_grad,
    global_count,
    local_count,
    attn_gain,
    qkv_weight,
    proj_weight,
    attn_scale,
    mlp_gain,
    up_weight,
    down_weight,
    mlp_scale,
):
    groups = lax.axis_size("tensor")
    shards = lax.axis_size("dp")
    rows = 2 * BLOCK
    place = lax.axis_index("dp").astype(jnp.int32)
    member = lax.axis_index("tensor").astype(jnp.int32)
    where = jnp.stack([place % 4, place % 2, (place // 2) % 2, (place // 4) % 2])
    info = jnp.concatenate([member[None], global_count[0], local_count[0], where])
    row = lambda vector: vector.reshape(1, D)

    act = shape((rows, D), BF16)
    act_t = shape((D, rows), BF16)
    acc = shape((rows, D), F32)
    packed = shape((rows, HEAD_COLS), BF16)
    ctx = shape((rows, 256), BF16)
    unit_flops = 2 * rows * D * D

    def bind(kernel, *flags):
        def run(*refs):
            return kernel(groups, *flags, *refs)

        return run

    mixed, block_a, block_b = pl.pallas_call(
        start_kernel,
        in_specs=[HBM] * 4,
        out_specs=[VMEM] * 3,
        out_shape=(shape((D, D), BF16), shape((D // 4, D), BF16), shape((D // 2, D), BF16)),
        scratch_shapes=[pltpu.SemaphoreType.DMA((5,))],
        compiler_params=pltpu.CompilerParams(vmem_limit_bytes=60 * MIB),
    )(qkv_weight.T, proj_weight, up_weight, down_weight)
    order = Order(after(info, block_a))
    own_a = swap(block_a, "tensor", 2)
    wa = [mixed, swap(mixed, "tensor", 1)]
    up_one = swap(after(up_weight, block_a), "tensor", 1)
    down_one = swap(after(down_weight, block_a), "tensor", 1)
    norm, norm_t, gmlp, gmlp_t = order.call(
        bind(prepare_kernel),
        (tokens, out_grad, row(attn_gain), row(mlp_scale)),
        (act, act_t, act, act_t),
    )
    packs, ctxs = {}, {}

    def attend(r, part):
        last = r == 3
        args = (norm, wa[r]) + part
        outs = (packed, ctx, acc)
        spaces, scratch = None, []
        if last:
            spaces = ([VMEM] * (len(args) + 3) + [HBM] * 2, [VMEM] * 8)
            args += (tokens, row(attn_scale), row(mlp_gain), up_weight, down_weight)
            outs += (acc, act, act_t, shape((D, D), BF16), shape((D, D), BF16))
            scratch = [pltpu.SemaphoreType.DMA((2,))]
        got = order.call(bind(attend_kernel, r == 0, last), args, outs, scratch=scratch, spaces=spaces)
        packs[r], ctxs[r] = got[:2]
        return tuple(got[2:])

    half_rows = D // 2
    part = attend(0, ())
    own_a = after(own_a, part[0])
    one_a, two_a = second_hop(own_a)
    own_b = swap(after(block_b, own_a), "tensor", 2)
    wa[1], up_one, down_one = after((wa[1], up_one, down_one), own_a)
    part = attend(1, after(part, up_one, down_one))
    one_a, two_a = after((one_a, two_a), part[0])
    own_a = after(own_a, own_b)
    wa.append(assemble(order, (own_a, one_a, two_a) + third_hop(one_a, two_a)).reshape(D, D))
    wa.append(swap(wa[2], "tensor", 1))
    own_b = after(own_b, wa[2])
    one_b, two_b = second_hop(own_b)
    part = attend(2, part)
    attn_out, middle, norm_two, norm_two_t, up_zero, down_zero = attend(3, part)

    def mlp(weights, carried, extra, outs, first, last):
        return order.call(
            bind(mlp_kernel, first, last, len(weights) == 1),
            (norm_two, norm_two_t, gmlp, gmlp_t) + weights + carried + extra,
            (shape((2, D, D), BF16),) + tuple(outs),
            scratch=[pltpu.VMEM((rows, D), F32)] * 2 if last else [],
            limit=16,
        )

    wgrads = {}
    wgrads[0], mlp_sum, grad_sum = mlp((up_zero, down_zero), (), (), (acc, acc), True, False)
    one_b, two_b = after((one_b, two_b), mlp_sum)
    three_b = third_hop(one_b, two_b)
    wgrads[1], mlp_sum, grad_sum = mlp((up_one, down_one), (mlp_sum, grad_sum), (), (acc, acc), False, False)
    both_two = assemble(order, (own_b, one_b, two_b) + three_b)
    both_three = swap(both_two, "tensor", 1)
    got_one = swap(after(wgrads[1], both_two), "tensor", 1)
    wgrads[2], mlp_sum, grad_sum = mlp((both_two,), (mlp_sum, grad_sum), (), (acc, acc), False, False)
    extra = (middle, attn_out, out_grad, row(mlp_gain), row(mlp_scale), row(attn_scale))
    outs = (shape(tokens.shape, BF16), acc, act, act_t, shape((3, D), F32))
    wgrads[3], block_out, grad_mid, gattn, gattn_t, small = mlp(
        (both_three,), (mlp_sum, grad_sum), extra, outs, False, True
    )
    got_three = swap(wgrads[3], "tensor", 1)

    agrads, gpacks = {}, {}
    half = shape((1, D // 2, D), BF16)

    def back(r):
        out = order.call(
            bind(attend_back_kernel),
            (wa[r], packs[r], ctxs[r], gattn, gattn_t, norm_t),
            (packed, half, half),
            scratch=[pltpu.VMEM((rows, 256), BF16)],
        )
        gpacks[r] = out[0]
        agrads[r] = tuple(out[1:])

    def input_back():
        return order.call(
            input_back_kernel,
            tuple(gpacks[r] for r in range(4)) + tuple(wa) + (tokens, grad_mid, row(attn_gain), small),
            (shape(tokens.shape, BF16), shape((4, D), F32)),
            scratch=[pltpu.VMEM((rows, D), F32)],
        )

    width = D // shards
    split = qkv_weight.shape[1]
    back(1)
    if shards == 8:
        view = lambda a: a.reshape((a.shape[0], a.shape[1] // width, width, D))
        swap_core = lambda values: tuple(swap(value, "tensor", 1) for value in values)
        tiny = shape((4, D), F32)
        blocks = lambda count: shape((count, width, 256), BF16)
        whole = lambda count: shape((count, width, D), BF16)
        args = tuple(view(a) for a in (wgrads[0], got_one, wgrads[2], got_three))
        out = order.call(merge_zero_kernel, args, (blocks(16),) * 6)
        keeps_m = tuple(out[3:6])
        got_m = (swap_y(out[0]), swap_x(out[1]), swap_z(out[2]))
        got_one = swap_core(after(agrads[1], keeps_m[0]))
        back(3)
        got_three = swap_core(agrads[3])
        back(0)
        back(2)
        args = tuple(view(a) for a in agrads[0] + got_one + agrads[2] + got_three)
        out = order.call(
            merge_one_kernel, keeps_m + got_m + args, (blocks(16),) * 3 + (blocks(8),) * 6
        )
        keeps = tuple(out[3:9])
        got = (swap_y(out[0]), swap_x(out[1]), swap_z(out[2]))
        input_grad, small = input_back()
        small = order.call(add_kernel, (small, swap(small, "tensor", 1)), (tiny,))[0]
        smalls = (small, swap_y(small))
        out = order.call(
            merge_two_kernel, keeps + got + smalls, (blocks(8),) * 3 + (blocks(4),) * 6 + (tiny,)
        )
        keeps = tuple(out[3:9])
        got = (swap_y(out[0]), swap_x(out[1]), swap_z(out[2]))
        smalls = (out[9], swap_x(out[9]))
        out = order.call(
            merge_three_kernel,
            keeps + got + smalls,
            (blocks(2),) * 3 + (whole(2), whole(2)) + (blocks(2),) * 3 + (tiny,),
        )
        keeps = tuple(out[4:8])
        got = (swap_y(out[0]), swap_x(out[1]), swap_z(out[2]), swap_far(out[3]))
        smalls = (out[8], swap_z(out[8]))
        give, keep, up_grad, down_grad, small = order.call(
            merge_four_kernel,
            keeps + got + smalls,
            (whole(1), whole(1), shape((width, D), F32), shape((width, D), F32), tiny),
        )
        down_grad = down_grad.T
        out = order.call(
            merge_last_kernel,
            (keep, swap_far(give), small, swap_far(small)),
            (shape((width, split), F32), shape((D - split, width), F32)) + (shape((1, width), F32),) * 4,
        )
        smalls = [value.reshape(width) for value in out[2:]]
        qkv_grad, proj_grad = out[:2]
    else:
        for r in (3, 0, 2):
            back(r)
        input_grad, small = input_back()
        up_grad = scatter_sum([wgrads[r][0] for r in range(4)], False)
        down_grad = scatter_sum([wgrads[r][1] for r in range(4)], True).T
        mixed_grad = scatter_sum([jnp.concatenate(agrads[r], axis=1)[0] for r in range(4)], False)
        qkv_grad = mixed_grad[:, :split]
        proj_grad = mixed_grad[:, split:].T
        small = lax.psum(small, ("dp", "tensor"))
        small = lax.dynamic_slice_in_dim(small, place * width, width, axis=1)
        smalls = [small[i] for i in range(4)]
    return (
        block_out,
        input_grad,
        smalls[3],
        qkv_grad,
        proj_grad,
        smalls[2],
        smalls[1],
        up_grad,
        down_grad,
        smalls[0],
    )


def solution(mesh):
    in_specs = (
        P(None, ("dp", "tensor"), None),
        P(None, ("dp", "tensor"), None),
        P("dp", None),
        P("dp", None),
        P(),
        P(None, "tensor"),
        P("tensor", None),
        P(),
        P(),
        P(None, "tensor"),
        P("tensor", None),
        P(),
    )
    out_specs = (
        P(None, ("dp", "tensor"), None),
        P(None, ("dp", "tensor"), None),
        P("dp"),
        P("dp", "tensor"),
        P("tensor", "dp"),
        P("dp"),
        P("dp"),
        P("dp", "tensor"),
        P("tensor", "dp"),
        P("dp"),
    )
    return jax.shard_map(body, mesh=mesh, in_specs=in_specs, out_specs=out_specs, check_vma=False)
```

```python
import math

import jax
import jax.numpy as jnp
from jax import lax
from jax.experimental import pallas as pl
from jax.experimental.pallas import tpu as pltpu
from jax.sharding import PartitionSpec as P

D = 768
HD = 64
GLEN = 197
GPAD = 200
LLEN = 37
LPAD = 40
SLOT = GPAD + 2 * LPAD
GROW = 208
LROW = 2 * LPAD
BLOCK = GROW + LROW
FACTOR = HD ** (-0.5)
HEAD_COLS = 640
F32 = jnp.float32
BF16 = jnp.bfloat16
NN = (((1,), (0,)), ((), ()))
NT = (((1,), (1,)), ((), ()))
TN = (((0,), (0,)), ((), ()))
MIB = 1024 * 1024


def dot(left, right, dims=NN):
    return lax.dot_general(left, right, dims, preferred_element_type=F32)


def pad_rows(values):
    return jnp.concatenate(
        [values[:GPAD], jnp.zeros((GROW - GPAD, values.shape[1]), values.dtype), values[GPAD:]], axis=0
    )


def drop_rows(values):
    return jnp.concatenate([values[:GPAD], values[GROW:]], axis=0)


def row_keep(info_ref, micro, groups):
    member = info_ref[0]
    row = lax.broadcasted_iota(jnp.int32, (BLOCK, 1), 0)
    live = jnp.where(member < info_ref[1 + micro], GLEN, 0)
    first = jnp.where(member < info_ref[3 + micro], LLEN, 0)
    second = jnp.where(member + groups < info_ref[3 + micro], LLEN, 0)
    keep = (
        (row < live)
        | ((row >= GROW) & (row < GROW + first))
        | ((row >= GROW + LPAD) & (row < GROW + LPAD + second))
    )
    return jnp.where(keep, 1.0, 0.0).astype(F32)


def global_mask(info_ref, micro, axis):
    shape = (1, GROW) if axis == 1 else (GROW, 1)
    key = lax.broadcasted_iota(jnp.int32, shape, axis)
    live = jnp.where(info_ref[0] < info_ref[1 + micro], GLEN, 0)
    fill = jnp.where(key < GPAD, -30000.0, -3e38).astype(F32)
    return key < live, fill


def local_mask(info_ref, micro, groups, axis):
    key = lax.broadcasted_iota(jnp.int32, (LROW, LROW), axis)
    query = lax.broadcasted_iota(jnp.int32, (LROW, LROW), 1 - axis)
    member = info_ref[0]
    first = jnp.where(member < info_ref[3 + micro], LLEN, 0)
    second = jnp.where(member + groups < info_ref[3 + micro], LLEN, 0)
    same = (key < LPAD) == (query < LPAD)
    alive = (key < first) | ((key >= LPAD) & (key < LPAD + second))
    fill = jnp.where(same, -30000.0, -3e38).astype(F32)
    return same & alive, fill


def slots(info_ref, groups, axis):
    places = []
    for micro in range(2):
        start = micro * BLOCK
        places.append((slice(start, start + GROW),) + global_mask(info_ref, micro, axis))
        places.append((slice(start + GROW, start + BLOCK),) + local_mask(info_ref, micro, groups, axis))
    return places


def unit_rows(values):
    center = values - jnp.mean(values, axis=-1, keepdims=True)
    inverse = lax.rsqrt(jnp.mean(center * center, axis=-1, keepdims=True) + 1e-06)
    return center * inverse, inverse


def norm_back(grad_norm, gain, unit, inverse):
    scaled = grad_norm * gain
    centered = scaled - jnp.mean(scaled, axis=-1, keepdims=True)
    return inverse * (centered - unit * jnp.mean(scaled * unit, axis=-1, keepdims=True))


def low_half(tile):
    lane = lax.broadcasted_iota(jnp.int32, tile.shape, 1)
    return jnp.where(lane < HD, tile, jnp.zeros_like(tile))


def high_half(tile):
    lane = lax.broadcasted_iota(jnp.int32, tile.shape, 1)
    return jnp.where(lane < HD, jnp.zeros_like(tile), tile)


def turn(tile):
    return pltpu.roll(tile.astype(F32), HD, 1).astype(tile.dtype)


def softmax_rows(scores, live, fill):
    scores = jnp.where(live, scores, fill)
    raised = jnp.exp(scores - jnp.max(scores, axis=1, keepdims=True))
    return (raised * (1.0 / jnp.sum(raised, axis=1, keepdims=True))).astype(BF16)


def softmax_columns(scores, live, fill):
    scores = jnp.where(live, scores, fill)
    raised = jnp.exp(scores - jnp.max(scores, axis=0, keepdims=True))
    return raised * (1.0 / jnp.sum(raised, axis=0, keepdims=True))


def start_kernel(qkv_hbm, proj_hbm, up_hbm, down_hbm, mixed_ref, block_ref, block_b, sems):
    place = lax.rem(lax.axis_index("dp"), 4)
    quarter = D // 4
    half = D // 2
    blocks = [qkv_hbm.at[pl.ds(i * quarter, quarter)] for i in range(3)] + [proj_hbm]
    for i, block in enumerate(blocks):
        pltpu.make_async_copy(block, mixed_ref.at[pl.ds(i * quarter, quarter)], sems.at[i]).start()
    chosen = pl.ds(pl.multiple_of(lax.rem(place, 2) * half, half), half)

    @pl.when(place < 2)
    def _():
        pltpu.make_async_copy(up_hbm.at[chosen], block_b, sems.at[4]).start()

    @pl.when(place >= 2)
    def _():
        pltpu.make_async_copy(down_hbm.at[chosen], block_b, sems.at[4]).start()

    for i, block in enumerate(blocks):
        pltpu.make_async_copy(block, mixed_ref.at[pl.ds(i * quarter, quarter)], sems.at[i]).wait()
    block_ref[...] = mixed_ref[pl.ds(pl.multiple_of(place * quarter, quarter), quarter), :]
    pltpu.make_async_copy(up_hbm.at[chosen], block_b, sems.at[4]).wait()


def prepare_kernel(
    groups, info_ref, tokens_ref, grad_ref, gain_ref, scale_ref, norm_ref, gmlp_ref
):
    for micro in range(2):
        rows = slice(micro * BLOCK, (micro + 1) * BLOCK)
        values = pad_rows(tokens_ref[micro].astype(F32))
        unit, _ = unit_rows(values)
        norm_ref[rows, :] = (unit * gain_ref[...]).astype(BF16)
        keep = row_keep(info_ref, micro, groups)
        grad = pad_rows(grad_ref[micro].astype(F32))
        gmlp_ref[rows, :] = (keep * scale_ref[...] * grad).astype(BF16)


def attend_kernel(groups, first, last, *refs):
    info_ref, norm_ref = refs[:2]
    at = 2
    pieced = not first and refs[at].shape[0] < D
    if pieced:
        pieces = refs[at : at + 5]
        at += 5
    else:
        w_ref = refs[at]
        at += 1
    if not first:
        acc_ref = refs[at]
        at += 1
    if last:
        tokens_ref, scale_ref, gain_ref = refs[at : at + 3]
        at += 3
    packed_ref, ctx_ref, out_ref = refs[at : at + 3]
    at += 3
    if pieced:
        put_together(info_ref, pieces, refs[at])
        weights = refs[at][...].reshape(D, D)
        at += 1
    else:
        weights = w_ref[...]
    if last:
        middle_ref, norm_two_ref = refs[at : at + 2]
    packed_ref[...] = dot(norm_ref[...], weights[:HEAD_COLS, :], NT).astype(BF16)
    jobs = []
    for rows, live, fill in slots(info_ref, groups, 1):
        t0, t1, t2, t3, t4 = (packed_ref[rows, 128 * i : 128 * i + 128] for i in range(5))
        queries = (low_half(t0 * FACTOR), high_half(t1 * FACTOR), low_half(t3 * FACTOR))
        t2r = turn(t2)
        keys = (turn(t0), t2r, turn(t3))
        scores = [dot(query, key, NT) for query, key in zip(queries, keys)]
        jobs.append((rows, live, fill, scores, (high_half(turn(t1)), low_half(t2r), high_half(turn(t4)))))
    done = []
    for rows, live, fill, scores, values in jobs:
        done.append((rows, [softmax_rows(score, live, fill) for score in scores], values))
    for rows, probs, values in done:
        ctx_ref[rows, :128] = dot(probs[0], values[0]).astype(BF16)
        ctx_ref[rows, 128:] = (dot(probs[1], values[1]) + dot(probs[2], values[2])).astype(BF16)
    out = dot(ctx_ref[...], weights[512:, :])
    if not first:
        out = out + acc_ref[...]
    out_ref[...] = out
    if last:
        for micro in range(2):
            rows = slice(micro * BLOCK, (micro + 1) * BLOCK)
            keep = row_keep(info_ref, micro, groups)
            middle = pad_rows(tokens_ref[micro].astype(F32)) + keep * scale_ref[...] * out_ref[rows, :]
            middle_ref[rows, :] = middle
            unit, _ = unit_rows(middle)
            norm_two_ref[rows, :] = (unit * gain_ref[...]).astype(BF16)


def put_together(info_ref, pieces, out_ref):
    place = info_ref[5]
    half = out_ref.shape[1] // 2
    out_ref[place] = pieces[0][...]
    out_ref[place ^ 1] = pieces[1][...]
    out_ref[place ^ 2] = pieces[2][...]
    out_ref[place ^ 3, :half] = pieces[3][...]
    out_ref[place ^ 3, half:] = pieces[4][...]


def assemble_kernel(info_ref, *refs):
    put_together(info_ref, refs[:5], refs[5])


def early_kernel(info_ref, *refs):
    gmlp_ref, down_one_ref, up_hbm, down_hbm, up_ref, down_ref, out_zero, out_one, sems = refs
    fetches = (
        pltpu.make_async_copy(down_hbm, down_ref, sems.at[0]),
        pltpu.make_async_copy(up_hbm, up_ref, sems.at[1]),
    )
    fetches[0].start()
    out_one[...] = dot(gmlp_ref[...], down_one_ref[...], NT)
    fetches[0].wait()
    fetches[1].start()
    out_zero[...] = dot(gmlp_ref[...], down_ref[...], NT)
    fetches[1].wait()


def mlp_kernel(groups, first, last, joined, *refs):
    info_ref, norm_ref, gmlp_ref = refs[:3]
    at = 3
    if joined:
        both_ref = refs[at]
        at += 1
    else:
        up_ref, down_ref = refs[at : at + 2]
        at += 2
    if not joined:
        early_ref = refs[at]
        at += 1
    if not first:
        mlp_in, grad_in = refs[at : at + 2]
        at += 2
    if last:
        middle_ref, attn_ref, og_ref, gain_ref, mscale_ref, ascale_ref = refs[at : at + 6]
        at += 6
    wgrad_ref = refs[at]
    at += 1
    if not last:
        mlp_ref, grad_ref = refs[at : at + 2]
    else:
        block_ref, gmid_ref, gattn_ref, small_ref, mlp_ref, grad_ref = refs[at : at + 6]
    width = 768
    for c in range(D // width):
        cols = slice(c * width, (c + 1) * width)
        if joined:
            up = both_ref[:2, :, cols].reshape(D, width)
            half = D // 2
            pieces = []
            for h in range(2):
                low = max(c * width, h * half)
                high = min((c + 1) * width, (h + 1) * half)
                if low < high:
                    pieces.append(both_ref[2 + h, low - h * half : high - h * half, :])
            down = pieces[0] if len(pieces) == 1 else jnp.concatenate(pieces, axis=0)
        else:
            up = up_ref[:, cols]
            down = down_ref[cols, :]
        hidden = dot(norm_ref[...], up)
        grad_active = dot(gmlp_ref[...], down, NT) if joined else early_ref[...]
        cdf = 0.5 + 0.5 * lax.erf(hidden * (0.5**0.5))
        active = (hidden * cdf).astype(BF16)
        slope = cdf + hidden * (jnp.exp(-0.5 * hidden * hidden) * (1.0 / math.sqrt(2.0 * math.pi)))
        grad_hidden = (grad_active * slope).astype(BF16)
        mlp = dot(active, down)
        grad = dot(grad_hidden, up, NT)
        if c > 0:
            mlp_ref[...] += mlp
            grad_ref[...] += grad
        elif first:
            mlp_ref[...] = mlp
            grad_ref[...] = grad
        else:
            mlp_ref[...] = mlp_in[...] + mlp
            grad_ref[...] = grad_in[...] + grad
        wgrad_ref[0, :, cols] = dot(norm_ref[...], grad_hidden, TN).astype(BF16)
        wgrad_ref[1, :, cols] = dot(gmlp_ref[...], active, TN).astype(BF16)
    if last:
        small = [0.0, 0.0, 0.0]
        for micro in range(2):
            rows = slice(micro * BLOCK, (micro + 1) * BLOCK)
            keep = row_keep(info_ref, micro, groups)
            middle = middle_ref[rows, :]
            mlp = mlp_ref[rows, :]
            grad_out = pad_rows(og_ref[micro].astype(F32))
            block = middle + keep * mscale_ref[...] * mlp
            block_ref[micro] = drop_rows(block).astype(BF16)
            small[0] += jnp.sum(keep * mlp * grad_out, axis=0, keepdims=True)
            unit, inverse = unit_rows(middle)
            grad_two = grad_ref[rows, :]
            small[1] += jnp.sum(grad_two * unit, axis=0, keepdims=True)
            grad_mid = grad_out + norm_back(grad_two, gain_ref[...], unit, inverse)
            gmid_ref[rows, :] = grad_mid
            small[2] += jnp.sum(keep * attn_ref[rows, :] * grad_mid, axis=0, keepdims=True)
            gattn_ref[rows, :] = (keep * ascale_ref[...] * grad_mid).astype(BF16)
        small_ref[...] = jnp.concatenate(small, axis=0)


def attend_back_kernel(groups, *refs):
    info_ref, w_ref, packed_ref, ctx_ref, gattn_ref, norm_ref = refs[:6]
    gpack_ref, low_ref, high_ref, gctx_ref = refs[6:]
    gctx_ref[...] = dot(gattn_ref[...], w_ref[512:, :], NT).astype(BF16)
    places = slots(info_ref, groups, 0)
    for pair in (places[:2], places[2:]):
        jobs = []
        for rows, live, fill in pair:
            t0, t1, t2, t3, t4 = (packed_ref[rows, 128 * i : 128 * i + 128] for i in range(5))
            g0, g1 = gctx_ref[rows, :128], gctx_ref[rows, 128:]
            t1r = turn(t1)
            t0s, t2s, t3s = turn(t0 * FACTOR), t2 * FACTOR, turn(t3 * FACTOR)
            keys = (low_half(t0s), low_half(t2s), low_half(t3s))
            values = (high_half(t1r), low_half(turn(t2)), high_half(turn(t4)))
            scores = [dot(key, query, NT) for key, query in zip(keys, (t0, t1r, t3))]
            gps = [dot(value, grad, NT) for value, grad in zip(values, (g0, g1, g1))]
            tiles = (t0s, low_half(t1r * FACTOR), high_half(turn(t2s)), t3s, turn(g0), turn(g1))
            jobs.append((rows, live, fill, scores, gps, tiles))
        done = []
        for rows, live, fill, scores, gps, tiles in jobs:
            probs = [softmax_columns(score, live, fill) for score in scores]
            dots = [jnp.sum(prob * gp, axis=0, keepdims=True) for prob, gp in zip(probs, gps)]
            gs = [(prob * (gp - row)).astype(BF16) for prob, gp, row in zip(probs, gps, dots)]
            done.append((rows, [prob.astype(BF16) for prob in probs], gs, tiles))
        for rows, probs, gs, (t0s, query_b, key_b, t3s, g0r, g1r) in done:
            columns = (
                dot(gs[0], low_half(t0s), TN) + dot(gs[0], high_half(t0s)),
                dot(probs[0], low_half(g0r)) + dot(gs[1], key_b, TN),
                dot(gs[1], query_b) + dot(probs[1], high_half(g1r)),
                dot(gs[2], low_half(t3s), TN) + dot(gs[2], high_half(t3s)),
                dot(probs[2], low_half(g1r)),
            )
            for i, column in enumerate(columns):
                gpack_ref[rows, 128 * i : 128 * i + 128] = column.astype(BF16)
    half = D // 2
    for top, out in enumerate((low_ref, high_ref)):
        columns = slice(top * half, (top + 1) * half)
        norm = norm_ref[:, columns]
        out[0, :, :512] = dot(norm, gpack_ref[:, :512], TN).astype(BF16)
        tail = dot(gattn_ref[:, columns], ctx_ref[...], TN)
        out[0, :, 512:640] = (dot(norm, gpack_ref[:, 512:640], TN) + tail[:, :128]).astype(BF16)
        out[0, :, 640:] = tail[:, 128:].astype(BF16)


def input_back_kernel(info_ref, *refs):
    gpacks, weights = refs[:4], refs[4:8]
    tokens_ref, gmid_ref, gain_ref, three_ref, igrad_ref, small_ref, sum_ref = refs[8:]
    sum_ref[...] = dot(gpacks[0][...], weights[0][:HEAD_COLS, :])
    for gpack_ref, w_ref in zip(gpacks[1:], weights[1:]):
        sum_ref[...] += dot(gpack_ref[...], w_ref[:HEAD_COLS, :])
    small = 0.0
    for micro in range(2):
        rows = slice(micro * BLOCK, (micro + 1) * BLOCK)
        unit, inverse = unit_rows(pad_rows(tokens_ref[micro].astype(F32)))
        own = sum_ref[rows, :]
        small += jnp.sum(own * unit, axis=0, keepdims=True)
        back_rows = gmid_ref[rows, :] + norm_back(own, gain_ref[...], unit, inverse)
        igrad_ref[micro] = drop_rows(back_rows).astype(BF16)
    small_ref[...] = jnp.concatenate([three_ref[...], small], axis=0)


def add(left, right):
    return left + right


THIRDS = (slice(0, 256), slice(256, 512), slice(512, 768))


def sum_refs(refs):
    total = refs[0][...]
    for ref in refs[1:]:
        total = total + ref[...]
    return total


def halve_first(sources, count, info_ref, gives, keeps, base):
    x, z = info_ref[6], info_ref[7]
    give_y, give_x, give_z = gives
    keep_a, keep_b, keep_c = keeps

    def pair(low, third, i, high, s):
        return add(sources(low, third, i, high, s), sources(low + 1, third, i, high, s))

    for i in range(count):
        for s in range(8):
            give_y[base + 8 * i + s] = pair(2, 0, i, s // 4, s % 4)
            keep_a[8 * i + s] = pair(0, 0, i, s // 4, s % 4)
        for side in range(2):
            for s in range(4):
                at = 8 * i + 4 * side + s
                low = 2 * (s % 2)
                keep_b[at] = pair(2 * side, 1, i, s // 2, low + x)
                give_x[base + at] = pair(2 * side, 1, i, s // 2, low + 1 - x)
                low = s % 2
                keep_c[at] = pair(2 * side, 2, i, s // 2, low + 2 * z)
                give_z[base + at] = pair(2 * side, 2, i, s // 2, low + 2 * (1 - z))


def halve_second(olds, gots, count, info_ref, gives, keeps):
    x, z = info_ref[6], info_ref[7]
    give_x, give_z, give_y = gives
    keep_a, keep_b, keep_c = keeps
    old_a, old_b, old_c = olds
    got_a, got_b, got_c = gots
    for i in range(count):
        for s in range(4):
            at, low = 4 * i + s, 8 * i + 2 * s
            keep_a[at] = add(old_a[low + x], got_a[low + x])
            give_x[at] = add(old_a[low + 1 - x], got_a[low + 1 - x])
            keep_c[at] = add(old_c[8 * i + s], got_c[8 * i + s])
            give_y[at] = add(old_c[8 * i + 4 + s], got_c[8 * i + 4 + s])
        for side in range(2):
            for s in range(2):
                at, low = 4 * i + 2 * side + s, 8 * i + 4 * side + 2 * s
                keep_b[at] = add(old_b[low + z], got_b[low + z])
                give_z[at] = add(old_b[low + 1 - z], got_b[low + 1 - z])


def halve_third(olds, gots, skip, count, info_ref, gives, keeps):
    x, z = info_ref[6], info_ref[7]
    give_z, give_y, give_x = gives
    keep_a, keep_b, keep_c = keeps
    old_a, old_b, old_c = olds
    got_a, got_b, got_c = gots
    for i in range(count):
        for s in range(2):
            at, low = 2 * i + s, 4 * i + 2 * s
            keep_a[at] = add(old_a[low + z], got_a[skip + low + z])
            give_z[at] = add(old_a[low + 1 - z], got_a[skip + low + 1 - z])
            low = 4 * i + s
            keep_b[at] = add(old_b[low], got_b[skip + low])
            give_y[at] = add(old_b[low + 2], got_b[skip + low + 2])
            low = 4 * i + 2 * s
            keep_c[at] = add(old_c[low + x], got_c[skip + low + x])
            give_x[at] = add(old_c[low + 1 - x], got_c[skip + low + 1 - x])


def halve_fourth(olds, gots, count, info_ref, give, keep):
    z = info_ref[8]
    for i in range(count):
        for old, got, third in zip(olds, gots, THIRDS):
            keep[i, :, third] = add(old[2 * i + z], got[2 * i + z])
            give[i, :, third] = add(old[2 * i + 1 - z], got[2 * i + 1 - z])


class Shifted:
    def __init__(self, ref, offset):
        self.ref = ref
        self.offset = offset

    def __getitem__(self, at):
        return self.ref[self.offset + at]

    def __setitem__(self, at, value):
        self.ref[self.offset + at] = value


def shift(refs, offset):
    return tuple(Shifted(ref, offset) for ref in refs)


def add_kernel(info_ref, left, right, out_ref):
    out_ref[...] = left[...] + right[...]


def merge_zero_kernel(info_ref, *refs):
    parts, gives, keeps = refs[:4], refs[4:7], refs[7:10]

    def source(part, third, i, high, s):
        return parts[part][i, 4 * high + s, :, THIRDS[third]]

    halve_first(source, 2, info_ref, gives, keeps, 0)


def merge_one_kernel(info_ref, *refs):
    olds, gots, parts = refs[:3], refs[3:6], refs[6:14]
    give_y, give_x, give_z = refs[14:17]
    keeps_m, keeps_a = refs[17:20], refs[20:23]

    def source(part, third, i, high, s):
        return parts[2 * part + high][i, s, :, THIRDS[third]]

    halve_second(olds, gots, 2, info_ref, (give_x, give_z, give_y), keeps_m)
    halve_first(source, 1, info_ref, (give_y, give_x, give_z), keeps_a, 8)


def merge_two_kernel(info_ref, *refs):
    olds_m, olds_a = refs[:3], refs[3:6]
    got_y, got_x, got_z = refs[6:9]
    smalls = refs[9:11]
    give_y, give_x, give_z = refs[11:14]
    keeps_m, keeps_a, small_ref = refs[14:17], refs[17:20], refs[20]
    halve_third(
        olds_m, (got_x, got_z, got_y), 0, 2, info_ref, (give_z, give_y, give_x), keeps_m
    )
    halve_second(
        olds_a,
        shift((got_y, got_x, got_z), 8),
        1,
        info_ref,
        shift((give_x, give_z, give_y), 4),
        keeps_a,
    )
    small_ref[...] = sum_refs(smalls)


def merge_three_kernel(info_ref, *refs):
    olds_m, olds_a = refs[:3], refs[3:6]
    got_y, got_x, got_z = refs[6:9]
    smalls = refs[9:11]
    give_y, give_x, give_z, give_far = refs[11:15]
    keep_m, keeps_a, small_ref = refs[15], refs[16:19], refs[19]
    halve_fourth(olds_m, (got_z, got_y, got_x), 2, info_ref, give_far, keep_m)
    halve_third(
        olds_a, (got_x, got_z, got_y), 4, 1, info_ref, (give_z, give_y, give_x), keeps_a
    )
    small_ref[...] = sum_refs(smalls)


def merge_four_kernel(info_ref, *refs):
    olds_a = refs[:3]
    got_y, got_x, got_z = refs[3:6]
    give_far, keep_a, small_ref = refs[8:]
    halve_fourth(olds_a, (got_z, got_y, got_x), 1, info_ref, give_far, keep_a)
    small_ref[...] = sum_refs(refs[6:8])


def finish_mlp_kernel(info_ref, old_m, got_far, up_ref, down_ref):
    up_ref[...] = old_m[0].astype(F32) + got_far[0].astype(F32)
    down_ref[...] = old_m[1].astype(F32) + got_far[1].astype(F32)


def merge_last_kernel(info_ref, *refs):
    old, got, qkv_ref, proj_ref = refs[:2] + refs[4:6]
    small = sum_refs(refs[2:4])
    total = old[0].astype(F32) + got[0].astype(F32)
    split = qkv_ref.shape[1]
    qkv_ref[...] = total[:, :split]
    proj_ref[...] = total[:, 512:].T[split - 512 :]
    width = small.shape[1] // 8
    place = info_ref[5] + 4 * info_ref[8]
    for d in range(8):

        @pl.when(place == d)
        def _():
            for i, ref in enumerate(refs[6:]):
                ref[...] = small[i : i + 1, d * width : (d + 1) * width]


VMEM = pl.BlockSpec(memory_space=pltpu.VMEM)
HBM = pl.BlockSpec(memory_space=pltpu.HBM)
SMEM = pl.BlockSpec(memory_space=pltpu.SMEM)


def shape(dims, dtype):
    return jax.ShapeDtypeStruct(dims, dtype)


class Order:
    def __init__(self, info):
        self.info = info

    def call(self, kernel, args, outs, scratch=(), limit=16, spaces=None):
        specs = [SMEM] + [VMEM] * len(args)
        out_specs = [VMEM] * len(outs)
        if spaces is not None:
            specs[1:] = spaces[0]
            out_specs = spaces[1]
        out = pl.pallas_call(
            kernel,
            in_specs=specs,
            out_specs=out_specs,
            out_shape=outs,
            scratch_shapes=list(scratch),
            compiler_params=pltpu.CompilerParams(vmem_limit_bytes=limit * MIB),
            cost_estimate=pl.CostEstimate(flops=1000, bytes_accessed=1000, transcendentals=0),
        )(self.info, *args)
        self.info = after(self.info, out[0])
        return out


def swap(value, axis, bit):
    size = lax.axis_size(axis)
    return lax.ppermute(value, axis, [(i, i ^ bit) for i in range(size)])


def after(value, *others):
    return lax.optimization_barrier((value,) + others)[0]


def second_hop(own):
    return swap(own, "dp", 1), swap(own, "dp", 2)


def third_hop(one, two):
    half = one.shape[0] // 2
    return swap(two[:half], "dp", 1), swap(one[half:], "dp", 2)


def assemble(order, pieces):
    return order.call(assemble_kernel, pieces, (shape((4,) + pieces[0].shape, BF16),))[0]


def swap_core(value):
    return swap(value, "tensor", 1)


def swap_y(value):
    return swap(value, "tensor", 2)


def swap_x(value):
    return swap(value, "dp", 1)


def swap_z(value):
    return swap(value, "dp", 2)


def swap_far(value):
    return swap(value, "dp", 4)


def dp_halve(value, bit):
    slices = value.shape[0]
    mine = (lax.axis_index("dp") // bit) % 2
    paired = value.reshape((slices // 2, 2) + value.shape[1:])
    keep = lax.dynamic_index_in_dim(paired, mine, 1, keepdims=False)
    give = lax.dynamic_index_in_dim(paired, 1 - mine, 1, keepdims=False)
    got = swap(give.astype(BF16), "dp", bit)
    return keep.astype(F32) + got.astype(F32)


def scatter_sum(parts, first_dp):
    shards = lax.axis_size("dp")
    zero = parts[0].astype(F32) + swap(parts[1], "tensor", 1).astype(F32)
    two = parts[2].astype(F32) + swap(parts[3], "tensor", 1).astype(F32)
    form = (shards, D // shards, parts[0].shape[1])
    zero = zero.reshape(form)
    two = two.reshape(form)
    bit = 1
    if first_dp:
        zero = dp_halve(zero, bit)
        two = dp_halve(two, bit)
        bit = 2
    zero = zero + swap(two.astype(BF16), "tensor", 2).astype(F32)
    while bit < shards:
        zero = dp_halve(zero, bit)
        bit = bit * 2
    return zero[0]


def body(
    tokens,
    out_grad,
    global_count,
    local_count,
    attn_gain,
    qkv_weight,
    proj_weight,
    attn_scale,
    mlp_gain,
    up_weight,
    down_weight,
    mlp_scale,
):
    groups = lax.axis_size("tensor")
    shards = lax.axis_size("dp")
    rows = 2 * BLOCK
    place = lax.axis_index("dp").astype(jnp.int32)
    member = lax.axis_index("tensor").astype(jnp.int32)
    where = jnp.stack([place % 4, place % 2, (place // 2) % 2, (place // 4) % 2])
    info = jnp.concatenate([member[None], global_count[0], local_count[0], where])
    row = lambda vector: vector.reshape(1, D)

    act = shape((rows, D), BF16)
    acc = shape((rows, D), F32)
    packed = shape((rows, HEAD_COLS), BF16)
    ctx = shape((rows, 256), BF16)
    unit_flops = 2 * rows * D * D

    def bind(kernel, *flags):
        def run(*refs):
            return kernel(groups, *flags, *refs)

        return run

    mixed, block_a, block_b = pl.pallas_call(
        start_kernel,
        in_specs=[HBM] * 4,
        out_specs=[VMEM] * 3,
        out_shape=(shape((D, D), BF16), shape((D // 4, D), BF16), shape((D // 2, D), BF16)),
        scratch_shapes=[pltpu.SemaphoreType.DMA((5,))],
        compiler_params=pltpu.CompilerParams(vmem_limit_bytes=60 * MIB),
    )(qkv_weight.T, proj_weight, up_weight, down_weight)
    order = Order(after(info, block_a))
    attn_gain, mlp_scale = after((attn_gain, mlp_scale), block_a)
    own_a = swap(block_a, "tensor", 2)
    wa = [mixed, swap(mixed, "tensor", 1)]
    down_one = swap(after(down_weight, block_a), "tensor", 1)
    norm, gmlp = order.call(
        bind(prepare_kernel),
        (tokens, out_grad, row(attn_gain), row(mlp_scale)),
        (act, act),
    )
    packs, ctxs = {}, {}

    def attend(r, part):
        last = r == 3
        pieced = r > 1
        args = (norm,) + (wa[r] if pieced else (wa[r],)) + part
        outs = (packed, ctx, acc)
        if pieced:
            outs += (shape((4, D // 4, D), BF16),)
        if last:
            args += (tokens, row(attn_scale), row(mlp_gain))
            outs += (acc, act)
        got = order.call(bind(attend_kernel, r == 0, last), args, outs)
        packs[r], ctxs[r] = got[:2]
        if pieced:
            wa[r] = got[3].reshape(D, D)
        return (got[2],) + tuple(got[4:])

    part = attend(0, ())
    own_a = after(own_a, part[0], wa[1], down_one)
    one_a, two_a = second_hop(own_a)
    core_a = (swap_core(own_a),)
    own_b = swap(after(block_b, own_a), "tensor", 2)
    part = attend(1, after(part, core_a[0]))
    one_a, two_a = after((one_a, two_a), part[0])
    three_a = third_hop(one_a, two_a)
    core_a += (swap_core(one_a), swap_core(two_a))
    square = shape((D, D), BF16)
    up_zero, down_zero, early_zero, early_one = order.call(
        early_kernel,
        (gmlp, down_one, up_weight, down_weight),
        (square, square, acc, acc),
        scratch=[pltpu.SemaphoreType.DMA((2,))],
        spaces=([VMEM] * 2 + [HBM] * 2, [VMEM] * 4),
    )
    own_b = after(own_b, early_zero, core_a[1], core_a[2], *three_a)
    one_b, two_b = second_hop(own_b)
    wa.append((own_a, one_a, two_a) + three_a)
    wa.append(core_a + tuple(swap_core(piece) for piece in three_a))
    part = attend(2, part)
    attn_out, middle, norm_two = attend(3, part)

    def mlp(weights, carried, extra, outs, first, last):
        return order.call(
            bind(mlp_kernel, first, last, len(weights) == 1),
            (norm_two, gmlp) + weights + carried + extra,
            (shape((2, D, D), BF16),) + tuple(outs),
            scratch=[pltpu.VMEM((rows, D), F32)] * 2 if last else [],
            limit=16,
        )

    wgrads = {}
    wgrads[0], mlp_sum, grad_sum = mlp((up_zero, down_zero, early_zero), (), (), (acc, acc), True, False)
    one_b, two_b = after((one_b, two_b), mlp_sum)
    three_b = third_hop(one_b, two_b)
    up_one = swap_core(after(up_weight, one_b))
    wgrads[1], mlp_sum, grad_sum = mlp(
        (up_one, down_one, early_one), (mlp_sum, grad_sum), (), (acc, acc), False, False
    )
    both_two = assemble(order, (own_b, one_b, two_b) + three_b)
    both_three = swap_core(both_two)
    got_one = swap_core(after(wgrads[1], both_two))
    wgrads[2], mlp_sum, grad_sum = mlp((both_two,), (mlp_sum, grad_sum), (), (acc, acc), False, False)
    extra = (middle, attn_out, out_grad, row(mlp_gain), row(mlp_scale), row(attn_scale))
    outs = (shape(tokens.shape, BF16), acc, act, shape((3, D), F32))
    wgrads[3], block_out, grad_mid, gattn, small = mlp(
        (both_three,), (mlp_sum, grad_sum), extra, outs, False, True
    )
    got_three = swap_core(wgrads[3])

    agrads, gpacks = {}, {}
    half = shape((1, D // 2, D), BF16)

    def back(r):
        out = order.call(
            bind(attend_back_kernel),
            (wa[r], packs[r], ctxs[r], gattn, norm),
            (packed, half, half),
            scratch=[pltpu.VMEM((rows, 256), BF16)],
        )
        gpacks[r] = out[0]
        agrads[r] = tuple(out[1:])

    def input_back():
        return order.call(
            input_back_kernel,
            tuple(gpacks[r] for r in range(4)) + tuple(wa) + (tokens, grad_mid, row(attn_gain), small),
            (shape(tokens.shape, BF16), shape((4, D), F32)),
            scratch=[pltpu.VMEM((rows, D), F32)],
        )

    width = D // shards
    split = qkv_weight.shape[1]
    back(1)
    if shards == 8:
        view = lambda a: a.reshape((a.shape[0], a.shape[1] // width, width, D))
        swap_pair = lambda values: tuple(swap_core(value) for value in values)
        tiny = shape((4, D), F32)
        blocks = lambda count: shape((count, width, 256), BF16)
        whole = lambda count: shape((count, width, D), BF16)
        args = tuple(view(a) for a in (wgrads[0], got_one, wgrads[2], got_three))
        out = order.call(merge_zero_kernel, args, (blocks(16),) * 6)
        keeps_m = tuple(out[3:6])
        got_m = (swap_y(out[0]), swap_x(out[1]), swap_z(out[2]))
        got_one = swap_pair(after(agrads[1], keeps_m[0]))
        back(3)
        got_three = swap_pair(agrads[3])
        back(0)
        back(2)
        args = tuple(view(a) for a in agrads[0] + got_one + agrads[2] + got_three)
        out = order.call(
            merge_one_kernel, keeps_m + got_m + args, (blocks(16),) * 3 + (blocks(8),) * 6
        )
        keeps = tuple(out[3:9])
        got = (swap_y(out[0]), swap_x(out[1]), swap_z(out[2]))
        input_grad, small = input_back()
        small = order.call(add_kernel, (small, swap(small, "tensor", 1)), (tiny,))[0]
        smalls = (small, swap_y(small))
        out = order.call(
            merge_two_kernel, keeps + got + smalls, (blocks(8),) * 3 + (blocks(4),) * 6 + (tiny,)
        )
        keeps = tuple(out[3:9])
        got = (swap_y(out[0]), swap_x(out[1]), swap_z(out[2]))
        smalls = (out[9], swap_x(out[9]))
        out = order.call(
            merge_three_kernel,
            keeps + got + smalls,
            (blocks(2),) * 3 + (whole(2), whole(2)) + (blocks(2),) * 3 + (tiny,),
        )
        keeps = tuple(out[4:8])
        got = (swap_y(out[0]), swap_x(out[1]), swap_z(out[2]), swap_far(out[3]))
        smalls = (out[8], swap_z(out[8]))
        give, keep, small = order.call(
            merge_four_kernel, keeps[1:] + got[:3] + smalls, (whole(1), whole(1), tiny)
        )
        up_grad, down_grad = order.call(
            finish_mlp_kernel, (keeps[0], got[3]), (shape((width, D), F32), shape((width, D), F32))
        )
        down_grad = down_grad.T
        out = order.call(
            merge_last_kernel,
            (keep, swap_far(give), small, swap_far(small)),
            (shape((width, split), F32), shape((D - split, width), F32)) + (shape((1, width), F32),) * 4,
        )
        smalls = [value.reshape(width) for value in out[2:]]
        qkv_grad, proj_grad = out[:2]
    else:
        for r in (3, 0, 2):
            back(r)
        input_grad, small = input_back()
        up_grad = scatter_sum([wgrads[r][0] for r in range(4)], False)
        down_grad = scatter_sum([wgrads[r][1] for r in range(4)], True).T
        mixed_grad = scatter_sum([jnp.concatenate(agrads[r], axis=1)[0] for r in range(4)], False)
        qkv_grad = mixed_grad[:, :split]
        proj_grad = mixed_grad[:, split:].T
        small = lax.psum(small, ("dp", "tensor"))
        small = lax.dynamic_slice_in_dim(small, place * width, width, axis=1)
        smalls = [small[i] for i in range(4)]
    return (
        block_out,
        input_grad,
        smalls[3],
        qkv_grad,
        proj_grad,
        smalls[2],
        smalls[1],
        up_grad,
        down_grad,
        smalls[0],
    )


def solution(mesh):
    in_specs = (
        P(None, ("dp", "tensor"), None),
        P(None, ("dp", "tensor"), None),
        P("dp", None),
        P("dp", None),
        P(),
        P(None, "tensor"),
        P("tensor", None),
        P(),
        P(),
        P(None, "tensor"),
        P("tensor", None),
        P(),
    )
    out_specs = (
        P(None, ("dp", "tensor"), None),
        P(None, ("dp", "tensor"), None),
        P("dp"),
        P("dp", "tensor"),
        P("tensor", "dp"),
        P("dp"),
        P("dp"),
        P("dp", "tensor"),
        P("tensor", "dp"),
        P("dp"),
    )
    return jax.shard_map(body, mesh=mesh, in_specs=in_specs, out_specs=out_specs, check_vma=False)
```

```python
import math

import jax
import jax.numpy as jnp
from jax import lax
from jax.experimental import pallas as pl
from jax.experimental.pallas import tpu as pltpu
from jax.sharding import PartitionSpec as P

D = 768
HD = 64
GLEN = 197
GPAD = 200
LLEN = 37
LPAD = 40
SLOT = GPAD + 2 * LPAD
GROW = 208
LROW = 2 * LPAD
BLOCK = GROW + LROW
FACTOR = HD ** (-0.5)
HEAD_COLS = 640
F32 = jnp.float32
BF16 = jnp.bfloat16
NN = (((1,), (0,)), ((), ()))
NT = (((1,), (1,)), ((), ()))
TN = (((0,), (0,)), ((), ()))
MIB = 1024 * 1024


def dot(left, right, dims=NN):
    return lax.dot_general(left, right, dims, preferred_element_type=F32)


def pad_rows(values):
    return jnp.concatenate(
        [values[:GPAD], jnp.zeros((GROW - GPAD, values.shape[1]), values.dtype), values[GPAD:]], axis=0
    )


def drop_rows(values):
    return jnp.concatenate([values[:GPAD], values[GROW:]], axis=0)


def row_keep(info_ref, micro, groups):
    member = info_ref[0]
    row = lax.broadcasted_iota(jnp.int32, (BLOCK, 1), 0)
    live = jnp.where(member < info_ref[1 + micro], GLEN, 0)
    first = jnp.where(member < info_ref[3 + micro], LLEN, 0)
    second = jnp.where(member + groups < info_ref[3 + micro], LLEN, 0)
    keep = (
        (row < live)
        | ((row >= GROW) & (row < GROW + first))
        | ((row >= GROW + LPAD) & (row < GROW + LPAD + second))
    )
    return jnp.where(keep, 1.0, 0.0).astype(F32)


def global_mask(info_ref, micro, axis):
    shape = (1, GROW) if axis == 1 else (GROW, 1)
    key = lax.broadcasted_iota(jnp.int32, shape, axis)
    live = jnp.where(info_ref[0] < info_ref[1 + micro], GLEN, 0)
    fill = jnp.where(key < GPAD, -30000.0, -3e38).astype(F32)
    return key < live, fill


def local_mask(info_ref, micro, groups, axis):
    key = lax.broadcasted_iota(jnp.int32, (LROW, LROW), axis)
    query = lax.broadcasted_iota(jnp.int32, (LROW, LROW), 1 - axis)
    member = info_ref[0]
    first = jnp.where(member < info_ref[3 + micro], LLEN, 0)
    second = jnp.where(member + groups < info_ref[3 + micro], LLEN, 0)
    same = (key < LPAD) == (query < LPAD)
    alive = (key < first) | ((key >= LPAD) & (key < LPAD + second))
    fill = jnp.where(same, -30000.0, -3e38).astype(F32)
    return same & alive, fill


def slots(info_ref, groups, axis):
    places = []
    for micro in range(2):
        start = micro * BLOCK
        places.append((slice(start, start + GROW),) + global_mask(info_ref, micro, axis))
        places.append((slice(start + GROW, start + BLOCK),) + local_mask(info_ref, micro, groups, axis))
    return places


def unit_rows(values):
    center = values - jnp.mean(values, axis=-1, keepdims=True)
    inverse = lax.rsqrt(jnp.mean(center * center, axis=-1, keepdims=True) + 1e-06)
    return center * inverse, inverse


def norm_back(grad_norm, gain, unit, inverse):
    scaled = grad_norm * gain
    centered = scaled - jnp.mean(scaled, axis=-1, keepdims=True)
    return inverse * (centered - unit * jnp.mean(scaled * unit, axis=-1, keepdims=True))


def low_half(tile):
    lane = lax.broadcasted_iota(jnp.int32, tile.shape, 1)
    return jnp.where(lane < HD, tile, jnp.zeros_like(tile))


def high_half(tile):
    lane = lax.broadcasted_iota(jnp.int32, tile.shape, 1)
    return jnp.where(lane < HD, jnp.zeros_like(tile), tile)


def turn(tile):
    return pltpu.roll(tile.astype(F32), HD, 1).astype(tile.dtype)


def softmax_rows(scores, live, fill):
    scores = jnp.where(live, scores, fill)
    raised = jnp.exp(scores - jnp.max(scores, axis=1, keepdims=True))
    return (raised * (1.0 / jnp.sum(raised, axis=1, keepdims=True))).astype(BF16)


def softmax_columns(scores, live, fill):
    scores = jnp.where(live, scores, fill)
    raised = jnp.exp(scores - jnp.max(scores, axis=0, keepdims=True))
    return raised * (1.0 / jnp.sum(raised, axis=0, keepdims=True))


def start_kernel(qkv_hbm, proj_hbm, up_hbm, down_hbm, mixed_ref, block_ref, block_b, sems):
    place = lax.rem(lax.axis_index("dp"), 4)
    quarter = D // 4
    half = D // 2
    blocks = [qkv_hbm.at[pl.ds(i * quarter, quarter)] for i in range(3)] + [proj_hbm]
    for i, block in enumerate(blocks):
        pltpu.make_async_copy(block, mixed_ref.at[pl.ds(i * quarter, quarter)], sems.at[i]).start()
    chosen = pl.ds(pl.multiple_of(lax.rem(place, 2) * half, half), half)

    @pl.when(place < 2)
    def _():
        pltpu.make_async_copy(up_hbm.at[chosen], block_b, sems.at[4]).start()

    @pl.when(place >= 2)
    def _():
        pltpu.make_async_copy(down_hbm.at[chosen], block_b, sems.at[4]).start()

    for i, block in enumerate(blocks):
        pltpu.make_async_copy(block, mixed_ref.at[pl.ds(i * quarter, quarter)], sems.at[i]).wait()
    block_ref[...] = mixed_ref[pl.ds(pl.multiple_of(place * quarter, quarter), quarter), :]
    pltpu.make_async_copy(up_hbm.at[chosen], block_b, sems.at[4]).wait()


def prepare_kernel(
    groups, info_ref, tokens_ref, grad_ref, gain_ref, scale_ref, norm_ref, gmlp_ref
):
    for micro in range(2):
        rows = slice(micro * BLOCK, (micro + 1) * BLOCK)
        values = pad_rows(tokens_ref[micro].astype(F32))
        unit, _ = unit_rows(values)
        norm_ref[rows, :] = (unit * gain_ref[...]).astype(BF16)
        keep = row_keep(info_ref, micro, groups)
        grad = pad_rows(grad_ref[micro].astype(F32))
        gmlp_ref[rows, :] = (keep * scale_ref[...] * grad).astype(BF16)


def attend_kernel(groups, first, last, *refs):
    info_ref, norm_ref = refs[:2]
    at = 2
    pieced = not first and refs[at].shape[0] < D
    if pieced:
        pieces = refs[at : at + 5]
        at += 5
    else:
        w_ref = refs[at]
        at += 1
    if not first:
        acc_ref = refs[at]
        at += 1
    if last:
        tokens_ref, scale_ref, gain_ref = refs[at : at + 3]
        at += 3
    packed_ref, ctx_ref, out_ref = refs[at : at + 3]
    at += 3
    if pieced:
        put_together(info_ref, pieces, refs[at])
        weights = refs[at][...].reshape(D, D)
        at += 1
    else:
        weights = w_ref[...]
    if last:
        middle_ref, norm_two_ref = refs[at : at + 2]
    packed_ref[...] = dot(norm_ref[...], weights[:HEAD_COLS, :], NT).astype(BF16)
    jobs = []
    for rows, live, fill in slots(info_ref, groups, 1):
        t0, t1, t2, t3, t4 = (packed_ref[rows, 128 * i : 128 * i + 128] for i in range(5))
        queries = (low_half(t0 * FACTOR), high_half(t1 * FACTOR), low_half(t3 * FACTOR))
        t2r = turn(t2)
        keys = (turn(t0), t2r, turn(t3))
        scores = [dot(query, key, NT) for query, key in zip(queries, keys)]
        jobs.append((rows, live, fill, scores, (high_half(turn(t1)), low_half(t2r), high_half(turn(t4)))))
    done = []
    for rows, live, fill, scores, values in jobs:
        done.append((rows, [softmax_rows(score, live, fill) for score in scores], values))
    for rows, probs, values in done:
        ctx_ref[rows, :128] = dot(probs[0], values[0]).astype(BF16)
        ctx_ref[rows, 128:] = (dot(probs[1], values[1]) + dot(probs[2], values[2])).astype(BF16)
    out = dot(ctx_ref[...], weights[512:, :])
    if not first:
        out = out + acc_ref[...]
    out_ref[...] = out
    if last:
        for micro in range(2):
            rows = slice(micro * BLOCK, (micro + 1) * BLOCK)
            keep = row_keep(info_ref, micro, groups)
            middle = pad_rows(tokens_ref[micro].astype(F32)) + keep * scale_ref[...] * out_ref[rows, :]
            middle_ref[rows, :] = middle
            unit, _ = unit_rows(middle)
            norm_two_ref[rows, :] = (unit * gain_ref[...]).astype(BF16)


def put_together(info_ref, pieces, out_ref):
    place = info_ref[5]
    half = out_ref.shape[1] // 2
    out_ref[place] = pieces[0][...]
    out_ref[place ^ 1] = pieces[1][...]
    out_ref[place ^ 2] = pieces[2][...]
    if len(pieces) == 4:
        out_ref[place ^ 3] = pieces[3][...]
    else:
        out_ref[place ^ 3, :half] = pieces[3][...]
        out_ref[place ^ 3, half:] = pieces[4][...]


def assemble_kernel(info_ref, *refs):
    put_together(info_ref, refs[:-1], refs[-1])


def early_kernel(info_ref, *refs):
    gmlp_ref, down_one_ref, up_hbm, down_hbm, up_one_hbm = refs[:5]
    up_ref, down_ref, up_one_ref, block_ref, out_zero, out_one, sems = refs[5:]
    fetches = (
        pltpu.make_async_copy(down_hbm, down_ref, sems.at[0]),
        pltpu.make_async_copy(up_hbm, up_ref, sems.at[1]),
        pltpu.make_async_copy(up_one_hbm, up_one_ref, sems.at[2]),
    )
    for fetch in fetches:
        fetch.start()
    out_one[...] = dot(gmlp_ref[...], down_one_ref[...], NT)
    fetches[0].wait()
    out_zero[...] = dot(gmlp_ref[...], down_ref[...], NT)
    fetches[1].wait()
    place = info_ref[5] ^ 3
    half = D // 2
    chosen = pl.ds(pl.multiple_of((place % 2) * half, half), half)

    @pl.when(place < 2)
    def _():
        block_ref[...] = up_ref[chosen, :]

    @pl.when(place >= 2)
    def _():
        block_ref[...] = down_ref[chosen, :]

    fetches[2].wait()


def mlp_kernel(groups, first, last, joined, *refs):
    info_ref, norm_ref, gmlp_ref = refs[:3]
    at = 3
    if joined:
        both_ref = refs[at]
        at += 1
    else:
        up_ref, down_ref = refs[at : at + 2]
        at += 2
    if not joined:
        early_ref = refs[at]
        at += 1
    if not first:
        mlp_in, grad_in = refs[at : at + 2]
        at += 2
    if last:
        middle_ref, attn_ref, og_ref, gain_ref, mscale_ref, ascale_ref = refs[at : at + 6]
        at += 6
    wgrad_ref = refs[at]
    at += 1
    if not last:
        mlp_ref, grad_ref = refs[at : at + 2]
    else:
        block_ref, gmid_ref, gattn_ref, small_ref, mlp_ref, grad_ref = refs[at : at + 6]
    width = 768
    for c in range(D // width):
        cols = slice(c * width, (c + 1) * width)
        if joined:
            up = both_ref[:2, :, cols].reshape(D, width)
            half = D // 2
            pieces = []
            for h in range(2):
                low = max(c * width, h * half)
                high = min((c + 1) * width, (h + 1) * half)
                if low < high:
                    pieces.append(both_ref[2 + h, low - h * half : high - h * half, :])
            down = pieces[0] if len(pieces) == 1 else jnp.concatenate(pieces, axis=0)
        else:
            up = up_ref[:, cols]
            down = down_ref[cols, :]
        hidden = dot(norm_ref[...], up)
        grad_active = dot(gmlp_ref[...], down, NT) if joined else early_ref[...]
        cdf = 0.5 + 0.5 * lax.erf(hidden * (0.5**0.5))
        active = (hidden * cdf).astype(BF16)
        slope = cdf + hidden * (jnp.exp(-0.5 * hidden * hidden) * (1.0 / math.sqrt(2.0 * math.pi)))
        grad_hidden = (grad_active * slope).astype(BF16)
        mlp = dot(active, down)
        grad = dot(grad_hidden, up, NT)
        if c > 0:
            mlp_ref[...] += mlp
            grad_ref[...] += grad
        elif first:
            mlp_ref[...] = mlp
            grad_ref[...] = grad
        else:
            mlp_ref[...] = mlp_in[...] + mlp
            grad_ref[...] = grad_in[...] + grad
        wgrad_ref[0, :, cols] = dot(norm_ref[...], grad_hidden, TN).astype(BF16)
        wgrad_ref[1, :, cols] = dot(gmlp_ref[...], active, TN).astype(BF16)
    if last:
        small = [0.0, 0.0, 0.0]
        for micro in range(2):
            rows = slice(micro * BLOCK, (micro + 1) * BLOCK)
            keep = row_keep(info_ref, micro, groups)
            middle = middle_ref[rows, :]
            mlp = mlp_ref[rows, :]
            grad_out = pad_rows(og_ref[micro].astype(F32))
            block = middle + keep * mscale_ref[...] * mlp
            block_ref[micro] = drop_rows(block).astype(BF16)
            small[0] += jnp.sum(keep * mlp * grad_out, axis=0, keepdims=True)
            unit, inverse = unit_rows(middle)
            grad_two = grad_ref[rows, :]
            small[1] += jnp.sum(grad_two * unit, axis=0, keepdims=True)
            grad_mid = grad_out + norm_back(grad_two, gain_ref[...], unit, inverse)
            gmid_ref[rows, :] = grad_mid
            small[2] += jnp.sum(keep * attn_ref[rows, :] * grad_mid, axis=0, keepdims=True)
            gattn_ref[rows, :] = (keep * ascale_ref[...] * grad_mid).astype(BF16)
        small_ref[...] = jnp.concatenate(small, axis=0)


def attend_back_kernel(groups, *refs):
    info_ref, w_ref, packed_ref, ctx_ref, gattn_ref, norm_ref = refs[:6]
    gpack_ref, low_ref, high_ref, gctx_ref = refs[6:]
    gctx_ref[...] = dot(gattn_ref[...], w_ref[512:, :], NT).astype(BF16)
    places = slots(info_ref, groups, 0)
    for pair in (places[:2], places[2:]):
        jobs = []
        for rows, live, fill in pair:
            t0, t1, t2, t3, t4 = (packed_ref[rows, 128 * i : 128 * i + 128] for i in range(5))
            g0, g1 = gctx_ref[rows, :128], gctx_ref[rows, 128:]
            t1r = turn(t1)
            t0s, t2s, t3s = turn(t0 * FACTOR), t2 * FACTOR, turn(t3 * FACTOR)
            keys = (low_half(t0s), low_half(t2s), low_half(t3s))
            values = (high_half(t1r), low_half(turn(t2)), high_half(turn(t4)))
            scores = [dot(key, query, NT) for key, query in zip(keys, (t0, t1r, t3))]
            gps = [dot(value, grad, NT) for value, grad in zip(values, (g0, g1, g1))]
            tiles = (t0s, low_half(t1r * FACTOR), high_half(turn(t2s)), t3s, turn(g0), turn(g1))
            jobs.append((rows, live, fill, scores, gps, tiles))
        done = []
        for rows, live, fill, scores, gps, tiles in jobs:
            probs = [softmax_columns(score, live, fill) for score in scores]
            dots = [jnp.sum(prob * gp, axis=0, keepdims=True) for prob, gp in zip(probs, gps)]
            gs = [(prob * (gp - row)).astype(BF16) for prob, gp, row in zip(probs, gps, dots)]
            done.append((rows, [prob.astype(BF16) for prob in probs], gs, tiles))
        for rows, probs, gs, (t0s, query_b, key_b, t3s, g0r, g1r) in done:
            columns = (
                dot(gs[0], low_half(t0s), TN) + dot(gs[0], high_half(t0s)),
                dot(probs[0], low_half(g0r)) + dot(gs[1], key_b, TN),
                dot(gs[1], query_b) + dot(probs[1], high_half(g1r)),
                dot(gs[2], low_half(t3s), TN) + dot(gs[2], high_half(t3s)),
                dot(probs[2], low_half(g1r)),
            )
            for i, column in enumerate(columns):
                gpack_ref[rows, 128 * i : 128 * i + 128] = column.astype(BF16)
    half = D // 2
    for top, out in enumerate((low_ref, high_ref)):
        columns = slice(top * half, (top + 1) * half)
        norm = norm_ref[:, columns]
        out[0, :, :512] = dot(norm, gpack_ref[:, :512], TN).astype(BF16)
        tail = dot(gattn_ref[:, columns], ctx_ref[...], TN)
        out[0, :, 512:640] = (dot(norm, gpack_ref[:, 512:640], TN) + tail[:, :128]).astype(BF16)
        out[0, :, 640:] = tail[:, 128:].astype(BF16)


def input_back_kernel(info_ref, *refs):
    gpacks, weights = refs[:4], refs[4:8]
    tokens_ref, gmid_ref, gain_ref, three_ref, igrad_ref, small_ref, sum_ref = refs[8:]
    sum_ref[...] = dot(gpacks[0][...], weights[0][:HEAD_COLS, :])
    for gpack_ref, w_ref in zip(gpacks[1:], weights[1:]):
        sum_ref[...] += dot(gpack_ref[...], w_ref[:HEAD_COLS, :])
    small = 0.0
    for micro in range(2):
        rows = slice(micro * BLOCK, (micro + 1) * BLOCK)
        unit, inverse = unit_rows(pad_rows(tokens_ref[micro].astype(F32)))
        own = sum_ref[rows, :]
        small += jnp.sum(own * unit, axis=0, keepdims=True)
        back_rows = gmid_ref[rows, :] + norm_back(own, gain_ref[...], unit, inverse)
        igrad_ref[micro] = drop_rows(back_rows).astype(BF16)
    small_ref[...] = jnp.concatenate([three_ref[...], small], axis=0)


def add(left, right):
    return left + right


THIRDS = (slice(0, 256), slice(256, 512), slice(512, 768))


def sum_refs(refs):
    total = refs[0][...]
    for ref in refs[1:]:
        total = total + ref[...]
    return total


def halve_first(sources, count, info_ref, gives, keeps, base):
    x, z = info_ref[6], info_ref[7]
    give_y, give_x, give_z = gives
    keep_a, keep_b, keep_c = keeps

    def pair(low, third, i, high, s):
        return add(sources(low, third, i, high, s), sources(low + 1, third, i, high, s))

    for i in range(count):
        for s in range(8):
            give_y[base + 8 * i + s] = pair(2, 0, i, s // 4, s % 4)
            keep_a[8 * i + s] = pair(0, 0, i, s // 4, s % 4)
        for side in range(2):
            for s in range(4):
                at = 8 * i + 4 * side + s
                low = 2 * (s % 2)
                keep_b[at] = pair(2 * side, 1, i, s // 2, low + x)
                give_x[base + at] = pair(2 * side, 1, i, s // 2, low + 1 - x)
                low = s % 2
                keep_c[at] = pair(2 * side, 2, i, s // 2, low + 2 * z)
                give_z[base + at] = pair(2 * side, 2, i, s // 2, low + 2 * (1 - z))


def halve_second(olds, gots, count, info_ref, gives, keeps):
    x, z = info_ref[6], info_ref[7]
    give_x, give_z, give_y = gives
    keep_a, keep_b, keep_c = keeps
    old_a, old_b, old_c = olds
    got_a, got_b, got_c = gots
    for i in range(count):
        for s in range(4):
            at, low = 4 * i + s, 8 * i + 2 * s
            keep_a[at] = add(old_a[low + x], got_a[low + x])
            give_x[at] = add(old_a[low + 1 - x], got_a[low + 1 - x])
            keep_c[at] = add(old_c[8 * i + s], got_c[8 * i + s])
            give_y[at] = add(old_c[8 * i + 4 + s], got_c[8 * i + 4 + s])
        for side in range(2):
            for s in range(2):
                at, low = 4 * i + 2 * side + s, 8 * i + 4 * side + 2 * s
                keep_b[at] = add(old_b[low + z], got_b[low + z])
                give_z[at] = add(old_b[low + 1 - z], got_b[low + 1 - z])


def halve_third(olds, gots, skip, count, info_ref, gives, keeps):
    x, z = info_ref[6], info_ref[7]
    give_z, give_y, give_x = gives
    keep_a, keep_b, keep_c = keeps
    old_a, old_b, old_c = olds
    got_a, got_b, got_c = gots
    for i in range(count):
        for s in range(2):
            at, low = 2 * i + s, 4 * i + 2 * s
            keep_a[at] = add(old_a[low + z], got_a[skip + low + z])
            give_z[at] = add(old_a[low + 1 - z], got_a[skip + low + 1 - z])
            low = 4 * i + s
            keep_b[at] = add(old_b[low], got_b[skip + low])
            give_y[at] = add(old_b[low + 2], got_b[skip + low + 2])
            low = 4 * i + 2 * s
            keep_c[at] = add(old_c[low + x], got_c[skip + low + x])
            give_x[at] = add(old_c[low + 1 - x], got_c[skip + low + 1 - x])


def halve_fourth(olds, gots, count, info_ref, give, keep):
    z = info_ref[8]
    for i in range(count):
        for old, got, third in zip(olds, gots, THIRDS):
            keep[i, :, third] = add(old[2 * i + z], got[2 * i + z])
            give[i, :, third] = add(old[2 * i + 1 - z], got[2 * i + 1 - z])


class Shifted:
    def __init__(self, ref, offset):
        self.ref = ref
        self.offset = offset

    def __getitem__(self, at):
        return self.ref[self.offset + at]

    def __setitem__(self, at, value):
        self.ref[self.offset + at] = value


def shift(refs, offset):
    return tuple(Shifted(ref, offset) for ref in refs)


def add_kernel(info_ref, left, right, out_ref):
    out_ref[...] = left[...] + right[...]


def merge_zero_kernel(info_ref, *refs):
    parts, gives, keeps = refs[:4], refs[4:7], refs[7:10]

    def source(part, third, i, high, s):
        return parts[part][i, 4 * high + s, :, THIRDS[third]]

    halve_first(source, 2, info_ref, gives, keeps, 0)


def merge_one_kernel(info_ref, *refs):
    olds, gots, parts = refs[:3], refs[3:6], refs[6:14]
    give_y, give_x, give_z = refs[14:17]
    keeps_m, keeps_a = refs[17:20], refs[20:23]

    def source(part, third, i, high, s):
        return parts[2 * part + high][i, s, :, THIRDS[third]]

    halve_second(olds, gots, 2, info_ref, (give_x, give_z, give_y), keeps_m)
    halve_first(source, 1, info_ref, (give_y, give_x, give_z), keeps_a, 8)


def merge_two_kernel(info_ref, *refs):
    olds_m, olds_a = refs[:3], refs[3:6]
    got_y, got_x, got_z = refs[6:9]
    smalls = refs[9:11]
    give_y, give_x, give_z = refs[11:14]
    keeps_m, keeps_a, small_ref = refs[14:17], refs[17:20], refs[20]
    halve_third(
        olds_m, (got_x, got_z, got_y), 0, 2, info_ref, (give_z, give_y, give_x), keeps_m
    )
    halve_second(
        olds_a,
        shift((got_y, got_x, got_z), 8),
        1,
        info_ref,
        shift((give_x, give_z, give_y), 4),
        keeps_a,
    )
    small_ref[...] = sum_refs(smalls)


def merge_three_kernel(info_ref, *refs):
    olds_m, olds_a = refs[:3], refs[3:6]
    got_y, got_x, got_z = refs[6:9]
    smalls = refs[9:11]
    give_y, give_x, give_z, give_far = refs[11:15]
    keep_m, keeps_a, small_ref = refs[15], refs[16:19], refs[19]
    halve_fourth(olds_m, (got_z, got_y, got_x), 2, info_ref, give_far, keep_m)
    halve_third(
        olds_a, (got_x, got_z, got_y), 4, 1, info_ref, (give_z, give_y, give_x), keeps_a
    )
    small_ref[...] = sum_refs(smalls)


def merge_four_kernel(info_ref, *refs):
    olds_a = refs[:3]
    got_y, got_x, got_z = refs[3:6]
    give_far, keep_a, small_ref = refs[8:]
    halve_fourth(olds_a, (got_z, got_y, got_x), 1, info_ref, give_far, keep_a)
    small_ref[...] = sum_refs(refs[6:8])


def finish_mlp_kernel(info_ref, old_m, got_far, up_ref, down_ref):
    up_ref[...] = old_m[0].astype(F32) + got_far[0].astype(F32)
    down_ref[...] = old_m[1].astype(F32) + got_far[1].astype(F32)


def merge_last_kernel(info_ref, *refs):
    old, got, qkv_ref, proj_ref = refs[:2] + refs[4:6]
    small = sum_refs(refs[2:4])
    total = old[0].astype(F32) + got[0].astype(F32)
    split = qkv_ref.shape[1]
    qkv_ref[...] = total[:, :split]
    proj_ref[...] = total[:, 512:].T[split - 512 :]
    width = small.shape[1] // 8
    place = info_ref[5] + 4 * info_ref[8]
    for d in range(8):

        @pl.when(place == d)
        def _():
            for i, ref in enumerate(refs[6:]):
                ref[...] = small[i : i + 1, d * width : (d + 1) * width]


VMEM = pl.BlockSpec(memory_space=pltpu.VMEM)
HBM = pl.BlockSpec(memory_space=pltpu.HBM)
SMEM = pl.BlockSpec(memory_space=pltpu.SMEM)


def shape(dims, dtype):
    return jax.ShapeDtypeStruct(dims, dtype)


class Order:
    def __init__(self, info):
        self.info = info

    def call(self, kernel, args, outs, scratch=(), limit=16, spaces=None):
        specs = [SMEM] + [VMEM] * len(args)
        out_specs = [VMEM] * len(outs)
        if spaces is not None:
            specs[1:] = spaces[0]
            out_specs = spaces[1]
        out = pl.pallas_call(
            kernel,
            in_specs=specs,
            out_specs=out_specs,
            out_shape=outs,
            scratch_shapes=list(scratch),
            compiler_params=pltpu.CompilerParams(vmem_limit_bytes=limit * MIB),
            cost_estimate=pl.CostEstimate(flops=1000, bytes_accessed=1000, transcendentals=0),
        )(self.info, *args)
        self.info = after(self.info, out[0])
        return out


def swap(value, axis, bit):
    size = lax.axis_size(axis)
    return lax.ppermute(value, axis, [(i, i ^ bit) for i in range(size)])


def after(value, *others):
    return lax.optimization_barrier((value,) + others)[0]


def second_hop(own):
    return swap(own, "dp", 1), swap(own, "dp", 2)


def third_hop(one, two):
    half = one.shape[0] // 2
    return swap(two[:half], "dp", 1), swap(one[half:], "dp", 2)


def assemble(order, pieces):
    return order.call(assemble_kernel, pieces, (shape((4,) + pieces[0].shape, BF16),))[0]


def swap_core(value):
    return swap(value, "tensor", 1)


def swap_y(value):
    return swap(value, "tensor", 2)


def swap_x(value):
    return swap(value, "dp", 1)


def swap_z(value):
    return swap(value, "dp", 2)


def swap_far(value):
    return swap(value, "dp", 4)


def dp_halve(value, bit):
    slices = value.shape[0]
    mine = (lax.axis_index("dp") // bit) % 2
    paired = value.reshape((slices // 2, 2) + value.shape[1:])
    keep = lax.dynamic_index_in_dim(paired, mine, 1, keepdims=False)
    give = lax.dynamic_index_in_dim(paired, 1 - mine, 1, keepdims=False)
    got = swap(give.astype(BF16), "dp", bit)
    return keep.astype(F32) + got.astype(F32)


def scatter_sum(parts, first_dp):
    shards = lax.axis_size("dp")
    zero = parts[0].astype(F32) + swap(parts[1], "tensor", 1).astype(F32)
    two = parts[2].astype(F32) + swap(parts[3], "tensor", 1).astype(F32)
    form = (shards, D // shards, parts[0].shape[1])
    zero = zero.reshape(form)
    two = two.reshape(form)
    bit = 1
    if first_dp:
        zero = dp_halve(zero, bit)
        two = dp_halve(two, bit)
        bit = 2
    zero = zero + swap(two.astype(BF16), "tensor", 2).astype(F32)
    while bit < shards:
        zero = dp_halve(zero, bit)
        bit = bit * 2
    return zero[0]


def body(
    tokens,
    out_grad,
    global_count,
    local_count,
    attn_gain,
    qkv_weight,
    proj_weight,
    attn_scale,
    mlp_gain,
    up_weight,
    down_weight,
    mlp_scale,
):
    groups = lax.axis_size("tensor")
    shards = lax.axis_size("dp")
    rows = 2 * BLOCK
    place = lax.axis_index("dp").astype(jnp.int32)
    member = lax.axis_index("tensor").astype(jnp.int32)
    where = jnp.stack([place % 4, place % 2, (place // 2) % 2, (place // 4) % 2])
    info = jnp.concatenate([member[None], global_count[0], local_count[0], where])
    row = lambda vector: vector.reshape(1, D)

    act = shape((rows, D), BF16)
    acc = shape((rows, D), F32)
    packed = shape((rows, HEAD_COLS), BF16)
    ctx = shape((rows, 256), BF16)
    unit_flops = 2 * rows * D * D

    def bind(kernel, *flags):
        def run(*refs):
            return kernel(groups, *flags, *refs)

        return run

    mixed, block_a, block_b = pl.pallas_call(
        start_kernel,
        in_specs=[HBM] * 4,
        out_specs=[VMEM] * 3,
        out_shape=(shape((D, D), BF16), shape((D // 4, D), BF16), shape((D // 2, D), BF16)),
        scratch_shapes=[pltpu.SemaphoreType.DMA((5,))],
        compiler_params=pltpu.CompilerParams(vmem_limit_bytes=60 * MIB),
    )(qkv_weight.T, proj_weight, up_weight, down_weight)
    order = Order(after(info, block_a))
    attn_gain, mlp_scale = after((attn_gain, mlp_scale), block_a)
    own_a = swap(block_a, "tensor", 2)
    wa = [mixed, swap(mixed, "tensor", 1)]
    up_one = swap_core(after(up_weight, block_a))
    norm, gmlp = order.call(
        bind(prepare_kernel),
        (tokens, out_grad, row(attn_gain), row(mlp_scale)),
        (act, act),
    )
    packs, ctxs = {}, {}

    def attend(r, part):
        last = r == 3
        pieced = r > 1
        args = (norm,) + (wa[r] if pieced else (wa[r],)) + part
        outs = (packed, ctx, acc)
        if pieced:
            outs += (shape((4, D // 4, D), BF16),)
        if last:
            args += (tokens, row(attn_scale), row(mlp_gain))
            outs += (acc, act)
        got = order.call(bind(attend_kernel, r == 0, last), args, outs)
        packs[r], ctxs[r] = got[:2]
        if pieced:
            wa[r] = got[3].reshape(D, D)
        return (got[2],) + tuple(got[4:])

    part = attend(0, ())
    own_a = after(own_a, part[0], wa[1], up_one)
    one_a, two_a = second_hop(own_a)
    core_a = (swap_core(own_a),)
    own_b = swap(after(block_b, own_a), "tensor", 2)
    down_one = swap_core(after(down_weight, own_a))
    part = attend(1, after(part, core_a[0], down_one))
    one_a, two_a = after((one_a, two_a), part[0])
    three_a = third_hop(one_a, two_a)
    core_a += (swap_core(one_a), swap_core(two_a))
    square = shape((D, D), BF16)
    up_zero, down_zero, up_one, block_c, early_zero, early_one = order.call(
        early_kernel,
        (gmlp, down_one, up_weight, down_weight, up_one),
        (square, square, square, shape((D // 2, D), BF16), acc, acc),
        scratch=[pltpu.SemaphoreType.DMA((3,))],
        spaces=([VMEM] * 2 + [HBM] * 3, [VMEM] * 6),
    )
    three_b = swap(block_c, "tensor", 2)
    own_b = after(own_b, early_zero, core_a[1], core_a[2], *three_a)
    one_b, two_b = second_hop(own_b)
    wa.append((own_a, one_a, two_a) + three_a)
    wa.append(core_a + tuple(swap_core(piece) for piece in three_a))
    part = attend(2, part)
    attn_out, middle, norm_two = attend(3, part)

    def mlp(weights, carried, extra, outs, first, last):
        return order.call(
            bind(mlp_kernel, first, last, len(weights) == 1),
            (norm_two, gmlp) + weights + carried + extra,
            (shape((2, D, D), BF16),) + tuple(outs),
            scratch=[pltpu.VMEM((rows, D), F32)] * 2 if last else [],
            limit=16,
        )

    wgrads = {}
    wgrads[0], mlp_sum, grad_sum = mlp((up_zero, down_zero, early_zero), (), (), (acc, acc), True, False)
    wgrads[1], mlp_sum, grad_sum = mlp(
        (up_one, down_one, early_one), (mlp_sum, grad_sum), (), (acc, acc), False, False
    )
    both_two = assemble(order, (own_b, one_b, two_b, three_b))
    both_three = swap_core(both_two)
    got_one = swap_core(after(wgrads[1], both_two))
    wgrads[2], mlp_sum, grad_sum = mlp((both_two,), (mlp_sum, grad_sum), (), (acc, acc), False, False)
    extra = (middle, attn_out, out_grad, row(mlp_gain), row(mlp_scale), row(attn_scale))
    outs = (shape(tokens.shape, BF16), acc, act, shape((3, D), F32))
    wgrads[3], block_out, grad_mid, gattn, small = mlp(
        (both_three,), (mlp_sum, grad_sum), extra, outs, False, True
    )
    got_three = swap_core(wgrads[3])

    agrads, gpacks = {}, {}
    half = shape((1, D // 2, D), BF16)

    def back(r):
        out = order.call(
            bind(attend_back_kernel),
            (wa[r], packs[r], ctxs[r], gattn, norm),
            (packed, half, half),
            scratch=[pltpu.VMEM((rows, 256), BF16)],
        )
        gpacks[r] = out[0]
        agrads[r] = tuple(out[1:])

    def input_back():
        return order.call(
            input_back_kernel,
            tuple(gpacks[r] for r in range(4)) + tuple(wa) + (tokens, grad_mid, row(attn_gain), small),
            (shape(tokens.shape, BF16), shape((4, D), F32)),
            scratch=[pltpu.VMEM((rows, D), F32)],
        )

    width = D // shards
    split = qkv_weight.shape[1]
    back(1)
    if shards == 8:
        view = lambda a: a.reshape((a.shape[0], a.shape[1] // width, width, D))
        swap_pair = lambda values: tuple(swap_core(value) for value in values)
        tiny = shape((4, D), F32)
        blocks = lambda count: shape((count, width, 256), BF16)
        whole = lambda count: shape((count, width, D), BF16)
        args = tuple(view(a) for a in (wgrads[0], got_one, wgrads[2], got_three))
        out = order.call(merge_zero_kernel, args, (blocks(16),) * 6)
        keeps_m = tuple(out[3:6])
        got_m = (swap_y(out[0]), swap_x(out[1]), swap_z(out[2]))
        got_one = swap_pair(after(agrads[1], keeps_m[0]))
        back(3)
        got_three = swap_pair(agrads[3])
        back(0)
        back(2)
        args = tuple(view(a) for a in agrads[0] + got_one + agrads[2] + got_three)
        out = order.call(
            merge_one_kernel, keeps_m + got_m + args, (blocks(16),) * 3 + (blocks(8),) * 6
        )
        keeps = tuple(out[3:9])
        got = (swap_y(out[0]), swap_x(out[1]), swap_z(out[2]))
        input_grad, small = input_back()
        small = order.call(add_kernel, (small, swap(small, "tensor", 1)), (tiny,))[0]
        smalls = (small, swap_y(small))
        out = order.call(
            merge_two_kernel, keeps + got + smalls, (blocks(8),) * 3 + (blocks(4),) * 6 + (tiny,)
        )
        keeps = tuple(out[3:9])
        got = (swap_y(out[0]), swap_x(out[1]), swap_z(out[2]))
        smalls = (out[9], swap_x(out[9]))
        out = order.call(
            merge_three_kernel,
            keeps + got + smalls,
            (blocks(2),) * 3 + (whole(2), whole(2)) + (blocks(2),) * 3 + (tiny,),
        )
        keeps = tuple(out[4:8])
        got = (swap_y(out[0]), swap_x(out[1]), swap_z(out[2]), swap_far(out[3]))
        smalls = (out[8], swap_z(out[8]))
        give, keep, small = order.call(
            merge_four_kernel, keeps[1:] + got[:3] + smalls, (whole(1), whole(1), tiny)
        )
        up_grad, down_grad = order.call(
            finish_mlp_kernel, (keeps[0], got[3]), (shape((width, D), F32), shape((width, D), F32))
        )
        down_grad = down_grad.T
        out = order.call(
            merge_last_kernel,
            (keep, swap_far(give), small, swap_far(small)),
            (shape((width, split), F32), shape((D - split, width), F32)) + (shape((1, width), F32),) * 4,
        )
        smalls = [value.reshape(width) for value in out[2:]]
        qkv_grad, proj_grad = out[:2]
    else:
        for r in (3, 0, 2):
            back(r)
        input_grad, small = input_back()
        up_grad = scatter_sum([wgrads[r][0] for r in range(4)], False)
        down_grad = scatter_sum([wgrads[r][1] for r in range(4)], True).T
        mixed_grad = scatter_sum([jnp.concatenate(agrads[r], axis=1)[0] for r in range(4)], False)
        qkv_grad = mixed_grad[:, :split]
        proj_grad = mixed_grad[:, split:].T
        small = lax.psum(small, ("dp", "tensor"))
        small = lax.dynamic_slice_in_dim(small, place * width, width, axis=1)
        smalls = [small[i] for i in range(4)]
    return (
        block_out,
        input_grad,
        smalls[3],
        qkv_grad,
        proj_grad,
        smalls[2],
        smalls[1],
        up_grad,
        down_grad,
        smalls[0],
    )


def solution(mesh):
    in_specs = (
        P(None, ("dp", "tensor"), None),
        P(None, ("dp", "tensor"), None),
        P("dp", None),
        P("dp", None),
        P(),
        P(None, "tensor"),
        P("tensor", None),
        P(),
        P(),
        P(None, "tensor"),
        P("tensor", None),
        P(),
    )
    out_specs = (
        P(None, ("dp", "tensor"), None),
        P(None, ("dp", "tensor"), None),
        P("dp"),
        P("dp", "tensor"),
        P("tensor", "dp"),
        P("dp"),
        P("dp"),
        P("dp", "tensor"),
        P("tensor", "dp"),
        P("dp"),
    )
    return jax.shard_map(body, mesh=mesh, in_specs=in_specs, out_specs=out_specs, check_vma=False)
```

```python
import math

import jax
import jax.numpy as jnp
from jax import lax
from jax.experimental import pallas as pl
from jax.experimental.pallas import tpu as pltpu
from jax.sharding import PartitionSpec as P

D = 768
HD = 64
GLEN = 197
GPAD = 200
LLEN = 37
LPAD = 40
SLOT = GPAD + 2 * LPAD
GROW = 208
LROW = 2 * LPAD
BLOCK = GROW + LROW
FACTOR = HD ** (-0.5)
HEAD_COLS = 640
F32 = jnp.float32
BF16 = jnp.bfloat16
NN = (((1,), (0,)), ((), ()))
NT = (((1,), (1,)), ((), ()))
TN = (((0,), (0,)), ((), ()))
MIB = 1024 * 1024


def dot(left, right, dims=NN):
    return lax.dot_general(left, right, dims, preferred_element_type=F32)


def pad_rows(values):
    return jnp.concatenate(
        [values[:GPAD], jnp.zeros((GROW - GPAD, values.shape[1]), values.dtype), values[GPAD:]], axis=0
    )


def drop_rows(values):
    return jnp.concatenate([values[:GPAD], values[GROW:]], axis=0)


def row_keep(info_ref, micro, groups):
    member = info_ref[0]
    row = lax.broadcasted_iota(jnp.int32, (BLOCK, 1), 0)
    live = jnp.where(member < info_ref[1 + micro], GLEN, 0)
    first = jnp.where(member < info_ref[3 + micro], LLEN, 0)
    second = jnp.where(member + groups < info_ref[3 + micro], LLEN, 0)
    keep = (
        (row < live)
        | ((row >= GROW) & (row < GROW + first))
        | ((row >= GROW + LPAD) & (row < GROW + LPAD + second))
    )
    return jnp.where(keep, 1.0, 0.0).astype(F32)


def global_mask(info_ref, micro, axis):
    shape = (1, GROW) if axis == 1 else (GROW, 1)
    key = lax.broadcasted_iota(jnp.int32, shape, axis)
    live = jnp.where(info_ref[0] < info_ref[1 + micro], GLEN, 0)
    fill = jnp.where(key < GPAD, -30000.0, -3e38).astype(F32)
    return key < live, fill


def local_mask(info_ref, micro, groups, axis):
    key = lax.broadcasted_iota(jnp.int32, (LROW, LROW), axis)
    query = lax.broadcasted_iota(jnp.int32, (LROW, LROW), 1 - axis)
    member = info_ref[0]
    first = jnp.where(member < info_ref[3 + micro], LLEN, 0)
    second = jnp.where(member + groups < info_ref[3 + micro], LLEN, 0)
    same = (key < LPAD) == (query < LPAD)
    alive = (key < first) | ((key >= LPAD) & (key < LPAD + second))
    fill = jnp.where(same, -30000.0, -3e38).astype(F32)
    return same & alive, fill


def slots(info_ref, groups, axis):
    places = []
    for micro in range(2):
        start = micro * BLOCK
        places.append((slice(start, start + GROW),) + global_mask(info_ref, micro, axis))
        places.append((slice(start + GROW, start + BLOCK),) + local_mask(info_ref, micro, groups, axis))
    return places


def unit_rows(values):
    center = values - jnp.mean(values, axis=-1, keepdims=True)
    inverse = lax.rsqrt(jnp.mean(center * center, axis=-1, keepdims=True) + 1e-06)
    return center * inverse, inverse


def norm_back(grad_norm, gain, unit, inverse):
    scaled = grad_norm * gain
    centered = scaled - jnp.mean(scaled, axis=-1, keepdims=True)
    return inverse * (centered - unit * jnp.mean(scaled * unit, axis=-1, keepdims=True))


def low_half(tile):
    lane = lax.broadcasted_iota(jnp.int32, tile.shape, 1)
    return jnp.where(lane < HD, tile, jnp.zeros_like(tile))


def high_half(tile):
    lane = lax.broadcasted_iota(jnp.int32, tile.shape, 1)
    return jnp.where(lane < HD, jnp.zeros_like(tile), tile)


def turn(tile):
    return pltpu.roll(tile.astype(F32), HD, 1).astype(tile.dtype)


def softmax_rows(scores, live, fill):
    scores = jnp.where(live, scores, fill)
    raised = jnp.exp(scores - jnp.max(scores, axis=1, keepdims=True))
    return (raised * (1.0 / jnp.sum(raised, axis=1, keepdims=True))).astype(BF16)


def softmax_columns(scores, live, fill):
    scores = jnp.where(live, scores, fill)
    raised = jnp.exp(scores - jnp.max(scores, axis=0, keepdims=True))
    return raised * (1.0 / jnp.sum(raised, axis=0, keepdims=True))


def start_kernel(qkv_hbm, proj_hbm, up_hbm, down_hbm, mixed_ref, block_ref, block_b, sems):
    place = lax.rem(lax.axis_index("dp"), 4)
    quarter = D // 4
    half = D // 2
    blocks = [qkv_hbm.at[pl.ds(i * quarter, quarter)] for i in range(3)] + [proj_hbm]
    for i, block in enumerate(blocks):
        pltpu.make_async_copy(block, mixed_ref.at[pl.ds(i * quarter, quarter)], sems.at[i]).start()
    chosen = pl.ds(pl.multiple_of(lax.rem(place, 2) * half, half), half)

    @pl.when(place < 2)
    def _():
        pltpu.make_async_copy(up_hbm.at[chosen], block_b, sems.at[4]).start()

    @pl.when(place >= 2)
    def _():
        pltpu.make_async_copy(down_hbm.at[chosen], block_b, sems.at[4]).start()

    for i, block in enumerate(blocks):
        pltpu.make_async_copy(block, mixed_ref.at[pl.ds(i * quarter, quarter)], sems.at[i]).wait()
    block_ref[...] = mixed_ref[pl.ds(pl.multiple_of(place * quarter, quarter), quarter), :]
    pltpu.make_async_copy(up_hbm.at[chosen], block_b, sems.at[4]).wait()


def prepare_kernel(
    groups, info_ref, tokens_ref, grad_ref, gain_ref, scale_ref, norm_ref, gmlp_ref
):
    for micro in range(2):
        rows = slice(micro * BLOCK, (micro + 1) * BLOCK)
        values = pad_rows(tokens_ref[micro].astype(F32))
        unit, _ = unit_rows(values)
        norm_ref[rows, :] = (unit * gain_ref[...]).astype(BF16)
        keep = row_keep(info_ref, micro, groups)
        grad = pad_rows(grad_ref[micro].astype(F32))
        gmlp_ref[rows, :] = (keep * scale_ref[...] * grad).astype(BF16)


def attend_kernel(groups, first, last, *refs):
    info_ref, norm_ref = refs[:2]
    at = 2
    pieced = not first and refs[at].shape[0] < D
    if pieced:
        pieces = refs[at : at + 5]
        at += 5
    else:
        w_ref = refs[at]
        at += 1
    if not first:
        acc_ref = refs[at]
        at += 1
    if last:
        tokens_ref, scale_ref, gain_ref = refs[at : at + 3]
        at += 3
    packed_ref, ctx_ref, out_ref = refs[at : at + 3]
    at += 3
    if pieced:
        put_together(info_ref, pieces, refs[at])
        weights = refs[at][...].reshape(D, D)
        at += 1
    else:
        weights = w_ref[...]
    if last:
        middle_ref, norm_two_ref = refs[at : at + 2]
    packed_ref[...] = dot(norm_ref[...], weights[:HEAD_COLS, :], NT).astype(BF16)
    jobs = []
    for rows, live, fill in slots(info_ref, groups, 1):
        t0, t1, t2, t3, t4 = (packed_ref[rows, 128 * i : 128 * i + 128] for i in range(5))
        queries = (low_half(t0 * FACTOR), high_half(t1 * FACTOR), low_half(t3 * FACTOR))
        t2r = turn(t2)
        keys = (turn(t0), t2r, turn(t3))
        scores = [dot(query, key, NT) for query, key in zip(queries, keys)]
        jobs.append((rows, live, fill, scores, (high_half(turn(t1)), low_half(t2r), high_half(turn(t4)))))
    done = []
    for rows, live, fill, scores, values in jobs:
        done.append((rows, [softmax_rows(score, live, fill) for score in scores], values))
    for rows, probs, values in done:
        ctx_ref[rows, :128] = dot(probs[0], values[0]).astype(BF16)
        ctx_ref[rows, 128:] = (dot(probs[1], values[1]) + dot(probs[2], values[2])).astype(BF16)
    out = dot(ctx_ref[...], weights[512:, :])
    if not first:
        out = out + acc_ref[...]
    out_ref[...] = out
    if last:
        for micro in range(2):
            rows = slice(micro * BLOCK, (micro + 1) * BLOCK)
            keep = row_keep(info_ref, micro, groups)
            middle = pad_rows(tokens_ref[micro].astype(F32)) + keep * scale_ref[...] * out_ref[rows, :]
            middle_ref[rows, :] = middle
            unit, _ = unit_rows(middle)
            norm_two_ref[rows, :] = (unit * gain_ref[...]).astype(BF16)


def put_together(info_ref, pieces, out_ref):
    place = info_ref[5]
    half = out_ref.shape[1] // 2
    out_ref[place] = pieces[0][...]
    out_ref[place ^ 1] = pieces[1][...]
    out_ref[place ^ 2] = pieces[2][...]
    if len(pieces) == 4:
        out_ref[place ^ 3] = pieces[3][...]
    else:
        out_ref[place ^ 3, :half] = pieces[3][...]
        out_ref[place ^ 3, half:] = pieces[4][...]


def assemble_kernel(info_ref, *refs):
    put_together(info_ref, refs[:-1], refs[-1])


def early_kernel(info_ref, *refs):
    gmlp_ref, down_one_ref, up_hbm, down_hbm, up_one_hbm = refs[:5]
    up_ref, down_ref, up_one_ref, block_ref, out_zero, out_one, sems = refs[5:]
    fetches = (
        pltpu.make_async_copy(down_hbm, down_ref, sems.at[0]),
        pltpu.make_async_copy(up_hbm, up_ref, sems.at[1]),
        pltpu.make_async_copy(up_one_hbm, up_one_ref, sems.at[2]),
    )
    for fetch in fetches:
        fetch.start()
    out_one[...] = dot(gmlp_ref[...], down_one_ref[...], NT)
    fetches[0].wait()
    out_zero[...] = dot(gmlp_ref[...], down_ref[...], NT)
    fetches[1].wait()
    place = info_ref[5] ^ 3
    half = D // 2
    chosen = pl.ds(pl.multiple_of((place % 2) * half, half), half)

    @pl.when(place < 2)
    def _():
        block_ref[...] = up_ref[chosen, :]

    @pl.when(place >= 2)
    def _():
        block_ref[...] = down_ref[chosen, :]

    fetches[2].wait()


def hidden_quarter(norm_ref, gmlp_ref, up, grad_active, wgrad_ref, active_ref):
    hidden = dot(norm_ref[...], up)
    cdf = 0.5 + 0.5 * lax.erf(hidden * (0.5**0.5))
    active_ref[...] = (hidden * cdf).astype(BF16)
    slope = cdf + hidden * (jnp.exp(-0.5 * hidden * hidden) * (1.0 / math.sqrt(2.0 * math.pi)))
    grad_hidden = (grad_active * slope).astype(BF16)
    wgrad_ref[0] = dot(norm_ref[...], grad_hidden, TN).astype(BF16)
    wgrad_ref[1] = dot(gmlp_ref[...], active_ref[...], TN).astype(BF16)
    return dot(grad_hidden, up, NT)


def mlp_pair_kernel(groups, info_ref, *refs):
    norm_ref, gmlp_ref, up_a, early_a, up_b, early_b = refs[:6]
    wgrad_a, wgrad_b, active_a, active_b, grad_ref = refs[6:]
    grad_ref[...] = hidden_quarter(norm_ref, gmlp_ref, up_a[...], early_a[...], wgrad_a, active_a)
    grad_ref[...] += hidden_quarter(norm_ref, gmlp_ref, up_b[...], early_b[...], wgrad_b, active_b)


def mlp_kernel(groups, last, *refs):
    info_ref, norm_ref, gmlp_ref, both_ref, grad_in = refs[:5]
    at = 5
    if last:
        middle_ref, og_ref, gain_ref, ascale_ref = refs[at : at + 4]
        at += 4
    wgrad_ref, active_ref, grad_ref = refs[at : at + 3]
    at += 3
    up = both_ref[:2].reshape(D, D)
    grad_active = dot(gmlp_ref[...], both_ref[2:].reshape(D, D), NT)
    grad_ref[...] = grad_in[...] + hidden_quarter(
        norm_ref, gmlp_ref, up, grad_active, wgrad_ref, active_ref
    )
    if last:
        gmid_ref, gattn_ref = refs[at:]
        for micro in range(2):
            rows = slice(micro * BLOCK, (micro + 1) * BLOCK)
            unit, inverse = unit_rows(middle_ref[rows, :])
            grad_mid = pad_rows(og_ref[micro].astype(F32))
            grad_mid = grad_mid + norm_back(grad_ref[rows, :], gain_ref[...], unit, inverse)
            gmid_ref[rows, :] = grad_mid
            keep = row_keep(info_ref, micro, groups)
            gattn_ref[rows, :] = (keep * ascale_ref[...] * grad_mid).astype(BF16)


def finish_block_kernel(groups, info_ref, *refs):
    middle_ref, grad_ref, attn_ref, gmid_ref, og_ref, scale_ref = refs[:6]
    actives, downs = refs[6:10], refs[10:14]
    block_ref, small_ref, mlp_ref = refs[14:]
    mlp = 0.0
    for active_ref, down_ref in zip(actives, downs):
        if len(down_ref.shape) == 3:
            down = down_ref[2:].reshape(D, D)
        else:
            down = down_ref[...]
        mlp += dot(active_ref[...], down)
    mlp_ref[...] = mlp
    small = [0.0, 0.0, 0.0]
    for micro in range(2):
        rows = slice(micro * BLOCK, (micro + 1) * BLOCK)
        keep = row_keep(info_ref, micro, groups)
        middle = middle_ref[rows, :]
        kept = keep * mlp_ref[rows, :]
        block_ref[micro] = drop_rows(middle + scale_ref[...] * kept).astype(BF16)
        small[0] += jnp.sum(kept * pad_rows(og_ref[micro].astype(F32)), axis=0, keepdims=True)
        unit, _ = unit_rows(middle)
        small[1] += jnp.sum(grad_ref[rows, :] * unit, axis=0, keepdims=True)
        small[2] += jnp.sum(keep * attn_ref[rows, :] * gmid_ref[rows, :], axis=0, keepdims=True)
    small_ref[...] = jnp.concatenate(small, axis=0)


def attend_back_kernel(groups, *refs):
    info_ref, w_ref, packed_ref, ctx_ref, gattn_ref, norm_ref = refs[:6]
    gpack_ref, low_ref, high_ref, gctx_ref = refs[6:]
    gctx_ref[...] = dot(gattn_ref[...], w_ref[512:, :], NT).astype(BF16)
    places = slots(info_ref, groups, 0)
    for pair in (places[:2], places[2:]):
        jobs = []
        for rows, live, fill in pair:
            t0, t1, t2, t3, t4 = (packed_ref[rows, 128 * i : 128 * i + 128] for i in range(5))
            g0, g1 = gctx_ref[rows, :128], gctx_ref[rows, 128:]
            t1r = turn(t1)
            t0s, t2s, t3s = turn(t0 * FACTOR), t2 * FACTOR, turn(t3 * FACTOR)
            keys = (low_half(t0s), low_half(t2s), low_half(t3s))
            values = (high_half(t1r), low_half(turn(t2)), high_half(turn(t4)))
            scores = [dot(key, query, NT) for key, query in zip(keys, (t0, t1r, t3))]
            gps = [dot(value, grad, NT) for value, grad in zip(values, (g0, g1, g1))]
            tiles = (t0s, low_half(t1r * FACTOR), high_half(turn(t2s)), t3s, turn(g0), turn(g1))
            jobs.append((rows, live, fill, scores, gps, tiles))
        done = []
        for rows, live, fill, scores, gps, tiles in jobs:
            probs = [softmax_columns(score, live, fill) for score in scores]
            dots = [jnp.sum(prob * gp, axis=0, keepdims=True) for prob, gp in zip(probs, gps)]
            gs = [(prob * (gp - row)).astype(BF16) for prob, gp, row in zip(probs, gps, dots)]
            done.append((rows, [prob.astype(BF16) for prob in probs], gs, tiles))
        for rows, probs, gs, (t0s, query_b, key_b, t3s, g0r, g1r) in done:
            columns = (
                dot(gs[0], low_half(t0s), TN) + dot(gs[0], high_half(t0s)),
                dot(probs[0], low_half(g0r)) + dot(gs[1], key_b, TN),
                dot(gs[1], query_b) + dot(probs[1], high_half(g1r)),
                dot(gs[2], low_half(t3s), TN) + dot(gs[2], high_half(t3s)),
                dot(probs[2], low_half(g1r)),
            )
            for i, column in enumerate(columns):
                gpack_ref[rows, 128 * i : 128 * i + 128] = column.astype(BF16)
    half = D // 2
    for top, out in enumerate((low_ref, high_ref)):
        columns = slice(top * half, (top + 1) * half)
        norm = norm_ref[:, columns]
        out[0, :, :512] = dot(norm, gpack_ref[:, :512], TN).astype(BF16)
        tail = dot(gattn_ref[:, columns], ctx_ref[...], TN)
        out[0, :, 512:640] = (dot(norm, gpack_ref[:, 512:640], TN) + tail[:, :128]).astype(BF16)
        out[0, :, 640:] = tail[:, 128:].astype(BF16)


def input_back_kernel(info_ref, *refs):
    gpacks, weights = refs[:4], refs[4:8]
    tokens_ref, gmid_ref, gain_ref, three_ref, igrad_ref, small_ref, sum_ref = refs[8:]
    sum_ref[...] = dot(gpacks[0][...], weights[0][:HEAD_COLS, :])
    for gpack_ref, w_ref in zip(gpacks[1:], weights[1:]):
        sum_ref[...] += dot(gpack_ref[...], w_ref[:HEAD_COLS, :])
    small = 0.0
    for micro in range(2):
        rows = slice(micro * BLOCK, (micro + 1) * BLOCK)
        unit, inverse = unit_rows(pad_rows(tokens_ref[micro].astype(F32)))
        own = sum_ref[rows, :]
        small += jnp.sum(own * unit, axis=0, keepdims=True)
        back_rows = gmid_ref[rows, :] + norm_back(own, gain_ref[...], unit, inverse)
        igrad_ref[micro] = drop_rows(back_rows).astype(BF16)
    small_ref[...] = jnp.concatenate([three_ref[...], small], axis=0)


def add(left, right):
    return left + right


THIRDS = (slice(0, 256), slice(256, 512), slice(512, 768))


def sum_refs(refs):
    total = refs[0][...]
    for ref in refs[1:]:
        total = total + ref[...]
    return total


def halve_first(sources, count, info_ref, gives, keeps, base):
    x, z = info_ref[6], info_ref[7]
    give_y, give_x, give_z = gives
    keep_a, keep_b, keep_c = keeps

    def pair(low, third, i, high, s):
        return add(sources(low, third, i, high, s), sources(low + 1, third, i, high, s))

    for i in range(count):
        for s in range(8):
            give_y[base + 8 * i + s] = pair(2, 0, i, s // 4, s % 4)
            keep_a[8 * i + s] = pair(0, 0, i, s // 4, s % 4)
        for side in range(2):
            for s in range(4):
                at = 8 * i + 4 * side + s
                low = 2 * (s % 2)
                keep_b[at] = pair(2 * side, 1, i, s // 2, low + x)
                give_x[base + at] = pair(2 * side, 1, i, s // 2, low + 1 - x)
                low = s % 2
                keep_c[at] = pair(2 * side, 2, i, s // 2, low + 2 * z)
                give_z[base + at] = pair(2 * side, 2, i, s // 2, low + 2 * (1 - z))


def halve_second(olds, gots, count, info_ref, gives, keeps):
    x, z = info_ref[6], info_ref[7]
    give_x, give_z, give_y = gives
    keep_a, keep_b, keep_c = keeps
    old_a, old_b, old_c = olds
    got_a, got_b, got_c = gots
    for i in range(count):
        for s in range(4):
            at, low = 4 * i + s, 8 * i + 2 * s
            keep_a[at] = add(old_a[low + x], got_a[low + x])
            give_x[at] = add(old_a[low + 1 - x], got_a[low + 1 - x])
            keep_c[at] = add(old_c[8 * i + s], got_c[8 * i + s])
            give_y[at] = add(old_c[8 * i + 4 + s], got_c[8 * i + 4 + s])
        for side in range(2):
            for s in range(2):
                at, low = 4 * i + 2 * side + s, 8 * i + 4 * side + 2 * s
                keep_b[at] = add(old_b[low + z], got_b[low + z])
                give_z[at] = add(old_b[low + 1 - z], got_b[low + 1 - z])


def halve_third(olds, gots, skip, count, info_ref, gives, keeps):
    x, z = info_ref[6], info_ref[7]
    give_z, give_y, give_x = gives
    keep_a, keep_b, keep_c = keeps
    old_a, old_b, old_c = olds
    got_a, got_b, got_c = gots
    for i in range(count):
        for s in range(2):
            at, low = 2 * i + s, 4 * i + 2 * s
            keep_a[at] = add(old_a[low + z], got_a[skip + low + z])
            give_z[at] = add(old_a[low + 1 - z], got_a[skip + low + 1 - z])
            low = 4 * i + s
            keep_b[at] = add(old_b[low], got_b[skip + low])
            give_y[at] = add(old_b[low + 2], got_b[skip + low + 2])
            low = 4 * i + 2 * s
            keep_c[at] = add(old_c[low + x], got_c[skip + low + x])
            give_x[at] = add(old_c[low + 1 - x], got_c[skip + low + 1 - x])


def halve_fourth(olds, gots, count, info_ref, give, keep):
    z = info_ref[8]
    for i in range(count):
        for old, got, third in zip(olds, gots, THIRDS):
            keep[i, :, third] = add(old[2 * i + z], got[2 * i + z])
            give[i, :, third] = add(old[2 * i + 1 - z], got[2 * i + 1 - z])


class Shifted:
    def __init__(self, ref, offset):
        self.ref = ref
        self.offset = offset

    def __getitem__(self, at):
        return self.ref[self.offset + at]

    def __setitem__(self, at, value):
        self.ref[self.offset + at] = value


def shift(refs, offset):
    return tuple(Shifted(ref, offset) for ref in refs)


def add_kernel(info_ref, left, right, out_ref):
    out_ref[...] = left[...] + right[...]


def merge_zero_kernel(info_ref, *refs):
    parts, gives, keeps = refs[:4], refs[4:7], refs[7:10]

    def source(part, third, i, high, s):
        return parts[part][i, 4 * high + s, :, THIRDS[third]]

    halve_first(source, 2, info_ref, gives, keeps, 0)


def merge_one_kernel(info_ref, *refs):
    olds, gots, parts = refs[:3], refs[3:6], refs[6:14]
    give_y, give_x, give_z = refs[14:17]
    keeps_m, keeps_a = refs[17:20], refs[20:23]

    def source(part, third, i, high, s):
        return parts[2 * part + high][i, s, :, THIRDS[third]]

    halve_second(olds, gots, 2, info_ref, (give_x, give_z, give_y), keeps_m)
    halve_first(source, 1, info_ref, (give_y, give_x, give_z), keeps_a, 8)


def merge_two_kernel(info_ref, *refs):
    olds_m, olds_a = refs[:3], refs[3:6]
    got_y, got_x, got_z = refs[6:9]
    smalls = refs[9:11]
    give_y, give_x, give_z = refs[11:14]
    keeps_m, keeps_a, small_ref = refs[14:17], refs[17:20], refs[20]
    halve_third(
        olds_m, (got_x, got_z, got_y), 0, 2, info_ref, (give_z, give_y, give_x), keeps_m
    )
    halve_second(
        olds_a,
        shift((got_y, got_x, got_z), 8),
        1,
        info_ref,
        shift((give_x, give_z, give_y), 4),
        keeps_a,
    )
    small_ref[...] = sum_refs(smalls)


def merge_three_kernel(info_ref, *refs):
    olds_m, olds_a = refs[:3], refs[3:6]
    got_y, got_x, got_z = refs[6:9]
    smalls = refs[9:11]
    give_y, give_x, give_z, give_far = refs[11:15]
    keep_m, keeps_a, small_ref = refs[15], refs[16:19], refs[19]
    halve_fourth(olds_m, (got_z, got_y, got_x), 2, info_ref, give_far, keep_m)
    halve_third(
        olds_a, (got_x, got_z, got_y), 4, 1, info_ref, (give_z, give_y, give_x), keeps_a
    )
    small_ref[...] = sum_refs(smalls)


def merge_four_kernel(info_ref, *refs):
    olds_a = refs[:3]
    got_y, got_x, got_z = refs[3:6]
    give_far, keep_a, small_ref = refs[8:]
    halve_fourth(olds_a, (got_z, got_y, got_x), 1, info_ref, give_far, keep_a)
    small_ref[...] = sum_refs(refs[6:8])


def finish_mlp_kernel(info_ref, old_m, got_far, up_ref, down_ref):
    up_ref[...] = old_m[0].astype(F32) + got_far[0].astype(F32)
    down_ref[...] = old_m[1].astype(F32) + got_far[1].astype(F32)


def merge_last_kernel(info_ref, *refs):
    old, got, qkv_ref, proj_ref = refs[:2] + refs[4:6]
    small = sum_refs(refs[2:4])
    total = old[0].astype(F32) + got[0].astype(F32)
    split = qkv_ref.shape[1]
    qkv_ref[...] = total[:, :split]
    proj_ref[...] = total[:, 512:].T[split - 512 :]
    width = small.shape[1] // 8
    place = info_ref[5] + 4 * info_ref[8]
    for d in range(8):

        @pl.when(place == d)
        def _():
            for i, ref in enumerate(refs[6:]):
                ref[...] = small[i : i + 1, d * width : (d + 1) * width]


VMEM = pl.BlockSpec(memory_space=pltpu.VMEM)
HBM = pl.BlockSpec(memory_space=pltpu.HBM)
SMEM = pl.BlockSpec(memory_space=pltpu.SMEM)


def shape(dims, dtype):
    return jax.ShapeDtypeStruct(dims, dtype)


class Order:
    def __init__(self, info):
        self.info = info

    def call(self, kernel, args, outs, scratch=(), limit=9, spaces=None):
        specs = [SMEM] + [VMEM] * len(args)
        out_specs = [VMEM] * len(outs)
        if spaces is not None:
            specs[1:] = spaces[0]
            out_specs = spaces[1]
        out = pl.pallas_call(
            kernel,
            in_specs=specs,
            out_specs=out_specs,
            out_shape=outs,
            scratch_shapes=list(scratch),
            compiler_params=pltpu.CompilerParams(vmem_limit_bytes=limit * MIB),
            cost_estimate=pl.CostEstimate(flops=1000, bytes_accessed=1000, transcendentals=0),
        )(self.info, *args)
        self.info = after(self.info, out[0])
        return out


def swap(value, axis, bit):
    size = lax.axis_size(axis)
    return lax.ppermute(value, axis, [(i, i ^ bit) for i in range(size)])


def after(value, *others):
    return lax.optimization_barrier((value,) + others)[0]


def second_hop(own):
    return swap(own, "dp", 1), swap(own, "dp", 2)


def third_hop(one, two):
    half = one.shape[0] // 2
    return swap(two[:half], "dp", 1), swap(one[half:], "dp", 2)


def assemble(order, pieces):
    return order.call(assemble_kernel, pieces, (shape((4,) + pieces[0].shape, BF16),))[0]


def swap_core(value):
    return swap(value, "tensor", 1)


def swap_y(value):
    return swap(value, "tensor", 2)


def swap_x(value):
    return swap(value, "dp", 1)


def swap_z(value):
    return swap(value, "dp", 2)


def swap_far(value):
    return swap(value, "dp", 4)


def dp_halve(value, bit):
    slices = value.shape[0]
    mine = (lax.axis_index("dp") // bit) % 2
    paired = value.reshape((slices // 2, 2) + value.shape[1:])
    keep = lax.dynamic_index_in_dim(paired, mine, 1, keepdims=False)
    give = lax.dynamic_index_in_dim(paired, 1 - mine, 1, keepdims=False)
    got = swap(give.astype(BF16), "dp", bit)
    return keep.astype(F32) + got.astype(F32)


def scatter_sum(parts, first_dp):
    shards = lax.axis_size("dp")
    zero = parts[0].astype(F32) + swap(parts[1], "tensor", 1).astype(F32)
    two = parts[2].astype(F32) + swap(parts[3], "tensor", 1).astype(F32)
    form = (shards, D // shards, parts[0].shape[1])
    zero = zero.reshape(form)
    two = two.reshape(form)
    bit = 1
    if first_dp:
        zero = dp_halve(zero, bit)
        two = dp_halve(two, bit)
        bit = 2
    zero = zero + swap(two.astype(BF16), "tensor", 2).astype(F32)
    while bit < shards:
        zero = dp_halve(zero, bit)
        bit = bit * 2
    return zero[0]


def body(
    tokens,
    out_grad,
    global_count,
    local_count,
    attn_gain,
    qkv_weight,
    proj_weight,
    attn_scale,
    mlp_gain,
    up_weight,
    down_weight,
    mlp_scale,
):
    groups = lax.axis_size("tensor")
    shards = lax.axis_size("dp")
    rows = 2 * BLOCK
    place = lax.axis_index("dp").astype(jnp.int32)
    member = lax.axis_index("tensor").astype(jnp.int32)
    where = jnp.stack([place % 4, place % 2, (place // 2) % 2, (place // 4) % 2])
    info = jnp.concatenate([member[None], global_count[0], local_count[0], where])
    row = lambda vector: vector.reshape(1, D)

    act = shape((rows, D), BF16)
    acc = shape((rows, D), F32)
    packed = shape((rows, HEAD_COLS), BF16)
    ctx = shape((rows, 256), BF16)
    unit_flops = 2 * rows * D * D

    def bind(kernel, *flags):
        def run(*refs):
            return kernel(groups, *flags, *refs)

        return run

    mixed, block_a, block_b = pl.pallas_call(
        start_kernel,
        in_specs=[HBM] * 4,
        out_specs=[VMEM] * 3,
        out_shape=(shape((D, D), BF16), shape((D // 4, D), BF16), shape((D // 2, D), BF16)),
        scratch_shapes=[pltpu.SemaphoreType.DMA((5,))],
        compiler_params=pltpu.CompilerParams(vmem_limit_bytes=60 * MIB),
    )(qkv_weight.T, proj_weight, up_weight, down_weight)
    order = Order(after(info, block_a))
    attn_gain, mlp_scale = after((attn_gain, mlp_scale), block_a)
    own_a = swap(block_a, "tensor", 2)
    wa = [mixed, swap(mixed, "tensor", 1)]
    up_one = swap_core(after(up_weight, block_a))
    norm, gmlp = order.call(
        bind(prepare_kernel),
        (tokens, out_grad, row(attn_gain), row(mlp_scale)),
        (act, act),
    )
    packs, ctxs = {}, {}

    def attend(r, part):
        last = r == 3
        pieced = r > 1
        args = (norm,) + (wa[r] if pieced else (wa[r],)) + part
        outs = (packed, ctx, acc)
        if pieced:
            outs += (shape((4, D // 4, D), BF16),)
        if last:
            args += (tokens, row(attn_scale), row(mlp_gain))
            outs += (acc, act)
        got = order.call(bind(attend_kernel, r == 0, last), args, outs)
        packs[r], ctxs[r] = got[:2]
        if pieced:
            wa[r] = got[3].reshape(D, D)
        return (got[2],) + tuple(got[4:])

    part = attend(0, ())
    own_a = after(own_a, part[0], wa[1], up_one)
    one_a, two_a = second_hop(own_a)
    core_a = (swap_core(own_a),)
    own_b = swap(after(block_b, own_a), "tensor", 2)
    down_one = swap_core(after(down_weight, own_a))
    part = attend(1, after(part, core_a[0], down_one))
    one_a, two_a = after((one_a, two_a), part[0])
    three_a = third_hop(one_a, two_a)
    core_a += (swap_core(one_a), swap_core(two_a))
    square = shape((D, D), BF16)
    up_zero, down_zero, up_one, block_c, early_zero, early_one = order.call(
        early_kernel,
        (gmlp, down_one, up_weight, down_weight, up_one),
        (square, square, square, shape((D // 2, D), BF16), acc, acc),
        scratch=[pltpu.SemaphoreType.DMA((3,))],
        spaces=([VMEM] * 2 + [HBM] * 3, [VMEM] * 6),
    )
    three_b = swap(block_c, "tensor", 2)
    own_b = after(own_b, early_zero, core_a[1], core_a[2], *three_a)
    one_b, two_b = second_hop(own_b)
    wa.append((own_a, one_a, two_a) + three_a)
    wa.append(core_a + tuple(swap_core(piece) for piece in three_a))
    part = attend(2, part)
    attn_out, middle, norm_two = attend(3, part)

    wgrads, actives = {}, {}

    def mlp(r, weights, carried, extra=(), outs=()):
        got = order.call(
            bind(mlp_kernel, r == 3),
            (norm_two, gmlp) + weights + carried + extra,
            (shape((2, D, D), BF16), act, acc) + outs,
        )
        wgrads[r], actives[r] = got[:2]
        return tuple(got[2:])

    two = shape((2, D, D), BF16)
    wgrads[0], wgrads[1], actives[0], actives[1], pair_sum = order.call(
        bind(mlp_pair_kernel),
        (norm_two, gmlp, up_zero, early_zero, up_one, early_one),
        (two, two, act, act, acc),
        limit=11,
    )
    grad_sum = (pair_sum,)
    both_two = assemble(order, (own_b, one_b, two_b, three_b))
    both_three = swap_core(both_two)
    grad_sum = mlp(2, (both_two,), grad_sum)
    got_one = swap_core(after(wgrads[1], grad_sum[0]))
    extra = (middle, out_grad, row(mlp_gain), row(attn_scale))
    grad_sum, grad_mid, gattn = mlp(3, (both_three,), grad_sum, extra, (acc, act))
    got_three = swap_core(wgrads[3])

    def finish_block():
        return order.call(
            bind(finish_block_kernel),
            (middle, grad_sum, attn_out, grad_mid, out_grad, row(mlp_scale))
            + tuple(actives[r] for r in range(4))
            + (down_zero, down_one, both_two, both_three),
            (shape(tokens.shape, BF16), shape((3, D), F32)),
            scratch=[pltpu.VMEM((rows, D), F32)],
            limit=9,
        )

    agrads, gpacks = {}, {}
    half = shape((1, D // 2, D), BF16)

    def back(r):
        out = order.call(
            bind(attend_back_kernel),
            (wa[r], packs[r], ctxs[r], gattn, norm),
            (packed, half, half),
            scratch=[pltpu.VMEM((rows, 256), BF16)],
        )
        gpacks[r] = out[0]
        agrads[r] = tuple(out[1:])

    def input_back():
        return order.call(
            input_back_kernel,
            tuple(gpacks[r] for r in range(4)) + tuple(wa) + (tokens, grad_mid, row(attn_gain), small),
            (shape(tokens.shape, BF16), shape((4, D), F32)),
            scratch=[pltpu.VMEM((rows, D), F32)],
        )

    width = D // shards
    split = qkv_weight.shape[1]
    back(1)
    if shards == 8:
        view = lambda a: a.reshape((a.shape[0], a.shape[1] // width, width, D))
        swap_pair = lambda values: tuple(swap_core(value) for value in values)
        tiny = shape((4, D), F32)
        blocks = lambda count: shape((count, width, 256), BF16)
        whole = lambda count: shape((count, width, D), BF16)
        args = tuple(view(a) for a in (wgrads[0], got_one, wgrads[2], got_three))
        out = order.call(merge_zero_kernel, args, (blocks(16),) * 6)
        keeps_m = tuple(out[3:6])
        got_m = (swap_y(out[0]), swap_x(out[1]), swap_z(out[2]))
        got_one = swap_pair(agrads[1])
        back(3)
        got_three = swap_pair(agrads[3])
        back(0)
        back(2)
        args = tuple(view(a) for a in agrads[0] + got_one + agrads[2] + got_three)
        out = order.call(
            merge_one_kernel, keeps_m + got_m + args, (blocks(16),) * 3 + (blocks(8),) * 6
        )
        keeps = tuple(out[3:9])
        got = (swap_y(out[0]), swap_x(out[1]), swap_z(out[2]))
        block_out, small = finish_block()
        input_grad, small = input_back()
        small = order.call(add_kernel, (small, swap(small, "tensor", 1)), (tiny,))[0]
        smalls = (small, swap_y(small))
        out = order.call(
            merge_two_kernel, keeps + got + smalls, (blocks(8),) * 3 + (blocks(4),) * 6 + (tiny,)
        )
        keeps = tuple(out[3:9])
        got = (swap_y(out[0]), swap_x(out[1]), swap_z(out[2]))
        smalls = (out[9], swap_x(out[9]))
        out = order.call(
            merge_three_kernel,
            keeps + got + smalls,
            (blocks(2),) * 3 + (whole(2), whole(2)) + (blocks(2),) * 3 + (tiny,),
        )
        keeps = tuple(out[4:8])
        got = (swap_y(out[0]), swap_x(out[1]), swap_z(out[2]), swap_far(out[3]))
        smalls = (out[8], swap_z(out[8]))
        give, keep, small = order.call(
            merge_four_kernel, keeps[1:] + got[:3] + smalls, (whole(1), whole(1), tiny)
        )
        up_grad, down_grad = order.call(
            finish_mlp_kernel, (keeps[0], got[3]), (shape((width, D), F32), shape((width, D), F32))
        )
        down_grad = down_grad.T
        out = order.call(
            merge_last_kernel,
            (keep, swap_far(give), small, swap_far(small)),
            (shape((width, split), F32), shape((D - split, width), F32)) + (shape((1, width), F32),) * 4,
        )
        smalls = [value.reshape(width) for value in out[2:]]
        qkv_grad, proj_grad = out[:2]
    else:
        for r in (3, 0, 2):
            back(r)
        block_out, small = finish_block()
        input_grad, small = input_back()
        up_grad = scatter_sum([wgrads[r][0] for r in range(4)], False)
        down_grad = scatter_sum([wgrads[r][1] for r in range(4)], True).T
        mixed_grad = scatter_sum([jnp.concatenate(agrads[r], axis=1)[0] for r in range(4)], False)
        qkv_grad = mixed_grad[:, :split]
        proj_grad = mixed_grad[:, split:].T
        small = lax.psum(small, ("dp", "tensor"))
        small = lax.dynamic_slice_in_dim(small, place * width, width, axis=1)
        smalls = [small[i] for i in range(4)]
    return (
        block_out,
        input_grad,
        smalls[3],
        qkv_grad,
        proj_grad,
        smalls[2],
        smalls[1],
        up_grad,
        down_grad,
        smalls[0],
    )


def solution(mesh):
    in_specs = (
        P(None, ("dp", "tensor"), None),
        P(None, ("dp", "tensor"), None),
        P("dp", None),
        P("dp", None),
        P(),
        P(None, "tensor"),
        P("tensor", None),
        P(),
        P(),
        P(None, "tensor"),
        P("tensor", None),
        P(),
    )
    out_specs = (
        P(None, ("dp", "tensor"), None),
        P(None, ("dp", "tensor"), None),
        P("dp"),
        P("dp", "tensor"),
        P("tensor", "dp"),
        P("dp"),
        P("dp"),
        P("dp", "tensor"),
        P("tensor", "dp"),
        P("dp"),
    )
    return jax.shard_map(body, mesh=mesh, in_specs=in_specs, out_specs=out_specs, check_vma=False)
```

```python
import math

import jax
import jax.numpy as jnp
from jax import lax
from jax.experimental import pallas as pl
from jax.experimental.pallas import tpu as pltpu
from jax.sharding import PartitionSpec as P

D = 768
HD = 64
GLEN = 197
GPAD = 200
LLEN = 37
LPAD = 40
SLOT = GPAD + 2 * LPAD
GROW = 208
LROW = 2 * LPAD
BLOCK = GROW + LROW
FACTOR = HD ** (-0.5)
HEAD_COLS = 640
F32 = jnp.float32
BF16 = jnp.bfloat16
NN = (((1,), (0,)), ((), ()))
NT = (((1,), (1,)), ((), ()))
TN = (((0,), (0,)), ((), ()))
MIB = 1024 * 1024


def dot(left, right, dims=NN):
    return lax.dot_general(left, right, dims, preferred_element_type=F32)


def pad_rows(values):
    return jnp.concatenate(
        [values[:GPAD], jnp.zeros((GROW - GPAD, values.shape[1]), values.dtype), values[GPAD:]], axis=0
    )


def drop_rows(values):
    return jnp.concatenate([values[:GPAD], values[GROW:]], axis=0)


def row_keep(info_ref, micro, groups):
    member = info_ref[0]
    row = lax.broadcasted_iota(jnp.int32, (BLOCK, 1), 0)
    live = jnp.where(member < info_ref[1 + micro], GLEN, 0)
    first = jnp.where(member < info_ref[3 + micro], LLEN, 0)
    second = jnp.where(member + groups < info_ref[3 + micro], LLEN, 0)
    keep = (
        (row < live)
        | ((row >= GROW) & (row < GROW + first))
        | ((row >= GROW + LPAD) & (row < GROW + LPAD + second))
    )
    return jnp.where(keep, 1.0, 0.0).astype(F32)


def global_mask(info_ref, micro, axis):
    shape = (1, GROW) if axis == 1 else (GROW, 1)
    key = lax.broadcasted_iota(jnp.int32, shape, axis)
    live = jnp.where(info_ref[0] < info_ref[1 + micro], GLEN, 0)
    fill = jnp.where(key < GPAD, -30000.0, -3e38).astype(F32)
    return key < live, fill


def local_mask(info_ref, micro, groups, axis):
    key = lax.broadcasted_iota(jnp.int32, (LROW, LROW), axis)
    query = lax.broadcasted_iota(jnp.int32, (LROW, LROW), 1 - axis)
    member = info_ref[0]
    first = jnp.where(member < info_ref[3 + micro], LLEN, 0)
    second = jnp.where(member + groups < info_ref[3 + micro], LLEN, 0)
    same = (key < LPAD) == (query < LPAD)
    alive = (key < first) | ((key >= LPAD) & (key < LPAD + second))
    fill = jnp.where(same, -30000.0, -3e38).astype(F32)
    return same & alive, fill


def slots(info_ref, groups, axis):
    places = []
    for micro in range(2):
        start = micro * BLOCK
        places.append((slice(start, start + GROW),) + global_mask(info_ref, micro, axis))
        places.append((slice(start + GROW, start + BLOCK),) + local_mask(info_ref, micro, groups, axis))
    return places


def unit_rows(values):
    center = values - jnp.mean(values, axis=-1, keepdims=True)
    inverse = lax.rsqrt(jnp.mean(center * center, axis=-1, keepdims=True) + 1e-06)
    return center * inverse, inverse


def norm_back(grad_norm, gain, unit, inverse):
    scaled = grad_norm * gain
    centered = scaled - jnp.mean(scaled, axis=-1, keepdims=True)
    return inverse * (centered - unit * jnp.mean(scaled * unit, axis=-1, keepdims=True))


def low_half(tile):
    lane = lax.broadcasted_iota(jnp.int32, tile.shape, 1)
    return jnp.where(lane < HD, tile, jnp.zeros_like(tile))


def high_half(tile):
    lane = lax.broadcasted_iota(jnp.int32, tile.shape, 1)
    return jnp.where(lane < HD, jnp.zeros_like(tile), tile)


def turn(tile):
    return pltpu.roll(tile.astype(F32), HD, 1).astype(tile.dtype)


def softmax_rows(scores, live, fill):
    scores = jnp.where(live, scores, fill)
    raised = jnp.exp(scores - jnp.max(scores, axis=1, keepdims=True))
    return (raised * (1.0 / jnp.sum(raised, axis=1, keepdims=True))).astype(BF16)


def softmax_columns(scores, live, fill):
    scores = jnp.where(live, scores, fill)
    raised = jnp.exp(scores - jnp.max(scores, axis=0, keepdims=True))
    return raised * (1.0 / jnp.sum(raised, axis=0, keepdims=True))


def start_kernel(qkv_hbm, proj_hbm, up_hbm, down_hbm, mixed_ref, block_ref, block_b, sems):
    place = lax.rem(lax.axis_index("dp"), 4)
    quarter = D // 4
    half = D // 2
    blocks = [qkv_hbm.at[pl.ds(i * quarter, quarter)] for i in range(3)] + [proj_hbm]
    for i, block in enumerate(blocks):
        pltpu.make_async_copy(block, mixed_ref.at[pl.ds(i * quarter, quarter)], sems.at[i]).start()
    chosen = pl.ds(pl.multiple_of(lax.rem(place, 2) * half, half), half)

    @pl.when(place < 2)
    def _():
        pltpu.make_async_copy(up_hbm.at[chosen], block_b, sems.at[4]).start()

    @pl.when(place >= 2)
    def _():
        pltpu.make_async_copy(down_hbm.at[chosen], block_b, sems.at[4]).start()

    for i, block in enumerate(blocks):
        pltpu.make_async_copy(block, mixed_ref.at[pl.ds(i * quarter, quarter)], sems.at[i]).wait()
    block_ref[...] = mixed_ref[pl.ds(pl.multiple_of(place * quarter, quarter), quarter), :]
    pltpu.make_async_copy(up_hbm.at[chosen], block_b, sems.at[4]).wait()


def prepare_kernel(
    groups, info_ref, tokens_ref, grad_ref, gain_ref, scale_ref, norm_ref, gmlp_ref
):
    for micro in range(2):
        rows = slice(micro * BLOCK, (micro + 1) * BLOCK)
        values = pad_rows(tokens_ref[micro].astype(F32))
        unit, _ = unit_rows(values)
        norm_ref[rows, :] = (unit * gain_ref[...]).astype(BF16)
        keep = row_keep(info_ref, micro, groups)
        grad = pad_rows(grad_ref[micro].astype(F32))
        gmlp_ref[rows, :] = (keep * scale_ref[...] * grad).astype(BF16)


def attend_kernel(groups, first, last, *refs):
    info_ref, norm_ref = refs[:2]
    at = 2
    pieced = not first and refs[at].shape[0] < D
    if pieced:
        pieces = refs[at : at + 5]
        at += 5
    else:
        w_ref = refs[at]
        at += 1
    if not first:
        acc_ref = refs[at]
        at += 1
    if last:
        tokens_ref, scale_ref, gain_ref = refs[at : at + 3]
        at += 3
    packed_ref, ctx_ref, out_ref = refs[at : at + 3]
    at += 3
    if pieced:
        put_together(info_ref, pieces, refs[at])
        weights = refs[at][...].reshape(D, D)
        at += 1
    else:
        weights = w_ref[...]
    if last:
        middle_ref, norm_two_ref = refs[at : at + 2]
    packed_ref[...] = dot(norm_ref[...], weights[:HEAD_COLS, :], NT).astype(BF16)
    jobs = []
    for rows, live, fill in slots(info_ref, groups, 1):
        t0, t1, t2, t3, t4 = (packed_ref[rows, 128 * i : 128 * i + 128] for i in range(5))
        queries = (low_half(t0 * FACTOR), high_half(t1 * FACTOR), low_half(t3 * FACTOR))
        t2r = turn(t2)
        keys = (turn(t0), t2r, turn(t3))
        scores = [dot(query, key, NT) for query, key in zip(queries, keys)]
        jobs.append((rows, live, fill, scores, (high_half(turn(t1)), low_half(t2r), high_half(turn(t4)))))
    done = []
    for rows, live, fill, scores, values in jobs:
        done.append((rows, [softmax_rows(score, live, fill) for score in scores], values))
    for rows, probs, values in done:
        ctx_ref[rows, :128] = dot(probs[0], values[0]).astype(BF16)
        ctx_ref[rows, 128:] = (dot(probs[1], values[1]) + dot(probs[2], values[2])).astype(BF16)
    out = dot(ctx_ref[...], weights[512:, :])
    if not first:
        out = out + acc_ref[...]
    out_ref[...] = out
    if last:
        for micro in range(2):
            rows = slice(micro * BLOCK, (micro + 1) * BLOCK)
            keep = row_keep(info_ref, micro, groups)
            middle = pad_rows(tokens_ref[micro].astype(F32)) + keep * scale_ref[...] * out_ref[rows, :]
            middle_ref[rows, :] = middle
            unit, _ = unit_rows(middle)
            norm_two_ref[rows, :] = (unit * gain_ref[...]).astype(BF16)


def put_together(info_ref, pieces, out_ref):
    place = info_ref[5]
    half = out_ref.shape[1] // 2
    out_ref[place] = pieces[0][...]
    out_ref[place ^ 1] = pieces[1][...]
    out_ref[place ^ 2] = pieces[2][...]
    if len(pieces) == 4:
        out_ref[place ^ 3] = pieces[3][...]
    else:
        out_ref[place ^ 3, :half] = pieces[3][...]
        out_ref[place ^ 3, half:] = pieces[4][...]


def assemble_kernel(info_ref, *refs):
    put_together(info_ref, refs[:-1], refs[-1])


def early_kernel(info_ref, *refs):
    gmlp_ref, down_one_ref, up_hbm, down_hbm, up_one_hbm = refs[:5]
    up_ref, down_ref, up_one_ref, block_ref, out_zero, out_one, sems = refs[5:]
    fetches = (
        pltpu.make_async_copy(down_hbm, down_ref, sems.at[0]),
        pltpu.make_async_copy(up_hbm, up_ref, sems.at[1]),
        pltpu.make_async_copy(up_one_hbm, up_one_ref, sems.at[2]),
    )
    for fetch in fetches:
        fetch.start()
    out_one[...] = dot(gmlp_ref[...], down_one_ref[...], NT)
    fetches[0].wait()
    out_zero[...] = dot(gmlp_ref[...], down_ref[...], NT)
    fetches[1].wait()
    place = info_ref[5] ^ 3
    half = D // 2
    chosen = pl.ds(pl.multiple_of((place % 2) * half, half), half)

    @pl.when(place < 2)
    def _():
        block_ref[...] = up_ref[chosen, :]

    @pl.when(place >= 2)
    def _():
        block_ref[...] = down_ref[chosen, :]

    fetches[2].wait()


def hidden_quarter(norm_ref, gmlp_ref, up, find_grad_active, wgrad_ref, active_ref, sums=None):
    hidden = dot(norm_ref[...], up)
    grad_active = find_grad_active()
    cdf = 0.5 + 0.5 * lax.erf(hidden * (0.5**0.5))
    active_ref[...] = (hidden * cdf).astype(BF16)
    slope = cdf + hidden * (jnp.exp(-0.5 * hidden * hidden) * (1.0 / math.sqrt(2.0 * math.pi)))
    grad_hidden = (grad_active * slope).astype(BF16)
    if sums is not None:
        grad_in, grad_ref = sums
        grad_ref[...] = grad_in[...] + dot(grad_hidden, up, NT)
    wgrad_ref[0] = dot(norm_ref[...], grad_hidden, TN).astype(BF16)
    wgrad_ref[1] = dot(gmlp_ref[...], active_ref[...], TN).astype(BF16)
    if sums is None:
        return dot(grad_hidden, up, NT)


def mlp_pair_kernel(groups, info_ref, *refs):
    norm_ref, gmlp_ref, up_a, early_a, up_b, early_b = refs[:6]
    wgrad_a, wgrad_b, active_a, active_b, grad_ref = refs[6:]
    grad_ref[...] = hidden_quarter(norm_ref, gmlp_ref, up_a[...], lambda: early_a[...], wgrad_a, active_a)
    grad_ref[...] += hidden_quarter(norm_ref, gmlp_ref, up_b[...], lambda: early_b[...], wgrad_b, active_b)


def mlp_kernel(groups, last, *refs):
    info_ref, norm_ref, gmlp_ref, both_ref, grad_in = refs[:5]
    at = 5
    if last:
        middle_ref, og_ref, gain_ref, ascale_ref = refs[at : at + 4]
        at += 4
    wgrad_ref, active_ref, grad_ref = refs[at : at + 3]
    at += 3
    up = both_ref[:2].reshape(D, D)
    find_grad_active = lambda: dot(gmlp_ref[...], both_ref[2:].reshape(D, D), NT)
    hidden_quarter(
        norm_ref, gmlp_ref, up, find_grad_active, wgrad_ref, active_ref, (grad_in, grad_ref)
    )
    if last:
        gmid_ref, gattn_ref = refs[at:]
        for micro in range(2):
            rows = slice(micro * BLOCK, (micro + 1) * BLOCK)
            unit, inverse = unit_rows(middle_ref[rows, :])
            grad_mid = pad_rows(og_ref[micro].astype(F32))
            grad_mid = grad_mid + norm_back(grad_ref[rows, :], gain_ref[...], unit, inverse)
            gmid_ref[rows, :] = grad_mid
            keep = row_keep(info_ref, micro, groups)
            gattn_ref[rows, :] = (keep * ascale_ref[...] * grad_mid).astype(BF16)


def finish_block_kernel(groups, info_ref, *refs):
    middle_ref, grad_ref, attn_ref, gmid_ref, og_ref, scale_ref = refs[:6]
    actives, downs = refs[6:10], refs[10:14]
    block_ref, small_ref, mlp_ref = refs[14:]
    mlp = 0.0
    for active_ref, down_ref in zip(actives, downs):
        if len(down_ref.shape) == 3:
            down = down_ref[2:].reshape(D, D)
        else:
            down = down_ref[...]
        mlp += dot(active_ref[...], down)
    mlp_ref[...] = mlp
    small = [0.0, 0.0, 0.0]
    for micro in range(2):
        rows = slice(micro * BLOCK, (micro + 1) * BLOCK)
        keep = row_keep(info_ref, micro, groups)
        middle = middle_ref[rows, :]
        kept = keep * mlp_ref[rows, :]
        block_ref[micro] = drop_rows(middle + scale_ref[...] * kept).astype(BF16)
        small[0] += jnp.sum(kept * pad_rows(og_ref[micro].astype(F32)), axis=0, keepdims=True)
        unit, _ = unit_rows(middle)
        small[1] += jnp.sum(grad_ref[rows, :] * unit, axis=0, keepdims=True)
        small[2] += jnp.sum(keep * attn_ref[rows, :] * gmid_ref[rows, :], axis=0, keepdims=True)
    small_ref[...] = jnp.concatenate(small, axis=0)


def attend_back_kernel(groups, *refs):
    info_ref, w_ref, packed_ref, ctx_ref, gattn_ref, norm_ref = refs[:6]
    gpack_ref, low_ref, high_ref, gctx_ref = refs[6:]
    gctx_ref[...] = dot(gattn_ref[...], w_ref[512:, :], NT).astype(BF16)
    places = slots(info_ref, groups, 0)
    for pair in (places[:2], places[2:]):
        jobs = []
        for rows, live, fill in pair:
            t0, t1, t2, t3, t4 = (packed_ref[rows, 128 * i : 128 * i + 128] for i in range(5))
            g0, g1 = gctx_ref[rows, :128], gctx_ref[rows, 128:]
            t1r = turn(t1)
            t0s, t2s, t3s = turn(t0 * FACTOR), t2 * FACTOR, turn(t3 * FACTOR)
            keys = (low_half(t0s), low_half(t2s), low_half(t3s))
            values = (high_half(t1r), low_half(turn(t2)), high_half(turn(t4)))
            scores = [dot(key, query, NT) for key, query in zip(keys, (t0, t1r, t3))]
            gps = [dot(value, grad, NT) for value, grad in zip(values, (g0, g1, g1))]
            tiles = (t0s, low_half(t1r * FACTOR), high_half(turn(t2s)), t3s, turn(g0), turn(g1))
            jobs.append((rows, live, fill, scores, gps, tiles))
        done = []
        for rows, live, fill, scores, gps, tiles in jobs:
            probs = [softmax_columns(score, live, fill) for score in scores]
            dots = [jnp.sum(prob * gp, axis=0, keepdims=True) for prob, gp in zip(probs, gps)]
            gs = [(prob * (gp - row)).astype(BF16) for prob, gp, row in zip(probs, gps, dots)]
            done.append((rows, [prob.astype(BF16) for prob in probs], gs, tiles))
        for rows, probs, gs, (t0s, query_b, key_b, t3s, g0r, g1r) in done:
            columns = (
                dot(gs[0], low_half(t0s), TN) + dot(gs[0], high_half(t0s)),
                dot(probs[0], low_half(g0r)) + dot(gs[1], key_b, TN),
                dot(gs[1], query_b) + dot(probs[1], high_half(g1r)),
                dot(gs[2], low_half(t3s), TN) + dot(gs[2], high_half(t3s)),
                dot(probs[2], low_half(g1r)),
            )
            for i, column in enumerate(columns):
                gpack_ref[rows, 128 * i : 128 * i + 128] = column.astype(BF16)
    half = D // 2
    for top, out in enumerate((low_ref, high_ref)):
        columns = slice(top * half, (top + 1) * half)
        norm = norm_ref[:, columns]
        out[0, :, :512] = dot(norm, gpack_ref[:, :512], TN).astype(BF16)
        tail = dot(gattn_ref[:, columns], ctx_ref[...], TN)
        out[0, :, 512:640] = (dot(norm, gpack_ref[:, 512:640], TN) + tail[:, :128]).astype(BF16)
        out[0, :, 640:] = tail[:, 128:].astype(BF16)


def input_back_kernel(info_ref, *refs):
    gpacks, weights = refs[:4], refs[4:8]
    tokens_ref, gmid_ref, gain_ref, three_ref, igrad_ref, small_ref, sum_ref = refs[8:]
    sum_ref[...] = dot(gpacks[0][...], weights[0][:HEAD_COLS, :])
    for gpack_ref, w_ref in zip(gpacks[1:], weights[1:]):
        sum_ref[...] += dot(gpack_ref[...], w_ref[:HEAD_COLS, :])
    small = 0.0
    for micro in range(2):
        rows = slice(micro * BLOCK, (micro + 1) * BLOCK)
        unit, inverse = unit_rows(pad_rows(tokens_ref[micro].astype(F32)))
        own = sum_ref[rows, :]
        small += jnp.sum(own * unit, axis=0, keepdims=True)
        back_rows = gmid_ref[rows, :] + norm_back(own, gain_ref[...], unit, inverse)
        igrad_ref[micro] = drop_rows(back_rows).astype(BF16)
    small_ref[...] = jnp.concatenate([three_ref[...], small], axis=0)


def add(left, right):
    return left + right


THIRDS = (slice(0, 256), slice(256, 512), slice(512, 768))


def sum_refs(refs):
    total = refs[0][...]
    for ref in refs[1:]:
        total = total + ref[...]
    return total


def halve_first(sources, count, info_ref, gives, keeps, base):
    x, z = info_ref[6], info_ref[7]
    give_y, give_x, give_z = gives
    keep_a, keep_b, keep_c = keeps

    def pair(low, third, i, high, s):
        return add(sources(low, third, i, high, s), sources(low + 1, third, i, high, s))

    for i in range(count):
        for s in range(8):
            give_y[base + 8 * i + s] = pair(2, 0, i, s // 4, s % 4)
            keep_a[8 * i + s] = pair(0, 0, i, s // 4, s % 4)
        for side in range(2):
            for s in range(4):
                at = 8 * i + 4 * side + s
                low = 2 * (s % 2)
                keep_b[at] = pair(2 * side, 1, i, s // 2, low + x)
                give_x[base + at] = pair(2 * side, 1, i, s // 2, low + 1 - x)
                low = s % 2
                keep_c[at] = pair(2 * side, 2, i, s // 2, low + 2 * z)
                give_z[base + at] = pair(2 * side, 2, i, s // 2, low + 2 * (1 - z))


def halve_second(olds, gots, count, info_ref, gives, keeps):
    x, z = info_ref[6], info_ref[7]
    give_x, give_z, give_y = gives
    keep_a, keep_b, keep_c = keeps
    old_a, old_b, old_c = olds
    got_a, got_b, got_c = gots
    for i in range(count):
        for s in range(4):
            at, low = 4 * i + s, 8 * i + 2 * s
            keep_a[at] = add(old_a[low + x], got_a[low + x])
            give_x[at] = add(old_a[low + 1 - x], got_a[low + 1 - x])
            keep_c[at] = add(old_c[8 * i + s], got_c[8 * i + s])
            give_y[at] = add(old_c[8 * i + 4 + s], got_c[8 * i + 4 + s])
        for side in range(2):
            for s in range(2):
                at, low = 4 * i + 2 * side + s, 8 * i + 4 * side + 2 * s
                keep_b[at] = add(old_b[low + z], got_b[low + z])
                give_z[at] = add(old_b[low + 1 - z], got_b[low + 1 - z])


def halve_third(olds, gots, skip, count, info_ref, gives, keeps):
    x, z = info_ref[6], info_ref[7]
    give_z, give_y, give_x = gives
    keep_a, keep_b, keep_c = keeps
    old_a, old_b, old_c = olds
    got_a, got_b, got_c = gots
    for i in range(count):
        for s in range(2):
            at, low = 2 * i + s, 4 * i + 2 * s
            keep_a[at] = add(old_a[low + z], got_a[skip + low + z])
            give_z[at] = add(old_a[low + 1 - z], got_a[skip + low + 1 - z])
            low = 4 * i + s
            keep_b[at] = add(old_b[low], got_b[skip + low])
            give_y[at] = add(old_b[low + 2], got_b[skip + low + 2])
            low = 4 * i + 2 * s
            keep_c[at] = add(old_c[low + x], got_c[skip + low + x])
            give_x[at] = add(old_c[low + 1 - x], got_c[skip + low + 1 - x])


def halve_fourth(olds, gots, count, info_ref, give, keep):
    z = info_ref[8]
    for i in range(count):
        for old, got, third in zip(olds, gots, THIRDS):
            keep[i, :, third] = add(old[2 * i + z], got[2 * i + z])
            give[i, :, third] = add(old[2 * i + 1 - z], got[2 * i + 1 - z])


class Shifted:
    def __init__(self, ref, offset):
        self.ref = ref
        self.offset = offset

    def __getitem__(self, at):
        return self.ref[self.offset + at]

    def __setitem__(self, at, value):
        self.ref[self.offset + at] = value


def shift(refs, offset):
    return tuple(Shifted(ref, offset) for ref in refs)


def add_kernel(info_ref, left, right, out_ref):
    out_ref[...] = left[...] + right[...]


def merge_zero_kernel(info_ref, *refs):
    parts, gives, keeps = refs[:4], refs[4:7], refs[7:10]

    def source(part, third, i, high, s):
        return parts[part][i, 4 * high + s, :, THIRDS[third]]

    halve_first(source, 2, info_ref, gives, keeps, 0)


def merge_one_kernel(info_ref, *refs):
    olds, gots, parts = refs[:3], refs[3:6], refs[6:14]
    give_y, give_x, give_z = refs[14:17]
    keeps_m, keeps_a = refs[17:20], refs[20:23]

    def source(part, third, i, high, s):
        return parts[2 * part + high][i, s, :, THIRDS[third]]

    halve_second(olds, gots, 2, info_ref, (give_x, give_z, give_y), keeps_m)
    halve_first(source, 1, info_ref, (give_y, give_x, give_z), keeps_a, 8)


def merge_two_kernel(info_ref, *refs):
    olds_m, olds_a = refs[:3], refs[3:6]
    got_y, got_x, got_z = refs[6:9]
    smalls = refs[9:11]
    give_y, give_x, give_z = refs[11:14]
    keeps_m, keeps_a, small_ref = refs[14:17], refs[17:20], refs[20]
    halve_third(
        olds_m, (got_x, got_z, got_y), 0, 2, info_ref, (give_z, give_y, give_x), keeps_m
    )
    halve_second(
        olds_a,
        shift((got_y, got_x, got_z), 8),
        1,
        info_ref,
        shift((give_x, give_z, give_y), 4),
        keeps_a,
    )
    small_ref[...] = sum_refs(smalls)


def merge_three_kernel(info_ref, *refs):
    olds_m, olds_a = refs[:3], refs[3:6]
    got_y, got_x, got_z = refs[6:9]
    smalls = refs[9:11]
    give_y, give_x, give_z, give_far = refs[11:15]
    keep_m, keeps_a, small_ref = refs[15], refs[16:19], refs[19]
    halve_fourth(olds_m, (got_z, got_y, got_x), 2, info_ref, give_far, keep_m)
    halve_third(
        olds_a, (got_x, got_z, got_y), 4, 1, info_ref, (give_z, give_y, give_x), keeps_a
    )
    small_ref[...] = sum_refs(smalls)


def merge_four_kernel(info_ref, *refs):
    olds_a = refs[:3]
    got_y, got_x, got_z = refs[3:6]
    give_far, keep_a, small_ref = refs[8:]
    halve_fourth(olds_a, (got_z, got_y, got_x), 1, info_ref, give_far, keep_a)
    small_ref[...] = sum_refs(refs[6:8])


def finish_mlp_kernel(info_ref, old_m, got_far, up_ref, down_ref):
    up_ref[...] = old_m[0].astype(F32) + got_far[0].astype(F32)
    down_ref[...] = old_m[1].astype(F32) + got_far[1].astype(F32)


def merge_last_kernel(info_ref, *refs):
    old, got, qkv_ref, proj_ref = refs[:2] + refs[4:6]
    small = sum_refs(refs[2:4])
    total = old[0].astype(F32) + got[0].astype(F32)
    split = qkv_ref.shape[1]
    qkv_ref[...] = total[:, :split]
    proj_ref[...] = total[:, 512:].T[split - 512 :]
    width = small.shape[1] // 8
    place = info_ref[5] + 4 * info_ref[8]
    for d in range(8):

        @pl.when(place == d)
        def _():
            for i, ref in enumerate(refs[6:]):
                ref[...] = small[i : i + 1, d * width : (d + 1) * width]


VMEM = pl.BlockSpec(memory_space=pltpu.VMEM)
HBM = pl.BlockSpec(memory_space=pltpu.HBM)
SMEM = pl.BlockSpec(memory_space=pltpu.SMEM)


def shape(dims, dtype):
    return jax.ShapeDtypeStruct(dims, dtype)


class Order:
    def __init__(self, info):
        self.info = info

    def call(self, kernel, args, outs, scratch=(), limit=9, spaces=None):
        specs = [SMEM] + [VMEM] * len(args)
        out_specs = [VMEM] * len(outs)
        if spaces is not None:
            specs[1:] = spaces[0]
            out_specs = spaces[1]
        out = pl.pallas_call(
            kernel,
            in_specs=specs,
            out_specs=out_specs,
            out_shape=outs,
            scratch_shapes=list(scratch),
            compiler_params=pltpu.CompilerParams(vmem_limit_bytes=limit * MIB),
            cost_estimate=pl.CostEstimate(flops=1000, bytes_accessed=1000, transcendentals=0),
        )(self.info, *args)
        self.info = after(self.info, out[0])
        return out


def swap(value, axis, bit):
    size = lax.axis_size(axis)
    return lax.ppermute(value, axis, [(i, i ^ bit) for i in range(size)])


def after(value, *others):
    return lax.optimization_barrier((value,) + others)[0]


def second_hop(own):
    return swap(own, "dp", 1), swap(own, "dp", 2)


def third_hop(one, two):
    half = one.shape[0] // 2
    return swap(two[:half], "dp", 1), swap(one[half:], "dp", 2)


def assemble(order, pieces):
    return order.call(assemble_kernel, pieces, (shape((4,) + pieces[0].shape, BF16),))[0]


def swap_core(value):
    return swap(value, "tensor", 1)


def swap_y(value):
    return swap(value, "tensor", 2)


def swap_x(value):
    return swap(value, "dp", 1)


def swap_z(value):
    return swap(value, "dp", 2)


def swap_far(value):
    return swap(value, "dp", 4)


def dp_halve(value, bit):
    slices = value.shape[0]
    mine = (lax.axis_index("dp") // bit) % 2
    paired = value.reshape((slices // 2, 2) + value.shape[1:])
    keep = lax.dynamic_index_in_dim(paired, mine, 1, keepdims=False)
    give = lax.dynamic_index_in_dim(paired, 1 - mine, 1, keepdims=False)
    got = swap(give.astype(BF16), "dp", bit)
    return keep.astype(F32) + got.astype(F32)


def scatter_sum(parts, first_dp):
    shards = lax.axis_size("dp")
    zero = parts[0].astype(F32) + swap(parts[1], "tensor", 1).astype(F32)
    two = parts[2].astype(F32) + swap(parts[3], "tensor", 1).astype(F32)
    form = (shards, D // shards, parts[0].shape[1])
    zero = zero.reshape(form)
    two = two.reshape(form)
    bit = 1
    if first_dp:
        zero = dp_halve(zero, bit)
        two = dp_halve(two, bit)
        bit = 2
    zero = zero + swap(two.astype(BF16), "tensor", 2).astype(F32)
    while bit < shards:
        zero = dp_halve(zero, bit)
        bit = bit * 2
    return zero[0]


def body(
    tokens,
    out_grad,
    global_count,
    local_count,
    attn_gain,
    qkv_weight,
    proj_weight,
    attn_scale,
    mlp_gain,
    up_weight,
    down_weight,
    mlp_scale,
):
    groups = lax.axis_size("tensor")
    shards = lax.axis_size("dp")
    rows = 2 * BLOCK
    place = lax.axis_index("dp").astype(jnp.int32)
    member = lax.axis_index("tensor").astype(jnp.int32)
    where = jnp.stack([place % 4, place % 2, (place // 2) % 2, (place // 4) % 2])
    info = jnp.concatenate([member[None], global_count[0], local_count[0], where])
    row = lambda vector: vector.reshape(1, D)

    act = shape((rows, D), BF16)
    acc = shape((rows, D), F32)
    packed = shape((rows, HEAD_COLS), BF16)
    ctx = shape((rows, 256), BF16)
    unit_flops = 2 * rows * D * D

    def bind(kernel, *flags):
        def run(*refs):
            return kernel(groups, *flags, *refs)

        return run

    mixed, block_a, block_b = pl.pallas_call(
        start_kernel,
        in_specs=[HBM] * 4,
        out_specs=[VMEM] * 3,
        out_shape=(shape((D, D), BF16), shape((D // 4, D), BF16), shape((D // 2, D), BF16)),
        scratch_shapes=[pltpu.SemaphoreType.DMA((5,))],
        compiler_params=pltpu.CompilerParams(vmem_limit_bytes=60 * MIB),
    )(qkv_weight.T, proj_weight, up_weight, down_weight)
    order = Order(after(info, block_a))
    attn_gain, mlp_scale = after((attn_gain, mlp_scale), block_a)
    own_a = swap(block_a, "tensor", 2)
    wa = [mixed, swap(mixed, "tensor", 1)]
    up_one = swap_core(after(up_weight, block_a))
    norm, gmlp = order.call(
        bind(prepare_kernel),
        (tokens, out_grad, row(attn_gain), row(mlp_scale)),
        (act, act),
    )
    packs, ctxs = {}, {}

    def attend(r, part):
        last = r == 3
        pieced = r > 1
        args = (norm,) + (wa[r] if pieced else (wa[r],)) + part
        outs = (packed, ctx, acc)
        if pieced:
            outs += (shape((4, D // 4, D), BF16),)
        if last:
            args += (tokens, row(attn_scale), row(mlp_gain))
            outs += (acc, act)
        got = order.call(bind(attend_kernel, r == 0, last), args, outs)
        packs[r], ctxs[r] = got[:2]
        if pieced:
            wa[r] = got[3].reshape(D, D)
        return (got[2],) + tuple(got[4:])

    part = attend(0, ())
    own_a = after(own_a, part[0], wa[1], up_one)
    one_a, two_a = second_hop(own_a)
    core_a = (swap_core(own_a),)
    own_b = swap(after(block_b, own_a), "tensor", 2)
    down_one = swap_core(after(down_weight, own_a))
    part = attend(1, after(part, core_a[0], down_one))
    one_a, two_a = after((one_a, two_a), part[0])
    three_a = third_hop(one_a, two_a)
    core_a += (swap_core(one_a), swap_core(two_a))
    square = shape((D, D), BF16)
    up_zero, down_zero, up_one, block_c, early_zero, early_one = order.call(
        early_kernel,
        (gmlp, down_one, up_weight, down_weight, up_one),
        (square, square, square, shape((D // 2, D), BF16), acc, acc),
        scratch=[pltpu.SemaphoreType.DMA((3,))],
        spaces=([VMEM] * 2 + [HBM] * 3, [VMEM] * 6),
    )
    three_b = swap(block_c, "tensor", 2)
    own_b = after(own_b, early_zero, core_a[1], core_a[2], *three_a)
    one_b, two_b = second_hop(own_b)
    wa.append((own_a, one_a, two_a) + three_a)
    wa.append(core_a + tuple(swap_core(piece) for piece in three_a))
    part = attend(2, part)
    attn_out, middle, norm_two = attend(3, part)

    wgrads, actives = {}, {}

    def mlp(r, weights, carried, extra=(), outs=()):
        got = order.call(
            bind(mlp_kernel, r == 3),
            (norm_two, gmlp) + weights + carried + extra,
            (shape((2, D, D), BF16), act, acc) + outs,
        )
        wgrads[r], actives[r] = got[:2]
        return tuple(got[2:])

    two = shape((2, D, D), BF16)
    wgrads[0], wgrads[1], actives[0], actives[1], pair_sum = order.call(
        bind(mlp_pair_kernel),
        (norm_two, gmlp, up_zero, early_zero, up_one, early_one),
        (two, two, act, act, acc),
        limit=11,
    )
    grad_sum = (pair_sum,)
    both_two = assemble(order, (own_b, one_b, two_b, three_b))
    both_three = swap_core(both_two)
    grad_sum = mlp(2, (both_two,), grad_sum)
    got_one = swap_core(after(wgrads[1], grad_sum[0]))
    extra = (middle, out_grad, row(mlp_gain), row(attn_scale))
    grad_sum, grad_mid, gattn = mlp(3, (both_three,), grad_sum, extra, (acc, act))
    got_three = swap_core(wgrads[3])

    def finish_block():
        return order.call(
            bind(finish_block_kernel),
            (middle, grad_sum, attn_out, grad_mid, out_grad, row(mlp_scale))
            + tuple(actives[r] for r in range(4))
            + (down_zero, down_one, both_two, both_three),
            (shape(tokens.shape, BF16), shape((3, D), F32)),
            scratch=[pltpu.VMEM((rows, D), F32)],
            limit=9,
        )

    agrads, gpacks = {}, {}
    half = shape((1, D // 2, D), BF16)

    def back(r):
        out = order.call(
            bind(attend_back_kernel),
            (wa[r], packs[r], ctxs[r], gattn, norm),
            (packed, half, half),
            scratch=[pltpu.VMEM((rows, 256), BF16)],
        )
        gpacks[r] = out[0]
        agrads[r] = tuple(out[1:])

    def input_back():
        return order.call(
            input_back_kernel,
            tuple(gpacks[r] for r in range(4)) + tuple(wa) + (tokens, grad_mid, row(attn_gain), small),
            (shape(tokens.shape, BF16), shape((4, D), F32)),
            scratch=[pltpu.VMEM((rows, D), F32)],
        )

    width = D // shards
    split = qkv_weight.shape[1]
    back(1)
    if shards == 8:
        view = lambda a: a.reshape((a.shape[0], a.shape[1] // width, width, D))
        swap_pair = lambda values: tuple(swap_core(value) for value in values)
        tiny = shape((4, D), F32)
        blocks = lambda count: shape((count, width, 256), BF16)
        whole = lambda count: shape((count, width, D), BF16)
        args = tuple(view(a) for a in (wgrads[0], got_one, wgrads[2], got_three))
        out = order.call(merge_zero_kernel, args, (blocks(16),) * 6)
        keeps_m = tuple(out[3:6])
        got_m = (swap_y(out[0]), swap_x(out[1]), swap_z(out[2]))
        got_one = swap_pair(agrads[1])
        back(3)
        got_three = swap_pair(agrads[3])
        back(0)
        back(2)
        args = tuple(view(a) for a in agrads[0] + got_one + agrads[2] + got_three)
        out = order.call(
            merge_one_kernel, keeps_m + got_m + args, (blocks(16),) * 3 + (blocks(8),) * 6
        )
        keeps = tuple(out[3:9])
        got = (swap_y(out[0]), swap_x(out[1]), swap_z(out[2]))
        block_out, small = finish_block()
        input_grad, small = input_back()
        small = order.call(add_kernel, (small, swap(small, "tensor", 1)), (tiny,))[0]
        smalls = (small, swap_y(small))
        out = order.call(
            merge_two_kernel, keeps + got + smalls, (blocks(8),) * 3 + (blocks(4),) * 6 + (tiny,)
        )
        keeps = tuple(out[3:9])
        got = (swap_y(out[0]), swap_x(out[1]), swap_z(out[2]))
        smalls = (out[9], swap_x(out[9]))
        out = order.call(
            merge_three_kernel,
            keeps + got + smalls,
            (blocks(2),) * 3 + (whole(2), whole(2)) + (blocks(2),) * 3 + (tiny,),
        )
        keeps = tuple(out[4:8])
        got = (swap_y(out[0]), swap_x(out[1]), swap_z(out[2]), swap_far(out[3]))
        smalls = (out[8], swap_z(out[8]))
        give, keep, small = order.call(
            merge_four_kernel, keeps[1:] + got[:3] + smalls, (whole(1), whole(1), tiny)
        )
        up_grad, down_grad = order.call(
            finish_mlp_kernel, (keeps[0], got[3]), (shape((width, D), F32), shape((width, D), F32))
        )
        down_grad = down_grad.T
        out = order.call(
            merge_last_kernel,
            (keep, swap_far(give), small, swap_far(small)),
            (shape((width, split), F32), shape((D - split, width), F32)) + (shape((1, width), F32),) * 4,
        )
        smalls = [value.reshape(width) for value in out[2:]]
        qkv_grad, proj_grad = out[:2]
    else:
        for r in (3, 0, 2):
            back(r)
        block_out, small = finish_block()
        input_grad, small = input_back()
        up_grad = scatter_sum([wgrads[r][0] for r in range(4)], False)
        down_grad = scatter_sum([wgrads[r][1] for r in range(4)], True).T
        mixed_grad = scatter_sum([jnp.concatenate(agrads[r], axis=1)[0] for r in range(4)], False)
        qkv_grad = mixed_grad[:, :split]
        proj_grad = mixed_grad[:, split:].T
        small = lax.psum(small, ("dp", "tensor"))
        small = lax.dynamic_slice_in_dim(small, place * width, width, axis=1)
        smalls = [small[i] for i in range(4)]
    return (
        block_out,
        input_grad,
        smalls[3],
        qkv_grad,
        proj_grad,
        smalls[2],
        smalls[1],
        up_grad,
        down_grad,
        smalls[0],
    )


def solution(mesh):
    in_specs = (
        P(None, ("dp", "tensor"), None),
        P(None, ("dp", "tensor"), None),
        P("dp", None),
        P("dp", None),
        P(),
        P(None, "tensor"),
        P("tensor", None),
        P(),
        P(),
        P(None, "tensor"),
        P("tensor", None),
        P(),
    )
    out_specs = (
        P(None, ("dp", "tensor"), None),
        P(None, ("dp", "tensor"), None),
        P("dp"),
        P("dp", "tensor"),
        P("tensor", "dp"),
        P("dp"),
        P("dp"),
        P("dp", "tensor"),
        P("tensor", "dp"),
        P("dp"),
    )
    return jax.shard_map(body, mesh=mesh, in_specs=in_specs, out_specs=out_specs, check_vma=False)
```
